128 devices in a mesh: ha: 16 (over x, y), wa: 8 (over z, core).
Axes of the slice: x: 4, y: 4, z: 4, core: 2. Of those that a mesh axis runs over, the one named last changes fastest.
Arguments:
- features: bfloat16 [16, 64, 64, 384], P(None, 'ha', 'wa'), may hold values from -6 to 6
- cache_first: bfloat16 [2, 64, 64, 384], P(None, 'ha', 'wa'), may hold values from -4 to 4
- cache_second: bfloat16 [2, 64, 64, 384], P(None, 'ha', 'wa'), may hold values from -4 to 4
- cache_head: bfloat16 [2, 64, 64, 384], P(None, 'ha', 'wa'), may hold values from -4 to 4
- gain_first: float32 [384], replicated, may hold values from 0.1 to 1.9
- gain_second: float32 [384], replicated, may hold values from 0.1 to 1.9
- gain_head: float32 [384], replicated, may hold values from 0.1 to 1.9
- conv_first: bfloat16 [3, 3, 3, 384, 384], replicated, may hold values from -0.0625 to 0.0625
- conv_second: bfloat16 [3, 3, 3, 384, 384], replicated, may hold values from -0.0625 to 0.0625
- conv_head: bfloat16 [3, 3, 3, 384, 32], replicated, may hold values from -0.0625 to 0.0625
- bias_first: float32 [384], replicated, may hold values from -3 to 3
- bias_second: float32 [384], replicated, may hold values from -3 to 3
- bias_head: float32 [32], replicated, may hold values from -3 to 3
Outputs:
- latent_tokens: bfloat16 [16384, 128], P(('ha', 'wa'))
The draws below stay inside these ranges and needn't reach their ends.
All inputs are finite; a program needn't handle non-finite values.
Results may differ from the reference program's by a relative error of at most 0.014.
Values may be sent and summed in bfloat16 or wider, within the bound.
No kernel may reach another device: no remote copies, remote signals or barrier semaphores. Data moves between devices by JAX's collectives and lax.ppermute only.
A program may use at most 192 MiB of HBM per device.

```python
import jax
import jax.numpy as jnp
from jax import lax

C = 384
Z = 16
F = 16
H = 64
W = 64


def level_of(own_key, extent, split, low, top_value):
    factor_of, own = 1.0, jax.random.fold_in(own_key, 6)
    for dim, parts in split:
        heights = jnp.exp(jax.random.uniform(jax.random.fold_in(own, dim), (parts,), jnp.float32, low / len(split), top_value / len(split)))
        factor_of = factor_of * jnp.repeat(heights, extent[dim] // parts).reshape([-1 if axis == dim else 1 for axis in range(len(extent))])
    return factor_of


def gaussian(own_key, shape, scale, most, split=(), held_as=jnp.bfloat16):
    entries = scale * jax.random.normal(own_key, shape, jnp.float32)
    if split:
        entries = entries * level_of(own_key, shape, split, -0.22, 0.18)
    return jnp.clip(entries, -most, most).astype(held_as)


def setup_inputs(seed: int = 0) -> dict:
    keys = jax.random.split(jax.random.key(seed), 14)
    return {
        "features": gaussian(keys[0], (F, H, W, C), 1.0, 6.0, ((1, 16), (2, 8))),
        "cache_first": gaussian(keys[1], (2, H, W, C), 0.6, 4.0, ((1, 16), (2, 8))),
        "cache_second": gaussian(keys[2], (2, H, W, C), 0.6, 4.0, ((1, 16), (2, 8))),
        "cache_head": gaussian(keys[3], (2, H, W, C), 0.6, 4.0, ((1, 16), (2, 8))),
        "gain_first": jnp.clip(1.0 + 0.18 * jax.random.normal(keys[4], (C,), jnp.float32), 0.1, 1.9),
        "gain_second": jnp.clip(1.0 + 0.18 * jax.random.normal(keys[5], (C,), jnp.float32), 0.1, 1.9),
        "gain_head": jnp.clip(1.0 + 0.18 * jax.random.normal(keys[6], (C,), jnp.float32), 0.1, 1.9),
        "conv_first": gaussian(keys[7], (3, 3, 3, C, C), (27 * C) ** -0.5, 0.0625),
        "conv_second": gaussian(keys[8], (3, 3, 3, C, C), (27 * C) ** -0.5, 0.0625),
        "conv_head": gaussian(keys[9], (3, 3, 3, C, 2 * Z), (27 * C) ** -0.5, 0.0625),
        "bias_first": gaussian(keys[10], (C,), 0.5, 3.0, (), jnp.float32),
        "bias_second": gaussian(keys[11], (C,), 0.5, 3.0, (), jnp.float32),
        "bias_head": gaussian(keys[12], (2 * Z,), 0.5, 3.0, (), jnp.float32),
    }


def activate(values, gain):
    wide = values.astype(jnp.float32)
    scale = lax.rsqrt(lax.optimization_barrier(jnp.mean(wide * wide, axis=-1, keepdims=True)) + 1e-06)
    return jax.nn.silu(wide * scale * gain).astype(jnp.bfloat16)

def causal_conv(padded, weight, frames, rows, cols):
    width_in = padded.shape[-1]
    out_width = weight.shape[-1]
    stacked = jnp.concatenate([padded[:, :, w_off:w_off + cols] for w_off in range(3)], axis=-1)
    total = jnp.zeros((frames * rows * cols, out_width), jnp.float32)
    for t_off in range(3):
        for h_off in range(3):
            taken = stacked[t_off:t_off + frames, h_off:h_off + rows].reshape(-1, 3 * width_in)
            kernel = weight[t_off, h_off].reshape(3 * width_in, out_width)
            total = total + jnp.dot(taken, kernel, preferred_element_type=jnp.float32)
    return total.reshape(frames, rows, cols, out_width)

def grid_conv(inputs, cached, weight):
    frames, rows, cols = (inputs.shape[0], inputs.shape[1], inputs.shape[2])
    extended = jnp.concatenate([cached, inputs], axis=0)
    padded = jnp.pad(extended, ((0, 0), (1, 1), (1, 1), (0, 0)))
    return causal_conv(padded, weight, frames, rows, cols)

def reference(features, cache_first, cache_second, cache_head, gain_first, gain_second, gain_head, conv_first, conv_second, conv_head, bias_first, bias_second, bias_head):
    first_in = activate(features, gain_first)
    hidden = (grid_conv(first_in, cache_first, conv_first) + bias_first).astype(jnp.bfloat16)
    second_in = activate(hidden, gain_second)
    block_out = (grid_conv(second_in, cache_second, conv_second) + bias_second + features.astype(jnp.float32)).astype(jnp.bfloat16)
    head_in = activate(block_out, gain_head)
    head = grid_conv(head_in, cache_head, conv_head) + bias_head
    frames, rows, cols, moment_count = head.shape
    moments = head.astype(jnp.bfloat16).reshape(frames, rows // 2, 2, cols // 2, 2, moment_count)
    patches = jnp.transpose(moments, (0, 1, 3, 2, 4, 5))
    return patches.reshape(frames * (rows // 2) * (cols // 2), 4 * moment_count)
```

```python
import functools

import jax
import jax.numpy as jnp
from jax import lax
from jax.experimental import pallas as pl
from jax.experimental.pallas import tpu as pltpu
from jax.sharding import PartitionSpec as P

BF16 = jnp.bfloat16
F32 = jnp.float32
F, R, Q, C = 16, 4, 8, 384
MSG = 19
VM = pl.BlockSpec(memory_space=pltpu.VMEM)
ANY = pl.BlockSpec(memory_space=pl.ANY)


def act(wide, gain):
    scale = lax.rsqrt(jnp.mean(wide * wide, axis=-1, keepdims=True) + 1e-06)
    u = wide * scale * gain
    return u / (1.0 + jnp.exp(-u))


def stack(now, c0, c1):
    row = lax.broadcasted_iota(jnp.int32, (F, C), 0)
    c0 = jnp.broadcast_to(c0, (F, C))
    c1 = jnp.broadcast_to(c1, (F, C))
    one = jnp.where(row == 0, c1, pltpu.roll(now, 1, 0))
    two = jnp.where(row == 0, c0, jnp.where(row == 1, c1, pltpu.roll(now, 2, 0)))
    return two.astype(BF16), one.astype(BF16), now.astype(BF16)


def put_rows(ref, start, value):
    for n in range(3):
        ref[n, pl.ds(start, value.shape[0])] = value[:, n * 128 : (n + 1) * 128]


def rows_at(ref, start, count, stride):
    where = pl.ds(start, count, stride=stride) if stride > 1 else pl.ds(start, count)
    return jnp.concatenate([ref[n, where, :] for n in range(3)], axis=-1)


def first_kernel(feat, cf, cs, gain, own, raw, lo, hi, wide, plain):
    def frame(f, _):
        x = feat[f].astype(F32).reshape(R * Q, C)
        put_rows(plain, f * R * Q, x)
        put_rows(wide, f * R * Q, act(x, gain[...]))
        return 0

    lax.fori_loop(0, F, frame, 0)
    for k in range(R * Q):
        cell = rows_at(wide, k, F, R * Q).astype(BF16)
        own[k] = cell
        if k < 16:
            lo[k] = cell
        else:
            hi[k - 16] = cell
        raw[k] = rows_at(plain, k, F, R * Q).astype(BF16)

    def cached(ref, h):
        return jnp.concatenate([ref[0, h].astype(F32), ref[1, h].astype(F32)], axis=0).astype(BF16)

    for n in range(2):
        lo[16 + n] = cached(cf, n)
        hi[16 + n] = cached(cf, 2 + n)
    lo[18] = cached(cs, 0)
    hi[18] = cached(cs, 3)


def fill_caches(cf, cs, top, bot, wide_f, wide_s):
    for n in range(2):
        put_rows(wide_f, n * 16, top[16 + n].astype(F32))
        put_rows(wide_f, (6 + n) * 16, bot[16 + n].astype(F32))
    put_rows(wide_s, 0, top[18].astype(F32))
    put_rows(wide_s, 5 * 16, bot[18].astype(F32))
    for h in range(R):
        for f in range(2):
            put_rows(wide_f, (2 + h) * 16 + f * 8, cf[f, h].astype(F32))
            put_rows(wide_s, (1 + h) * 16 + f * 8, cs[f, h].astype(F32))


def second_kernel(own, top, bot, cf, cs, left, right, wide_f, wide_s):
    wide_s[...] = jnp.zeros_like(wide_s)
    fill_caches(cf, cs, top, bot, wide_f, wide_s)
    for out, base, edge in ((left, 0, 0), (right, 6, 7)):
        for c in range(2):
            for h in range(8):
                w = base + c
                if h < 2:
                    cell = top[h * Q + w]
                elif h < 6:
                    cell = own[(h - 2) * Q + w]
                else:
                    cell = bot[(h - 6) * Q + w]
                out[h * 2 + c] = cell
            out[16 + c] = rows_at(wide_f, base + c, 16, 8).astype(BF16)
        out[18] = rows_at(wide_s, edge, 16, 8).astype(BF16)


def main_kernel(
    own, raw, top, bot, left, right, cf, cs, ch, g2, gh, b1, b2, w1, w2, wh, out,
    s1, s2, s3, acc1, acc2, acch, w1v, w2v, whv, wide_f, wide_s, side_f, side_s, wide_h, sems,
):
    copies = []
    for n, (src, dst) in enumerate(((w1, w1v), (w2, w2v))):
        for a in range(3):
            group = []
            for b in range(3):
                for t in range(3):
                    group.append(pltpu.make_async_copy(src.at[t, a, b], dst.at[a, b * 3 + t], sems.at[n * 3 + a]))
            copies.append(group)
    copies.append([pltpu.make_async_copy(wh, whv, sems.at[6])])
    for group in copies:
        for copy in group:
            copy.start()

    ha, wa = lax.axis_index("ha"), lax.axis_index("wa")
    up, down = ha > 0, ha < lax.axis_size("ha") - 1
    west, east = wa > 0, wa < lax.axis_size("wa") - 1

    fill_caches(cf, cs, top, bot, wide_f, wide_s)
    for n, msg in enumerate((left, right)):
        for c in range(2):
            side_f[n, pl.ds(c * 16, 16)] = msg[16 + c].astype(F32)
        side_s[n] = msg[18].astype(F32)
    for h in range(R):
        for f in range(2):
            wide_h[pl.ds(h * 16 + f * 8, 8)] = ch[f, h].astype(F32)

    def put(dst, valid, now, c0, c1):
        if valid is not None:
            keep = jnp.where(valid, 1.0, 0.0).astype(F32)
            now, c0, c1 = now * keep, c0 * keep, c1 * keep
        for n, part in enumerate(stack(now, c0, c1)):
            dst[:, pl.ds(n * C, C)] = part

    def middle(src, h0, count, valid):
        def cell(k, _):
            h, w = k // Q, k % Q
            base = (h0 + h) * 16 + w
            put(
                s1.at[h0 + h, w + 2], valid, src[k].astype(F32),
                rows_at(wide_f, base, 1, 1), rows_at(wide_f, base + 8, 1, 1),
            )
            return 0

        lax.fori_loop(0, count, cell, 0)

    middle(own, 2, 32, None)
    middle(top, 0, 16, up)
    middle(bot, 6, 16, down)
    for n, (msg, side, w0) in enumerate(((left, west, 0), (right, east, 10))):
        def cell(k, _, n=n, msg=msg, side=side, w0=w0):
            h, c = k // 2, k % 2
            valid = side & (up | (h >= 2)) & (down | (h < 6))
            base = c * 16 + h * 2
            put(
                s1.at[h, w0 + c], valid, msg[k].astype(F32),
                side_f[n, pl.ds(base, 1), :], side_f[n, pl.ds(base + 1, 1), :],
            )
            return 0

        lax.fori_loop(0, 16, cell, 0)

    def conv(src, weight, acc, rows, cols, first):
        for a in range(3):
            for copy in copies[first + a]:
                copy.wait()
            taken = jnp.concatenate(
                [src[a : a + rows, b : b + cols].reshape(rows * cols * F, 3 * C) for b in range(3)], axis=-1
            )
            part = jnp.dot(taken, weight[a].reshape(9 * C, C), preferred_element_type=F32)
            part = part.reshape(rows, cols, F, C)
            if a == 0:
                acc[...] = part
            else:
                acc[...] += part

    conv(s1, w1v, acc1, R + 2, Q + 2, 0)

    def hidden(h, w, c0, c1, valid):
        wide = (acc1[h, w] + b1[...]).astype(BF16).astype(F32)
        put(s2.at[h, w], valid, act(wide, g2[...]), c0, c1)

    def row_of(k, _):
        h, w = k // Q, k % Q
        base = h * 16 + w
        hidden(
            h, w + 1, rows_at(wide_s, base, 1, 1), rows_at(wide_s, base + 8, 1, 1),
            (up | (h >= 1)) & (down | (h < 5)),
        )
        return 0

    lax.fori_loop(0, 6 * Q, row_of, 0)
    for n, (side, w) in enumerate(((west, 0), (east, 9))):
        def edge(h, _, n=n, side=side, w=w):
            hidden(
                h, w, side_s[n, pl.ds(h * 2, 1), :], side_s[n, pl.ds(h * 2 + 1, 1), :],
                side & (up | (h >= 1)) & (down | (h < 5)),
            )
            return 0

        lax.fori_loop(0, 6, edge, 0)

    conv(s2, w2v, acc2, R, Q, 3)

    def last(k, _):
        h, w = k // Q, k % Q
        base = h * 16 + w
        wide = (acc2[h, w] + b2[...] + raw[k].astype(F32)).astype(BF16).astype(F32)
        put(
            s3.at[(h % 2) * 2 + w % 2, (h // 2) * 4 + w // 2], None, act(wide, gh[...]),
            wide_h[pl.ds(base, 1), :], wide_h[pl.ds(base + 8, 1), :],
        )
        return 0

    lax.fori_loop(0, R * Q, last, 0)
    for copy in copies[6]:
        copy.wait()
    acch[...] = jnp.zeros_like(acch)
    for rh in range(2):
        for rw in range(2):
            part = jnp.dot(
                s3[rh * 2 + rw].reshape(8 * F, 3 * C), whv[rh * 2 + rw], preferred_element_type=F32
            )
            for p in range(2):
                for q in range(4):
                    for m in range(2):
                        for n in range(2):
                            pp, qq = (p + rh - 1 + m) % 3, (q + rw - 1 + n) % 5
                            slot = pp * 4 + qq if qq < 4 else 12 + pp
                            block = part[(p * 4 + q) * F : (p * 4 + q + 1) * F, (m * 2 + n) * 128 : (m * 2 + n + 1) * 128]
                            acch[pl.ds(slot * F, F)] += block

    def frame(f, _):
        patches = acch[pl.ds(f, 16, stride=F), :].astype(BF16)
        for g in range(8):
            out[f, g] = patches
        return 0

    lax.fori_loop(0, F, frame, 0)


def last_kernel(slots, bias, out, held, sums, sem):
    ha_count = 16
    g = lax.axis_index("wa")
    copies = []
    for k in range(4):
        i = jnp.clip(2 * g - 1 + k, 0, ha_count - 1)
        copies.append(pltpu.make_async_copy(slots.at[pl.ds(i * 8, 8)], held.at[k], sem.at[k]))
        copies[-1].start()
    for copy in copies:
        copy.wait()
    lane = lax.broadcasted_iota(jnp.int32, (4, 128), 1)
    row = lax.broadcasted_iota(jnp.int32, (4, 128), 0)
    for k in range(2):
        for pr in range(2):
            other = k if pr == 0 else k + 2
            there = (2 * g + k > 0) if pr == 0 else (2 * g + k < ha_count - 1)
            upright = ((lane < 64) if pr == 0 else (lane >= 64)) & there

            def edge(j, pr=pr, k=k, other=other, upright=upright):
                mine = jnp.broadcast_to(held[k + 1, j, 12 + pr : 13 + pr].astype(F32), (4, 128))
                theirs = jnp.broadcast_to(held[other, j, 14:15].astype(F32), (4, 128))
                return mine + jnp.where(upright, theirs, 0.0)

            for j in range(8):
                total = held[k + 1, j, pr * 4 : pr * 4 + 4].astype(F32)
                total = total + jnp.where(upright, held[other, j, 8:12].astype(F32), 0.0)
                if j > 0:
                    total = total + jnp.where((row == 0) & (lane % 64 < 32), edge(j - 1), 0.0)
                if j < 7:
                    total = total + jnp.where((row == 3) & (lane % 64 >= 32), edge(j + 1), 0.0)
                sums[pl.ds((2 * k + pr) * 32 + j * 4, 4)] = total + bias[...]
    out[...] = sums[...].astype(BF16)


def shape(*dims, dtype=BF16):
    return jax.ShapeDtypeStruct(dims, dtype)


def params(limit):
    return pltpu.CompilerParams(vmem_limit_bytes=limit * 2**20)


def head_weights(conv_head):
    flat = jnp.transpose(conv_head, (1, 2, 0, 3, 4)).reshape(3, 3, 3 * C, 32)
    none = jnp.zeros((3 * C, 32), BF16)
    sets = []
    for rh in range(2):
        for rw in range(2):
            parts = []
            for m in range(2):
                for n in range(2):
                    for r in range(2):
                        for s in range(2):
                            a = rh - (2 * (rh - 1 + m) + r) + 1
                            b = rw - (2 * (rw - 1 + n) + s) + 1
                            parts.append(flat[a, b] if 0 <= a <= 2 and 0 <= b <= 2 else none)
            sets.append(jnp.concatenate(parts, axis=-1))
    return jnp.stack(sets)


def around(axis, step):
    count = lax.axis_size(axis)
    return [(n, (n + step) % count) for n in range(count)]


def local(
    features, cache_first, cache_second, cache_head, gain_first, gain_second, gain_head,
    conv_first, conv_second, conv_head, bias_first, bias_second, bias_head,
):
    line = lambda v: v.reshape(1, -1)
    own, raw, lo, hi = pl.pallas_call(
        first_kernel,
        out_shape=[shape(32, F, C), shape(32, F, C), shape(MSG, F, C), shape(MSG, F, C)],
        in_specs=[VM] * 4,
        out_specs=[VM] * 4,
        scratch_shapes=[pltpu.VMEM((3, F * R * Q, 128), F32)] * 2,
        compiler_params=params(16),
        name="act_first",
    )(features, cache_first, cache_second, line(gain_first))
    top = lax.ppermute(hi, "ha", around("ha", 1))
    bot = lax.ppermute(lo, "ha", around("ha", -1))
    to_left, to_right = pl.pallas_call(
        second_kernel,
        out_shape=[shape(MSG, F, C)] * 2,
        in_specs=[VM] * 5,
        out_specs=[VM] * 2,
        scratch_shapes=[pltpu.VMEM((3, 128, 128), F32)] * 2,
        compiler_params=params(16),
        name="pack_columns",
    )(own, top, bot, cache_first, cache_second)
    left = lax.ppermute(to_right, "wa", around("wa", 1))
    right = lax.ppermute(to_left, "wa", around("wa", -1))
    slots = pl.pallas_call(
        main_kernel,
        out_shape=shape(F, 8, 16, 128),
        in_specs=[VM] * 13 + [ANY] * 3,
        out_specs=VM,
        scratch_shapes=[
            pltpu.VMEM((R + 4, Q + 4, F, 3 * C), BF16),
            pltpu.VMEM((R + 2, Q + 2, F, 3 * C), BF16),
            pltpu.VMEM((4, 8, F, 3 * C), BF16),
            pltpu.VMEM((R + 2, Q + 2, F, C), F32),
            pltpu.VMEM((R, Q, F, C), F32),
            pltpu.VMEM((16 * F, 128), F32),
            pltpu.VMEM((3, 9, C, C), BF16),
            pltpu.VMEM((3, 9, C, C), BF16),
            pltpu.VMEM((4, 3 * C, 512), BF16),
            pltpu.VMEM((3, 128, 128), F32),
            pltpu.VMEM((3, 128, 128), F32),
            pltpu.VMEM((2, 32, C), F32),
            pltpu.VMEM((2, 16, C), F32),
            pltpu.VMEM((64, C), F32),
            pltpu.SemaphoreType.DMA((7,)),
        ],
        compiler_params=params(56),
        name="block",
    )(
        own, raw, top, bot, left, right, cache_first, cache_second, cache_head,
        line(gain_second), line(gain_head), line(bias_first), line(bias_second),
        conv_first, conv_second, head_weights(conv_head),
    )
    arrived = lax.all_to_all(slots.reshape(F * 8, 16, 128), ("ha", "wa"), 0, 0, tiled=True)
    return pl.pallas_call(
        last_kernel,
        out_shape=shape(128, 128),
        in_specs=[ANY, VM],
        out_specs=VM,
        scratch_shapes=[
            pltpu.VMEM((4, 8, 16, 128), BF16),
            pltpu.VMEM((128, 128), F32),
            pltpu.SemaphoreType.DMA((4,)),
        ],
        compiler_params=params(16),
        name="sum_patches",
    )(arrived, jnp.tile(bias_head, 4).reshape(1, 128))


def solution(mesh):
    tile = P(None, "ha", "wa", None)
    return jax.shard_map(
        local,
        mesh=mesh,
        in_specs=(tile,) * 4 + (P(),) * 9,
        out_specs=P(("ha", "wa"), None),
        check_vma=False,
    )
```

```python
import functools

import jax
import jax.numpy as jnp
from jax import lax
from jax.experimental import pallas as pl
from jax.experimental.pallas import tpu as pltpu
from jax.sharding import PartitionSpec as P

BF16 = jnp.bfloat16
F32 = jnp.float32
F, R, Q, C = 16, 4, 8, 384
MSG = 19
VM = pl.BlockSpec(memory_space=pltpu.VMEM)
ANY = pl.BlockSpec(memory_space=pl.ANY)


def act(wide, half_gain):
    scale = lax.rsqrt(jnp.mean(wide * wide, axis=-1, keepdims=True) + 1e-06)
    h = wide * scale * half_gain
    return h + h * jnp.tanh(h)


def line(ref):
    return ref[...].reshape(1, -1)


def put_rows(ref, start, value):
    for n in range(3):
        ref[n, pl.ds(start, value.shape[0])] = value[:, n * 128 : (n + 1) * 128]


def rows_at(ref, start, count, stride):
    where = pl.ds(start, count, stride=stride) if stride > 1 else pl.ds(start, count)
    return jnp.concatenate([ref[n, where, :] for n in range(3)], axis=-1)


def stack(now, c0, c1):
    row = lax.broadcasted_iota(jnp.int32, now.shape, 0) % F
    c0, c1 = (jnp.concatenate([jnp.broadcast_to(c, (F, C)) for c in cs], axis=0) for cs in (c0, c1))
    one = jnp.where(row == 0, c1, pltpu.roll(now, 1, 0))
    two = jnp.where(row == 0, c0, jnp.where(row == 1, c1, pltpu.roll(now, 2, 0)))
    return two.astype(BF16), one.astype(BF16), now.astype(BF16)


def put(dst, where, now, c0, c1, valid=None):
    if valid is not None:
        keep = jnp.where(valid, 1.0, 0.0).astype(F32)
        now, c0, c1 = now * keep, [c * keep for c in c0], [c * keep for c in c1]
    for n, part in enumerate(stack(now, c0, c1)):
        dst[where + (slice(None), pl.ds(n * C, C))] = part.reshape(-1, F, C)


def bring(pairs, sems):
    copies = [pltpu.make_async_copy(src, dst, sems.at[n]) for n, (src, dst) in enumerate(pairs)]
    for copy in copies:
        copy.start()
    return copies


def first_kernel(feat_h, cf_h, cs_h, gain_h, own, raw, lo, hi, feat, cf, cs, gain, wide, plain, sems):
    copies = bring(((gain_h, gain), (feat_h, feat), (cf_h, cf), (cs_h, cs)), sems)
    copies[0].wait()
    copies[1].wait()
    half = 0.5 * line(gain)

    def frame(f, _):
        x = feat[pl.ds(f * 4, 4)].astype(F32).reshape(4 * R * Q, C)
        put_rows(plain, f * 4 * R * Q, x)
        put_rows(wide, f * 4 * R * Q, act(x, half))
        return 0

    lax.fori_loop(0, F // 4, frame, 0)
    for k in range(R * Q):
        cell = rows_at(wide, k, F, R * Q).astype(BF16)
        own[k] = cell
        if k < 16:
            lo[k] = cell
        else:
            hi[k - 16] = cell
        raw[k] = rows_at(plain, k, F, R * Q).astype(BF16)

    def cached(ref, h):
        return jnp.concatenate([ref[0, h].astype(F32), ref[1, h].astype(F32)], axis=0).astype(BF16)

    copies[2].wait()
    copies[3].wait()
    for n in range(2):
        lo[16 + n] = cached(cf, n)
        hi[16 + n] = cached(cf, 2 + n)
    lo[18] = cached(cs, 0)
    hi[18] = cached(cs, 3)


def fill_caches(cf, cs, top, bot, wide_f, wide_s):
    for n in range(2):
        put_rows(wide_f, n * 16, top[16 + n].astype(F32))
        put_rows(wide_f, (6 + n) * 16, bot[16 + n].astype(F32))
    put_rows(wide_s, 0, top[18].astype(F32))
    put_rows(wide_s, 5 * 16, bot[18].astype(F32))
    for h in range(R):
        for f in range(2):
            put_rows(wide_f, (2 + h) * 16 + f * 8, cf[f, h].astype(F32))
            put_rows(wide_s, (1 + h) * 16 + f * 8, cs[f, h].astype(F32))


def second_kernel(own, top, bot, cf_h, cs_h, left, right, cf, cs, wide_f, wide_s, sems):
    copies = bring(((cf_h, cf), (cs_h, cs)), sems)
    wide_s[...] = jnp.zeros_like(wide_s)
    for out, base in ((left, 0), (right, 6)):
        for c in range(2):
            for h in range(8):
                w = base + c
                if h < 2:
                    cell = top[h * Q + w]
                elif h < 6:
                    cell = own[(h - 2) * Q + w]
                else:
                    cell = bot[(h - 6) * Q + w]
                out[h * 2 + c] = cell
    for copy in copies:
        copy.wait()
    fill_caches(cf, cs, top, bot, wide_f, wide_s)
    for out, base, edge in ((left, 0, 0), (right, 6, 7)):
        for c in range(2):
            out[16 + c] = rows_at(wide_f, base + c, 16, 8).astype(BF16)
        out[18] = rows_at(wide_s, edge, 16, 8).astype(BF16)


def main_kernel(
    own, raw, top, bot, left, right, cf_h, cs_h, ch_h, g2_h, gh_h, b1_h, b2_h, w1, w2, wh, out,
    s1, s2, s3, acc1, acc2, acch, w1v, w2v, whv, wy, wide_f, wide_s, side_f, side_s, wide_h,
    cf, cs, ch, g2, gh, b1, b2, sems, wsems,
):
    small = bring(
        ((cf_h, cf), (cs_h, cs), (ch_h, ch), (g2_h, g2), (gh_h, gh), (b1_h, b1), (b2_h, b2)), sems
    )
    copies = []
    for n, (src, dst) in enumerate(((w1, w1v), (w2, w2v))):
        for a in range(3):
            group = []
            for b in range(3):
                for t in range(3):
                    group.append(pltpu.make_async_copy(src.at[t, a, b], dst.at[a, b * 3 + t], wsems.at[n * 3 + a]))
            copies.append(group)
    copies.insert(3, [pltpu.make_async_copy(wh, whv, wsems.at[6])])
    for group in copies:
        for copy in group:
            copy.start()

    ha, wa = lax.axis_index("ha"), lax.axis_index("wa")
    up, down = ha > 0, ha < lax.axis_size("ha") - 1
    west, east = wa > 0, wa < lax.axis_size("wa") - 1

    for copy in small:
        copy.wait()
    fill_caches(cf, cs, top, bot, wide_f, wide_s)
    for n, msg in enumerate((left, right)):
        for c in range(2):
            side_f[n, pl.ds(c * 16, 16)] = msg[16 + c].astype(F32)
        side_s[n] = msg[18].astype(F32)
    for h in range(R):
        for f in range(2):
            wide_h[pl.ds(h * 16 + f * 8, 8)] = ch[f, h].astype(F32)

    def middle(src, h0, count, valid):
        def cells(h, _):
            base = (h0 + h) * 16
            put(
                s1, (h0 + h, pl.ds(2, Q)), src[pl.ds(h * Q, Q)].reshape(Q * F, C).astype(F32),
                [rows_at(wide_f, base + w, 1, 1) for w in range(Q)],
                [rows_at(wide_f, base + 8 + w, 1, 1) for w in range(Q)], valid,
            )
            return 0

        lax.fori_loop(0, count, cells, 0)

    middle(own, 2, 4, None)
    middle(top, 0, 2, up)
    middle(bot, 6, 2, down)
    for n, (msg, side, w0) in enumerate(((left, west, 0), (right, east, 10))):
        def cells(h, _, n=n, msg=msg, side=side, w0=w0):
            put(
                s1, (h, pl.ds(w0, 2)), msg[pl.ds(h * 2, 2)].reshape(2 * F, C).astype(F32),
                [side_f[n, pl.ds(c * 16 + h * 2, 1), :] for c in range(2)],
                [side_f[n, pl.ds(c * 16 + h * 2 + 1, 1), :] for c in range(2)],
                side & (up | (h >= 2)) & (down | (h < 6)),
            )
            return 0

        lax.fori_loop(0, 8, cells, 0)

    def conv(src, weight, acc, rows, cols, first):
        for a in range(3):
            for copy in copies[first + a]:
                copy.wait()
            taken = jnp.concatenate(
                [src[a : a + rows, b : b + cols].reshape(rows * cols * F, 3 * C) for b in range(3)], axis=-1
            )
            part = jnp.dot(taken, weight[a].reshape(9 * C, C), preferred_element_type=F32)
            part = part.reshape(rows, cols, F, C)
            if a == 0:
                acc[...] = part
            else:
                acc[...] += part

    conv(s1, w1v, acc1, R + 2, Q + 2, 0)

    half2 = 0.5 * line(g2)

    def hidden(h, _):
        base = h * 16
        inside = (up | (h >= 1)) & (down | (h < 5))
        for w0, count, valid, c0, c1 in (
            (1, Q, inside, [rows_at(wide_s, base + w, 1, 1) for w in range(Q)],
             [rows_at(wide_s, base + 8 + w, 1, 1) for w in range(Q)]),
            (0, 1, inside & west, [side_s[0, pl.ds(h * 2, 1), :]], [side_s[0, pl.ds(h * 2 + 1, 1), :]]),
            (9, 1, inside & east, [side_s[1, pl.ds(h * 2, 1), :]], [side_s[1, pl.ds(h * 2 + 1, 1), :]]),
        ):
            wide = (acc1[h, pl.ds(w0, count)].reshape(count * F, C) + line(b1)).astype(BF16).astype(F32)
            put(s2, (h, pl.ds(w0, count)), act(wide, half2), c0, c1, valid)
        return 0

    lax.fori_loop(0, 6, hidden, 0)

    for copy in copies[3]:
        copy.wait()
    none = jnp.zeros((C, 32), BF16)
    for t in range(3):
        for a in range(3):
            wy[pl.ds(t * C, C), pl.ds(a * 128, 128)] = jnp.concatenate(
                [whv[t, a, 0], whv[t, a, 1], whv[t, a, 2], none], axis=-1
            )

    conv(s2, w2v, acc2, R, Q, 4)

    halfh = 0.5 * line(gh)

    def last(h, _):
        base = h * 16
        wide = acc2[h].reshape(Q * F, C) + line(b2) + raw[pl.ds(h * Q, Q)].reshape(Q * F, C).astype(F32)
        put(
            s3, (pl.ds(h * Q, Q),), act(wide.astype(BF16).astype(F32), halfh),
            [wide_h[pl.ds(base + w, 1), :] for w in range(Q)],
            [wide_h[pl.ds(base + 8 + w, 1), :] for w in range(Q)],
        )
        return 0

    lax.fori_loop(0, R, last, 0)
    part = jnp.dot(s3[...].reshape(R * Q * F, 3 * C), wy[...], preferred_element_type=F32)
    lane = lax.broadcasted_iota(jnp.int32, (F, 128), 1)
    sums = {}
    for h in range(R):
        for w in range(Q):
            k = h * Q + w
            for a in range(3):
                block = part[k * F : (k + 1) * F, a * 128 : (a + 1) * 128]
                for b in range(3):
                    row, col = h + 1 - a, w + 1 - b
                    pp, qq = (row // 2) % 3, (col // 2) % 5
                    slot = pp * 4 + qq if qq < 4 else 12 + pp
                    low = (2 * (row % 2) + col % 2) * 32
                    shift = (low - 32 * b) % 128
                    moved = pltpu.roll(block, shift, 1) if shift else block
                    term = jnp.where((lane >= low) & (lane < low + 32), moved, 0.0)
                    sums[slot] = sums[slot] + term if slot in sums else term
    for slot, total in sums.items():
        acch[pl.ds(slot * F, F)] = total
    acch[pl.ds(15 * F, F)] = jnp.zeros((F, 128), F32)

    for f in range(F):
        patches = acch[pl.ds(f, 16, stride=F), :].astype(BF16)
        for g in range(8):
            out[f, g] = patches


def last_kernel(slots, bias, out, held, sums, sem):
    ha_count = 16
    g = lax.axis_index("wa")
    copies = []
    for k in range(4):
        i = jnp.clip(2 * g - 1 + k, 0, ha_count - 1)
        copies.append(pltpu.make_async_copy(slots.at[pl.ds(i * 8, 8)], held.at[k], sem.at[k]))
        copies[-1].start()
    for copy in copies:
        copy.wait()
    lane = lax.broadcasted_iota(jnp.int32, (4, 128), 1)
    row = lax.broadcasted_iota(jnp.int32, (4, 128), 0)
    for k in range(2):
        for pr in range(2):
            other = k if pr == 0 else k + 2
            there = (2 * g + k > 0) if pr == 0 else (2 * g + k < ha_count - 1)
            upright = ((lane < 64) if pr == 0 else (lane >= 64)) & there

            def edge(j, pr=pr, k=k, other=other, upright=upright):
                mine = jnp.broadcast_to(held[k + 1, j, 12 + pr : 13 + pr].astype(F32), (4, 128))
                theirs = jnp.broadcast_to(held[other, j, 14:15].astype(F32), (4, 128))
                return mine + jnp.where(upright, theirs, 0.0)

            for j in range(8):
                total = held[k + 1, j, pr * 4 : pr * 4 + 4].astype(F32)
                total = total + jnp.where(upright, held[other, j, 8:12].astype(F32), 0.0)
                if j > 0:
                    total = total + jnp.where((row == 0) & (lane % 64 < 32), edge(j - 1), 0.0)
                if j < 7:
                    total = total + jnp.where((row == 3) & (lane % 64 >= 32), edge(j + 1), 0.0)
                sums[pl.ds((2 * k + pr) * 32 + j * 4, 4)] = total + bias[...]
    out[...] = sums[...].astype(BF16)


def shape(*dims, dtype=BF16):
    return jax.ShapeDtypeStruct(dims, dtype)


def params(limit):
    return pltpu.CompilerParams(vmem_limit_bytes=limit * 2**20)


def around(axis, step):
    count = lax.axis_size(axis)
    return [(n, (n + step) % count) for n in range(count)]


def local(
    features, cache_first, cache_second, cache_head, gain_first, gain_second, gain_head,
    conv_first, conv_second, conv_head, bias_first, bias_second, bias_head,
):
    own, raw, lo, hi = pl.pallas_call(
        first_kernel,
        out_shape=[shape(32, F, C), shape(32, F, C), shape(MSG, F, C), shape(MSG, F, C)],
        in_specs=[ANY] * 4,
        out_specs=[VM] * 4,
        scratch_shapes=[
            pltpu.VMEM((F, R, Q, C), BF16),
            pltpu.VMEM((2, R, Q, C), BF16),
            pltpu.VMEM((2, R, Q, C), BF16),
            pltpu.VMEM((C,), F32),
            pltpu.VMEM((3, F * R * Q, 128), F32),
            pltpu.VMEM((3, F * R * Q, 128), F32),
            pltpu.SemaphoreType.DMA((4,)),
        ],
        compiler_params=params(16),
        name="act_first",
    )(features, cache_first, cache_second, gain_first)
    top = lax.ppermute(hi, "ha", around("ha", 1))
    bot = lax.ppermute(lo, "ha", around("ha", -1))
    to_left, to_right = pl.pallas_call(
        second_kernel,
        out_shape=[shape(MSG, F, C)] * 2,
        in_specs=[VM] * 3 + [ANY] * 2,
        out_specs=[VM] * 2,
        scratch_shapes=[
            pltpu.VMEM((2, R, Q, C), BF16),
            pltpu.VMEM((2, R, Q, C), BF16),
            pltpu.VMEM((3, 128, 128), F32),
            pltpu.VMEM((3, 128, 128), F32),
            pltpu.SemaphoreType.DMA((2,)),
        ],
        compiler_params=params(16),
        name="pack_columns",
    )(own, top, bot, cache_first, cache_second)
    left = lax.ppermute(to_right, "wa", around("wa", 1))
    right = lax.ppermute(to_left, "wa", around("wa", -1))
    slots = pl.pallas_call(
        main_kernel,
        out_shape=shape(F, 8, 16, 128),
        in_specs=[VM] * 6 + [ANY] * 10,
        out_specs=VM,
        scratch_shapes=[
            pltpu.VMEM((R + 4, Q + 4, F, 3 * C), BF16),
            pltpu.VMEM((R + 2, Q + 2, F, 3 * C), BF16),
            pltpu.VMEM((R * Q, F, 3 * C), BF16),
            pltpu.VMEM((R + 2, Q + 2, F, C), F32),
            pltpu.VMEM((R, Q, F, C), F32),
            pltpu.VMEM((16 * F, 128), F32),
            pltpu.VMEM((3, 9, C, C), BF16),
            pltpu.VMEM((3, 9, C, C), BF16),
            pltpu.VMEM((3, 3, 3, C, 32), BF16),
            pltpu.VMEM((3 * C, 3 * 128), BF16),
            pltpu.VMEM((3, 128, 128), F32),
            pltpu.VMEM((3, 128, 128), F32),
            pltpu.VMEM((2, 32, C), F32),
            pltpu.VMEM((2, 16, C), F32),
            pltpu.VMEM((64, C), F32),
            pltpu.VMEM((2, R, Q, C), BF16),
            pltpu.VMEM((2, R, Q, C), BF16),
            pltpu.VMEM((2, R, Q, C), BF16),
            pltpu.VMEM((C,), F32),
            pltpu.VMEM((C,), F32),
            pltpu.VMEM((C,), F32),
            pltpu.VMEM((C,), F32),
            pltpu.SemaphoreType.DMA((7,)),
            pltpu.SemaphoreType.DMA((7,)),
        ],
        compiler_params=params(56),
        name="block",
    )(
        own, raw, top, bot, left, right, cache_first, cache_second, cache_head,
        gain_second, gain_head, bias_first, bias_second, conv_first, conv_second, conv_head,
    )
    arrived = lax.all_to_all(slots.reshape(F * 8, 16, 128), ("ha", "wa"), 0, 0, tiled=True)
    return pl.pallas_call(
        last_kernel,
        out_shape=shape(128, 128),
        in_specs=[ANY, VM],
        out_specs=VM,
        scratch_shapes=[
            pltpu.VMEM((4, 8, 16, 128), BF16),
            pltpu.VMEM((128, 128), F32),
            pltpu.SemaphoreType.DMA((4,)),
        ],
        compiler_params=params(16),
        name="sum_patches",
    )(arrived, jnp.tile(bias_head, 4).reshape(1, 128))


def solution(mesh):
    tile = P(None, "ha", "wa", None)
    return jax.shard_map(
        local,
        mesh=mesh,
        in_specs=(tile,) * 4 + (P(),) * 9,
        out_specs=P(("ha", "wa"), None),
        check_vma=False,
    )
```

```python
import jax
import jax.numpy as jnp
from jax import lax
from jax.experimental import pallas as pl
from jax.experimental.pallas import tpu as pltpu
from jax.sharding import PartitionSpec as P

BF16 = jnp.bfloat16
F32 = jnp.float32
F, R, Q, C = 16, 4, 8, 384
MSG = 19
VM = pl.BlockSpec(memory_space=pltpu.VMEM)
ANY = pl.BlockSpec(memory_space=pl.ANY)


def act(wide, half_gain):
    scale = lax.rsqrt(jnp.mean(wide * wide, axis=-1, keepdims=True) + 1e-06)
    h = wide * scale * half_gain
    return h + h * jnp.tanh(h)


def line(ref):
    return ref[...].reshape(1, -1)


def put_rows(ref, start, value):
    for n in range(3):
        ref[n, pl.ds(start, value.shape[0])] = value[:, n * 128 : (n + 1) * 128]


def rows_at(ref, start, count, stride):
    where = pl.ds(start, count, stride=stride) if stride > 1 else pl.ds(start, count)
    return jnp.concatenate([ref[n, where, :] for n in range(3)], axis=-1)


def stack(now, c0, c1):
    row = lax.broadcasted_iota(jnp.int32, now.shape, 0) % F
    c0, c1 = (jnp.concatenate([jnp.broadcast_to(c, (F, C)) for c in cs], axis=0) for cs in (c0, c1))
    one = jnp.where(row == 0, c1, pltpu.roll(now, 1, 0))
    two = jnp.where(row == 0, c0, jnp.where(row == 1, c1, pltpu.roll(now, 2, 0)))
    return two.astype(BF16), one.astype(BF16), now.astype(BF16)


def put(dst, where, now, c0, c1, valid=None):
    if valid is not None:
        keep = jnp.where(valid, 1.0, 0.0).astype(F32)
        now, c0, c1 = now * keep, [c * keep for c in c0], [c * keep for c in c1]
    for n, part in enumerate(stack(now, c0, c1)):
        dst[where + (slice(None), pl.ds(n * C, C))] = part.reshape(-1, F, C)


def bring(pairs, sems):
    copies = [pltpu.make_async_copy(src, dst, sems.at[n]) for n, (src, dst) in enumerate(pairs)]
    for copy in copies:
        copy.start()
    return copies


def first_kernel(
    feat_h, cf_h, cs_h, ch_h, g1_h, g2_h, gh_h, b1_h, b2_h, own, raw, lo, hi, cfw, csw, chw, vec,
    feat, caches, g1, g2, gh, b1, b2, wide, plain, sems,
):
    copies = bring(
        ((g1_h, g1), (feat_h, feat), (cf_h, caches.at[0]), (cs_h, caches.at[1]), (ch_h, caches.at[2]),
         (g2_h, g2), (gh_h, gh), (b1_h, b1), (b2_h, b2)), sems
    )
    copies[0].wait()
    copies[1].wait()
    half = 0.5 * line(g1)

    def frame(f, _):
        x = feat[pl.ds(f * 4, 4)].astype(F32).reshape(4 * R * Q, C)
        put_rows(plain, f * 4 * R * Q, x)
        put_rows(wide, f * 4 * R * Q, act(x, half))
        return 0

    lax.fori_loop(0, F // 4, frame, 0)
    for k in range(R * Q):
        cell = rows_at(wide, k, F, R * Q).astype(BF16)
        own[k] = cell
        if k < 16:
            lo[k] = cell
        else:
            hi[k - 16] = cell
        raw[k] = rows_at(plain, k, F, R * Q).astype(BF16)
    for copy in copies[2:]:
        copy.wait()
    for n, value in enumerate((0.5 * line(g2), 0.5 * line(gh), line(b1), line(b2))):
        vec[pl.ds(n, 1)] = value
    for n, out in enumerate((cfw, csw, chw)):
        for h in range(R):
            for f in range(2):
                put_rows(out, h * 16 + f * 8, caches[n, f, h].astype(F32))
    for n in range(2):
        lo[16 + n] = rows_at(cfw, n * 16, 16, 1).astype(BF16)
        hi[16 + n] = rows_at(cfw, (2 + n) * 16, 16, 1).astype(BF16)
    lo[18] = rows_at(csw, 0, 16, 1).astype(BF16)
    hi[18] = rows_at(csw, 48, 16, 1).astype(BF16)


def pack_kernel(own, top, bot, cfw, csw, left, right, wide_f, wide_s):
    for n in range(2):
        put_rows(wide_f, n * 16, top[16 + n].astype(F32))
        put_rows(wide_f, (6 + n) * 16, bot[16 + n].astype(F32))
    put_rows(wide_s, 0, top[18].astype(F32))
    put_rows(wide_s, 5 * 16, bot[18].astype(F32))
    for n in range(3):
        wide_f[n, pl.ds(32, 64)] = cfw[n]
        wide_s[n, pl.ds(16, 64)] = csw[n]
        wide_s[n, pl.ds(96, 32)] = jnp.zeros((32, 128), F32)
    for out, base, edge in ((left, 0, 0), (right, 6, 7)):
        for c in range(2):
            for h in range(8):
                w = base + c
                if h < 2:
                    cell = top[h * Q + w]
                elif h < 6:
                    cell = own[(h - 2) * Q + w]
                else:
                    cell = bot[(h - 6) * Q + w]
                out[h * 2 + c] = cell
            out[16 + c] = rows_at(wide_f, base + c, 16, 8).astype(BF16)
        out[18] = rows_at(wide_s, edge, 16, 8).astype(BF16)


def cached_row(ref, base, w0, count):
    return [[rows_at(ref, base + 8 * f + w0 + w, 1, 1) for w in range(count)] for f in range(2)]


def cached_msg(block, count=Q):
    block = block.astype(F32)
    return [[block[8 * f + w : 8 * f + w + 1] for w in range(count)] for f in range(2)]


def taps(src, weight, a):
    return jnp.dot(src, weight[a].reshape(9 * C, C), preferred_element_type=F32)


def hidden(dst, where, total, vec, cached, valid=None):
    wide = (total + vec[pl.ds(2, 1), :]).astype(BF16).astype(F32)
    put(dst, where, act(wide, vec[pl.ds(0, 1), :]), cached[0], cached[1], valid)


def place():
    ha, wa = lax.axis_index("ha"), lax.axis_index("wa")
    return ha > 0, ha < lax.axis_size("ha") - 1, wa > 0, wa < lax.axis_size("wa") - 1


def inner_kernel(own, cfw, csw, vec, w1, w2, wh, s1, s2, w1v, w2v, wy, acc, sems):
    def group(src, dst, a, sem):
        return [
            pltpu.make_async_copy(src.at[t, a, b], dst.at[a, b * 3 + t], sem) for b in range(3) for t in range(3)
        ]

    first = [group(w1, w1v, a, sems.at[a]) for a in range(3)]
    later = [copy for a in range(3) for copy in group(w2, w2v, a, sems.at[3 + a])]
    for t in range(3):
        for a in range(3):
            for b in range(3):
                later.append(
                    pltpu.make_async_copy(
                        wh.at[t, a, b], wy.at[pl.ds(a * 128 + b * 32, 32), pl.ds(t * C, C)], sems.at[6]
                    )
                )
    for copies in first[:2]:
        for copy in copies:
            copy.start()
    for a in range(3):
        wy[pl.ds(a * 128 + 96, 32)] = jnp.zeros((32, 3 * C), BF16)

    def cells(h, _):
        c0, c1 = cached_row(cfw, h * 16, 0, Q)
        put(s1, (h, pl.ds(0, Q)), own[pl.ds(h * Q, Q)].reshape(Q * F, C).astype(F32), c0, c1)
        return 0

    lax.fori_loop(0, R, cells, 0)
    for a in range(3):
        for copy in first[a]:
            copy.wait()
        for copy in (first[2], later, ())[a]:
            copy.start()
        taken = jnp.concatenate([s1[a : a + 2, b : b + 6].reshape(12 * F, 3 * C) for b in range(3)], axis=-1)
        if a == 0:
            acc[...] = taps(taken, w1v, a)
        else:
            acc[...] += taps(taken, w1v, a)
    for h in range(2):
        hidden(s2, (h, pl.ds(0, 6)), acc[pl.ds(h * 6 * F, 6 * F)], vec, cached_row(csw, (1 + h) * 16, 1, 6))
    for copy in later:
        copy.wait()


def rows_kernel(top, bot, own1, csw, vec, w1v, s1, s2, acc):
    up, down, _, _ = place()
    for msg, h0, valid in ((top, 0, up), (bot, 6, down)):
        for h in range(2):
            c0, c1 = cached_msg(msg[16 + h])
            put(s1, (h0 + h, pl.ds(0, Q)), msg[pl.ds(h * Q, Q)].reshape(Q * F, C).astype(F32), c0, c1, valid)
    s1[2:6] = own1[...]
    for a in range(3):
        taken = jnp.concatenate(
            [
                jnp.concatenate(
                    [s1[4 * n + a : 4 * n + a + 2, b : b + 6].reshape(12 * F, 3 * C) for n in range(2)], axis=0
                )
                for b in range(3)
            ],
            axis=-1,
        )
        if a == 0:
            acc[...] = taps(taken, w1v, a)
        else:
            acc[...] += taps(taken, w1v, a)
    for n, cached, valid in (
        (0, [c[1:7] for c in cached_msg(top[18])], up),
        (1, cached_row(csw, 0, 1, 6), None),
        (2, cached_row(csw, 48, 1, 6), None),
        (3, [c[1:7] for c in cached_msg(bot[18])], down),
    ):
        hidden(s2, (n, pl.ds(0, 6)), acc[pl.ds(n * 6 * F, 6 * F)], vec, cached, valid)


def finish_kernel(
    left, right, top, bot, s1, inner2, rows2, raw, csw, chw, vec, w1v, w2v, wy, out,
    sides, s2, s3, acc1, acc2, acch, side_f, side_s,
):
    up, down, west, east = place()
    for n, msg in enumerate((left, right)):
        for c in range(2):
            side_f[n, pl.ds(c * 16, 16)] = msg[16 + c].astype(F32)
        side_s[n] = msg[18].astype(F32)
    sides[:, 0, 2:4] = s1[:, 0:2]
    sides[:, 1, 0:2] = s1[:, 6:8]
    for n, (msg, side, w0) in enumerate(((left, west, 0), (right, east, 2))):
        def cells(h, _, n=n, msg=msg, side=side, w0=w0):
            for k in range(2):
                hh = h * 2 + k
                put(
                    sides, (hh, n, pl.ds(w0, 2)), msg[pl.ds(hh * 2, 2)].reshape(2 * F, C).astype(F32),
                    [side_f[n, pl.ds(c * 16 + hh * 2, 1), :] for c in range(2)],
                    [side_f[n, pl.ds(c * 16 + hh * 2 + 1, 1), :] for c in range(2)],
                    side & (up | (hh >= 2)) & (down | (hh < 6)),
                )
            return 0

        lax.fori_loop(0, 4, cells, 0)

    for a in range(3):
        taken = jnp.concatenate(
            [sides[a : a + 6, :, b : b + 2].reshape(24 * F, 3 * C) for b in range(3)], axis=-1
        )
        if a == 0:
            acc1[...] = taps(taken, w1v, a)
        else:
            acc1[...] += taps(taken, w1v, a)
    s2[2:4, 2:8] = inner2[...]
    s2[0:2, 2:8] = rows2[0:2]
    s2[4:6, 2:8] = rows2[2:4]
    for h in range(6):
        inside = up if h == 0 else down if h == 5 else True
        if h == 0:
            c0, c1 = cached_msg(top[18])
        elif h == 5:
            c0, c1 = cached_msg(bot[18])
        else:
            c0, c1 = cached_row(csw, (h - 1) * 16, 0, Q)
        for n, side in enumerate((west, east)):
            first = [side_s[n, pl.ds(h * 2 + f, 1), :] for f in range(2)]
            keep = jnp.where(side, 1.0, 0.0).astype(F32)
            total = acc1[pl.ds((h * 2 + n) * 2 * F, 2 * F)]
            wide = (total + vec[pl.ds(2, 1), :]).astype(BF16).astype(F32)
            now = act(wide, vec[pl.ds(0, 1), :])
            own_w = 0 if n == 0 else Q - 1
            pair = [now[:F], now[F:]]
            pair[n] = pair[n] * keep
            now = jnp.concatenate(pair, axis=0)
            olds = []
            for f, c in enumerate((c0, c1)):
                two = [first[f] * keep, c[own_w]]
                olds.append(two if n == 0 else two[::-1])
            put(s2, (h, pl.ds(8 * n, 2)), now, olds[0], olds[1], None if inside is True else inside)

    for a in range(3):
        taken = jnp.concatenate([s2[a : a + R, b : b + Q].reshape(R * Q * F, 3 * C) for b in range(3)], axis=-1)
        if a == 0:
            acc2[...] = taps(taken, w2v, a)
        else:
            acc2[...] += taps(taken, w2v, a)

    def last(h, _):
        wide = acc2[pl.ds(h * Q * F, Q * F)] + vec[pl.ds(3, 1), :]
        wide = wide + raw[pl.ds(h * Q, Q)].reshape(Q * F, C).astype(F32)
        c0, c1 = cached_row(chw, h * 16, 0, Q)
        put(s3, (pl.ds(h * Q, Q),), act(wide.astype(BF16).astype(F32), vec[pl.ds(1, 1), :]), c0, c1)
        return 0

    lax.fori_loop(0, R, last, 0)
    part = lax.dot_general(
        s3[...].reshape(R * Q * F, 3 * C), wy[...], (((1,), (1,)), ((), ())), preferred_element_type=F32
    )
    lane = lax.broadcasted_iota(jnp.int32, (F, 128), 1)
    sums = {}
    for h in range(R):
        for w in range(Q):
            k = h * Q + w
            for a in range(3):
                block = part[k * F : (k + 1) * F, a * 128 : (a + 1) * 128]
                for b in range(3):
                    row, col = h + 1 - a, w + 1 - b
                    pp, qq = (row // 2) % 3, (col // 2) % 5
                    slot = pp * 4 + qq if qq < 4 else 12 + pp
                    low = (2 * (row % 2) + col % 2) * 32
                    shift = (low - 32 * b) % 128
                    moved = pltpu.roll(block, shift, 1) if shift else block
                    term = jnp.where((lane >= low) & (lane < low + 32), moved, 0.0)
                    sums[slot] = sums[slot] + term if slot in sums else term
    for slot, total in sums.items():
        acch[pl.ds(slot * F, F)] = total
    acch[pl.ds(15 * F, F)] = jnp.zeros((F, 128), F32)

    for f in range(F):
        patches = acch[pl.ds(f, 16, stride=F), :].astype(BF16)
        for g in range(8):
            out[f, g] = patches


def last_kernel(slots, bias, out, held, sums, sem):
    ha_count = 16
    g = lax.axis_index("wa")
    copies = []
    for k in range(4):
        i = jnp.clip(2 * g - 1 + k, 0, ha_count - 1)
        copies.append(pltpu.make_async_copy(slots.at[pl.ds(i * 8, 8)], held.at[k], sem.at[k]))
        copies[-1].start()
    for copy in copies:
        copy.wait()
    lane = lax.broadcasted_iota(jnp.int32, (4, 128), 1)
    row = lax.broadcasted_iota(jnp.int32, (4, 128), 0)
    for k in range(2):
        for pr in range(2):
            other = k if pr == 0 else k + 2
            there = (2 * g + k > 0) if pr == 0 else (2 * g + k < ha_count - 1)
            upright = ((lane < 64) if pr == 0 else (lane >= 64)) & there

            def edge(j, pr=pr, k=k, other=other, upright=upright):
                mine = jnp.broadcast_to(held[k + 1, j, 12 + pr : 13 + pr].astype(F32), (4, 128))
                theirs = jnp.broadcast_to(held[other, j, 14:15].astype(F32), (4, 128))
                return mine + jnp.where(upright, theirs, 0.0)

            for j in range(8):
                total = held[k + 1, j, pr * 4 : pr * 4 + 4].astype(F32)
                total = total + jnp.where(upright, held[other, j, 8:12].astype(F32), 0.0)
                if j > 0:
                    total = total + jnp.where((row == 0) & (lane % 64 < 32), edge(j - 1), 0.0)
                if j < 7:
                    total = total + jnp.where((row == 3) & (lane % 64 >= 32), edge(j + 1), 0.0)
                sums[pl.ds((2 * k + pr) * 32 + j * 4, 4)] = total + bias[...]
    out[...] = sums[...].astype(BF16)


def shape(*dims, dtype=BF16):
    return jax.ShapeDtypeStruct(dims, dtype)


def near(*dims, dtype=BF16):
    return pltpu.VMEM(dims, dtype)


def far(array):
    return pltpu.with_memory_space_constraint(array, pltpu.HBM)


def kernel(body, outs, ins, scratch, limit, name, flops=0, moved=0):
    return pl.pallas_call(
        body,
        out_shape=outs,
        in_specs=ins,
        out_specs=[VM] * len(outs),
        scratch_shapes=scratch,
        compiler_params=pltpu.CompilerParams(vmem_limit_bytes=limit * 2**20),
        cost_estimate=pl.CostEstimate(flops=flops, bytes_accessed=moved, transcendentals=0),
        name=name,
    )


def around(axis, step):
    count = lax.axis_size(axis)
    return [(n, (n + step) % count) for n in range(count)]


def local(
    features, cache_first, cache_second, cache_head, gain_first, gain_second, gain_head,
    conv_first, conv_second, conv_head, bias_first, bias_second, bias_head,
):
    own, raw, lo, hi, cfw, csw, chw, vec = kernel(
        first_kernel,
        [near(32, F, C), near(32, F, C), near(MSG, F, C), near(MSG, F, C)]
        + [near(3, 64, 128, dtype=F32)] * 3 + [near(8, C, dtype=F32)],
        [ANY] * 9,
        [
            pltpu.VMEM((F, R, Q, C), BF16),
            pltpu.VMEM((3, 2, R, Q, C), BF16),
        ]
        + [pltpu.VMEM((C,), F32)] * 5
        + [
            pltpu.VMEM((3, F * R * Q, 128), F32),
            pltpu.VMEM((3, F * R * Q, 128), F32),
            pltpu.SemaphoreType.DMA((9,)),
        ],
        12, "act_first",
    )(*[far(v) for v in (features, cache_first, cache_second, cache_head, gain_first, gain_second, gain_head,
                         bias_first, bias_second)])
    top = lax.ppermute(hi, "ha", around("ha", 1))
    bot = lax.ppermute(lo, "ha", around("ha", -1))
    cell_flops = 2 * F * 27 * C * C
    own1, inner2, w1v, w2v, wy = kernel(
        inner_kernel,
        [near(R, Q, F, 3 * C), near(2, 6, F, 3 * C), near(3, 9, C, C), near(3, 9, C, C), near(3 * 128, 3 * C)],
        [VM] * 4 + [ANY] * 3,
        [pltpu.VMEM((12 * F, C), F32), pltpu.SemaphoreType.DMA((7,))],
        8, "inner", 12 * cell_flops, 17 * 2**20,
    )(own, cfw, csw, vec, far(conv_first), far(conv_second), far(jnp.swapaxes(conv_head, 3, 4)))
    to_left, to_right = kernel(
        pack_kernel,
        [near(MSG, F, C)] * 2,
        [VM] * 5,
        [pltpu.VMEM((3, 128, 128), F32)] * 2,
        4, "pack_columns",
    )(own, top, bot, cfw, csw)
    left = lax.ppermute(to_right, "wa", around("wa", 1))
    right = lax.ppermute(to_left, "wa", around("wa", -1))
    s1, rows2 = kernel(
        rows_kernel,
        [near(8, Q, F, 3 * C), near(4, 6, F, 3 * C)],
        [VM] * 6,
        [pltpu.VMEM((24 * F, C), F32)],
        8, "rows", 24 * cell_flops, 10 * 2**20,
    )(top, bot, own1, csw, vec, w1v)
    (slots,) = kernel(
        finish_kernel,
        [shape(F, 8, 16, 128)],
        [VM] * 14,
        [
            pltpu.VMEM((8, 2, 4, F, 3 * C), BF16),
            pltpu.VMEM((R + 2, Q + 2, F, 3 * C), BF16),
            pltpu.VMEM((R * Q, F, 3 * C), BF16),
            pltpu.VMEM((24 * F, C), F32),
            pltpu.VMEM((R * Q * F, C), F32),
            pltpu.VMEM((16 * F, 128), F32),
            pltpu.VMEM((2, 32, C), F32),
            pltpu.VMEM((2, 16, C), F32),
        ],
        20, "finish", 60 * cell_flops, 20 * 2**20,
    )(left, right, top, bot, s1, inner2, rows2, raw, csw, chw, vec, w1v, w2v, wy)
    arrived = lax.all_to_all(slots.reshape(F * 8, 16, 128), ("ha", "wa"), 0, 0, tiled=True)
    return pl.pallas_call(
        last_kernel,
        out_shape=shape(128, 128),
        in_specs=[ANY, VM],
        out_specs=VM,
        scratch_shapes=[
            pltpu.VMEM((4, 8, 16, 128), BF16),
            pltpu.VMEM((128, 128), F32),
            pltpu.SemaphoreType.DMA((4,)),
        ],
        compiler_params=pltpu.CompilerParams(vmem_limit_bytes=8 * 2**20),
        name="sum_patches",
    )(arrived, jnp.tile(bias_head, 4).reshape(1, 128))


def solution(mesh):
    tile = P(None, "ha", "wa", None)
    return jax.shard_map(
        local,
        mesh=mesh,
        in_specs=(tile,) * 4 + (P(),) * 9,
        out_specs=P(("ha", "wa"), None),
        check_vma=False,
    )
```

```python
import jax
import jax.numpy as jnp
from jax import lax
from jax.experimental import pallas as pl
from jax.experimental.pallas import tpu as pltpu
from jax.sharding import PartitionSpec as P

BF16 = jnp.bfloat16
F32 = jnp.float32
F, R, Q, C = 16, 4, 8, 384
MSG = 19
VM = pl.BlockSpec(memory_space=pltpu.VMEM)
ANY = pl.BlockSpec(memory_space=pl.ANY)


def act(wide, half_gain):
    scale = lax.rsqrt(jnp.mean(wide * wide, axis=-1, keepdims=True) + 1e-06)
    h = wide * scale * half_gain
    return h + h * jnp.tanh(h)


def line(ref):
    return ref[...].reshape(1, -1)


def put_rows(ref, start, value):
    for n in range(3):
        ref[n, pl.ds(start, value.shape[0])] = value[:, n * 128 : (n + 1) * 128]


def rows_at(ref, start, count, stride):
    where = pl.ds(start, count, stride=stride) if stride > 1 else pl.ds(start, count)
    return jnp.concatenate([ref[n, where, :] for n in range(3)], axis=-1)


def stack(now, c0, c1):
    row = lax.broadcasted_iota(jnp.int32, now.shape, 0) % F
    c0, c1 = (jnp.concatenate([jnp.broadcast_to(c, (F, C)) for c in cs], axis=0) for cs in (c0, c1))
    one = jnp.where(row == 0, c1, pltpu.roll(now, 1, 0))
    two = jnp.where(row == 0, c0, jnp.where(row == 1, c1, pltpu.roll(now, 2, 0)))
    return two.astype(BF16), one.astype(BF16), now.astype(BF16)


def put(dst, where, now, c0, c1, valid=None):
    if valid is not None:
        keep = jnp.where(valid, 1.0, 0.0).astype(F32)
        now, c0, c1 = now * keep, [c * keep for c in c0], [c * keep for c in c1]
    for n, part in enumerate(stack(now, c0, c1)):
        dst[where + (slice(None), pl.ds(n * C, C))] = part.reshape(-1, F, C)


def bring(pairs, sems):
    copies = [pltpu.make_async_copy(src, dst, sems.at[n]) for n, (src, dst) in enumerate(pairs)]
    for copy in copies:
        copy.start()
    return copies


def first_kernel(
    feat_h, cf_h, cs_h, ch_h, g1_h, g2_h, gh_h, b1_h, b2_h, b3_h, own, plain, lo, hi, cfw, csw, chw, vec, bias,
    feat, caches, g1, g2, gh, b1, b2, b3, wide, sems,
):
    parts = [pl.ds(4 * n, 4) for n in range(4)]
    copies = bring(
        [(g1_h, g1)] + [(feat_h.at[part], feat.at[part]) for part in parts]
        + [(cf_h, caches.at[0]), (cs_h, caches.at[1]), (ch_h, caches.at[2]),
           (g2_h, g2), (gh_h, gh), (b1_h, b1), (b2_h, b2), (b3_h, b3)], sems
    )
    copies[0].wait()
    half = 0.5 * line(g1)
    for n, part in enumerate(parts):
        copies[1 + n].wait()
        x = feat[part].astype(F32).reshape(4 * R * Q, C)
        put_rows(plain, n * 4 * R * Q, x)
        put_rows(wide, n * 4 * R * Q, act(x, half))
    for k in range(R * Q):
        cell = rows_at(wide, k, F, R * Q).astype(BF16)
        own[k] = cell
        if k < 16:
            lo[k] = cell
        else:
            hi[k - 16] = cell
    for copy in copies[5:]:
        copy.wait()
    for n, value in enumerate((0.5 * line(g2), 0.5 * line(gh), line(b1), line(b2))):
        vec[pl.ds(n, 1)] = value
    bias[pl.ds(0, 1)] = jnp.concatenate([line(b3)] * 4, axis=-1)
    for n, out in enumerate((cfw, csw, chw)):
        for h in range(R):
            for f in range(2):
                put_rows(out, h * 16 + f * 8, caches[n, f, h].astype(F32))
    for n in range(2):
        lo[16 + n] = rows_at(cfw, n * 16, 16, 1).astype(BF16)
        hi[16 + n] = rows_at(cfw, (2 + n) * 16, 16, 1).astype(BF16)
    lo[18] = rows_at(csw, 0, 16, 1).astype(BF16)
    hi[18] = rows_at(csw, 48, 16, 1).astype(BF16)


def pack_kernel(own, top, bot, cfw, csw, left, right, wide_f, wide_s):
    for n in range(2):
        put_rows(wide_f, n * 16, top[16 + n].astype(F32))
        put_rows(wide_f, (6 + n) * 16, bot[16 + n].astype(F32))
    put_rows(wide_s, 0, top[18].astype(F32))
    put_rows(wide_s, 5 * 16, bot[18].astype(F32))
    for n in range(3):
        wide_f[n, pl.ds(32, 64)] = cfw[n]
        wide_s[n, pl.ds(16, 64)] = csw[n]
        wide_s[n, pl.ds(96, 32)] = jnp.zeros((32, 128), F32)
    for out, base, edge in ((left, 0, 0), (right, 6, 7)):
        for c in range(2):
            for h in range(8):
                w = base + c
                if h < 2:
                    cell = top[h * Q + w]
                elif h < 6:
                    cell = own[(h - 2) * Q + w]
                else:
                    cell = bot[(h - 6) * Q + w]
                out[h * 2 + c] = cell
            out[16 + c] = rows_at(wide_f, base + c, 16, 8).astype(BF16)
        out[18] = rows_at(wide_s, edge, 16, 8).astype(BF16)


def cached_row(ref, base, w0, count):
    return [[rows_at(ref, base + 8 * f + w0 + w, 1, 1) for w in range(count)] for f in range(2)]


def cached_msg(block, count=Q):
    block = block.astype(F32)
    return [[block[8 * f + w : 8 * f + w + 1] for w in range(count)] for f in range(2)]


def taps(src, weight, a):
    return jnp.dot(src, weight[a].reshape(9 * C, C), preferred_element_type=F32)


def hidden(dst, where, total, vec, cached, valid=None):
    wide = (total + vec[pl.ds(2, 1), :]).astype(BF16).astype(F32)
    put(dst, where, act(wide, vec[pl.ds(0, 1), :]), cached[0], cached[1], valid)


def place():
    ha, wa = lax.axis_index("ha"), lax.axis_index("wa")
    return ha > 0, ha < lax.axis_size("ha") - 1, wa > 0, wa < lax.axis_size("wa") - 1


def inner_kernel(own, plain, cfw, csw, vec, w1, w2, wh, s1, s2, w1v, w2v, wy, raw, acc, sems):
    def group(src, dst, a, sem):
        return [
            pltpu.make_async_copy(src.at[t, a, b], dst.at[a, b * 3 + t], sem) for b in range(3) for t in range(3)
        ]

    first = [group(w1, w1v, a, sems.at[a]) for a in range(3)]
    later = [copy for a in range(3) for copy in group(w2, w2v, a, sems.at[3 + a])]
    for t in range(3):
        for a in range(3):
            for b in range(3):
                later.append(
                    pltpu.make_async_copy(
                        wh.at[t, a, b], wy.at[pl.ds(a * 128 + b * 32, 32), pl.ds(t * C, C)], sems.at[6]
                    )
                )
    for copies in first[:2]:
        for copy in copies:
            copy.start()
    for a in range(3):
        wy[pl.ds(a * 128 + 96, 32)] = jnp.zeros((32, 3 * C), BF16)

    def cells(h, _):
        c0, c1 = cached_row(cfw, h * 16, 0, Q)
        put(s1, (h, pl.ds(0, Q)), own[pl.ds(h * Q, Q)].reshape(Q * F, C).astype(F32), c0, c1)
        return 0

    lax.fori_loop(0, R, cells, 0)
    for a in range(3):
        for copy in first[a]:
            copy.wait()
        for copy in (first[2], later, ())[a]:
            copy.start()
        taken = jnp.concatenate([s1[a : a + 2, b : b + 6].reshape(12 * F, 3 * C) for b in range(3)], axis=-1)
        if a == 0:
            acc[...] = taps(taken, w1v, a)
        else:
            acc[...] += taps(taken, w1v, a)
    for h in range(2):
        hidden(s2, (h, pl.ds(0, 6)), acc[pl.ds(h * 6 * F, 6 * F)], vec, cached_row(csw, (1 + h) * 16, 1, 6))
    for k in range(R * Q):
        raw[k] = rows_at(plain, k, F, R * Q).astype(BF16)
    for copy in later:
        copy.wait()


def rows_kernel(top, bot, own1, csw, vec, w1v, s1, s2, acc):
    up, down, _, _ = place()
    for msg, h0, valid in ((top, 0, up), (bot, 6, down)):
        for h in range(2):
            c0, c1 = cached_msg(msg[16 + h])
            put(s1, (h0 + h, pl.ds(0, Q)), msg[pl.ds(h * Q, Q)].reshape(Q * F, C).astype(F32), c0, c1, valid)
    s1[2:6] = own1[...]
    for a in range(3):
        taken = jnp.concatenate(
            [
                jnp.concatenate(
                    [s1[4 * n + a : 4 * n + a + 2, b : b + 6].reshape(12 * F, 3 * C) for n in range(2)], axis=0
                )
                for b in range(3)
            ],
            axis=-1,
        )
        if a == 0:
            acc[...] = taps(taken, w1v, a)
        else:
            acc[...] += taps(taken, w1v, a)
    for n, cached, valid in (
        (0, [c[1:7] for c in cached_msg(top[18])], up),
        (1, cached_row(csw, 0, 1, 6), None),
        (2, cached_row(csw, 48, 1, 6), None),
        (3, [c[1:7] for c in cached_msg(bot[18])], down),
    ):
        hidden(s2, (n, pl.ds(0, 6)), acc[pl.ds(n * 6 * F, 6 * F)], vec, cached, valid)


def finish_kernel(
    left, right, top, bot, s1, inner2, rows2, raw, csw, chw, vec, w1v, w2v, wy, out,
    sides, s2, s3, acc1, acc2, acch, side_f, side_s,
):
    up, down, west, east = place()
    for n, msg in enumerate((left, right)):
        for c in range(2):
            side_f[n, pl.ds(c * 16, 16)] = msg[16 + c].astype(F32)
        side_s[n] = msg[18].astype(F32)
    sides[:, 0, 2:4] = s1[:, 0:2]
    sides[:, 1, 0:2] = s1[:, 6:8]
    for n, (msg, side, w0) in enumerate(((left, west, 0), (right, east, 2))):
        def cells(h, _, n=n, msg=msg, side=side, w0=w0):
            for k in range(2):
                hh = h * 2 + k
                put(
                    sides, (hh, n, pl.ds(w0, 2)), msg[pl.ds(hh * 2, 2)].reshape(2 * F, C).astype(F32),
                    [side_f[n, pl.ds(c * 16 + hh * 2, 1), :] for c in range(2)],
                    [side_f[n, pl.ds(c * 16 + hh * 2 + 1, 1), :] for c in range(2)],
                    side & (up | (hh >= 2)) & (down | (hh < 6)),
                )
            return 0

        lax.fori_loop(0, 4, cells, 0)

    for a in range(3):
        taken = jnp.concatenate(
            [sides[a : a + 6, :, b : b + 2].reshape(24 * F, 3 * C) for b in range(3)], axis=-1
        )
        if a == 0:
            acc1[...] = taps(taken, w1v, a)
        else:
            acc1[...] += taps(taken, w1v, a)
    s2[2:4, 2:8] = inner2[...]
    s2[0:2, 2:8] = rows2[0:2]
    s2[4:6, 2:8] = rows2[2:4]
    for h in range(6):
        inside = up if h == 0 else down if h == 5 else True
        if h == 0:
            c0, c1 = cached_msg(top[18])
        elif h == 5:
            c0, c1 = cached_msg(bot[18])
        else:
            c0, c1 = cached_row(csw, (h - 1) * 16, 0, Q)
        for n, side in enumerate((west, east)):
            first = [side_s[n, pl.ds(h * 2 + f, 1), :] for f in range(2)]
            keep = jnp.where(side, 1.0, 0.0).astype(F32)
            total = acc1[pl.ds((h * 2 + n) * 2 * F, 2 * F)]
            wide = (total + vec[pl.ds(2, 1), :]).astype(BF16).astype(F32)
            now = act(wide, vec[pl.ds(0, 1), :])
            own_w = 0 if n == 0 else Q - 1
            pair = [now[:F], now[F:]]
            pair[n] = pair[n] * keep
            now = jnp.concatenate(pair, axis=0)
            olds = []
            for f, c in enumerate((c0, c1)):
                two = [first[f] * keep, c[own_w]]
                olds.append(two if n == 0 else two[::-1])
            put(s2, (h, pl.ds(8 * n, 2)), now, olds[0], olds[1], None if inside is True else inside)

    def window(a, rows):
        return jnp.concatenate([s2[a : a + rows, b : b + Q].reshape(rows * Q * F, 3 * C) for b in range(3)], axis=-1)

    for a in range(3):
        part = jnp.dot(window(a, R), w2v[a, :, :, 0:256].reshape(9 * C, 256), preferred_element_type=F32)
        if a == 0:
            acc2[:, 0:256] = part
        else:
            acc2[:, 0:256] += part
    side = [w2v[a, :, :, 256:384].reshape(9 * C, 128) for a in range(3)]
    pair = jnp.dot(window(0, R + 1), jnp.concatenate(side[:2], axis=-1), preferred_element_type=F32)
    acc2[:, 256:384] = (
        pair[: R * Q * F, :128] + pair[Q * F :, 128:]
        + jnp.dot(window(2, R), side[2], preferred_element_type=F32)
    )

    def last(h, _):
        wide = acc2[pl.ds(h * Q * F, Q * F)] + vec[pl.ds(3, 1), :]
        wide = wide + raw[pl.ds(h * Q, Q)].reshape(Q * F, C).astype(F32)
        c0, c1 = cached_row(chw, h * 16, 0, Q)
        put(s3, (pl.ds(h * Q, Q),), act(wide.astype(BF16).astype(F32), vec[pl.ds(1, 1), :]), c0, c1)
        return 0

    lax.fori_loop(0, R, last, 0)
    part = lax.dot_general(
        s3[...].reshape(R * Q * F, 3 * C), wy[...], (((1,), (1,)), ((), ())), preferred_element_type=F32
    )
    lane = lax.broadcasted_iota(jnp.int32, (F, 128), 1)
    sums = {}
    for h in range(R):
        for w in range(Q):
            k = h * Q + w
            for a in range(3):
                block = part[k * F : (k + 1) * F, a * 128 : (a + 1) * 128]
                for b in range(3):
                    row, col = h + 1 - a, w + 1 - b
                    pp, qq = (row // 2) % 3, (col // 2) % 5
                    slot = pp * 4 + qq if qq < 4 else 12 + pp
                    low = (2 * (row % 2) + col % 2) * 32
                    shift = (low - 32 * b) % 128
                    moved = pltpu.roll(block, shift, 1) if shift else block
                    term = jnp.where((lane >= low) & (lane < low + 32), moved, 0.0)
                    sums[slot] = sums[slot] + term if slot in sums else term
    for slot, total in sums.items():
        acch[pl.ds(slot * F, F)] = total
    acch[pl.ds(15 * F, F)] = jnp.zeros((F, 128), F32)

    for f in range(F):
        patches = acch[pl.ds(f, 16, stride=F), :].astype(BF16)
        for g in range(8):
            out[f, g] = patches


def last_kernel(slots, bias, out, sums):
    ha_count = 16
    g = lax.axis_index("wa")
    first = [jnp.clip(2 * g - 1 + k, 0, ha_count - 1) * 8 for k in range(4)]

    def held(k, j, low, count):
        return slots[first[k] + j, pl.ds(low, count)].astype(F32)

    lane = lax.broadcasted_iota(jnp.int32, (4, 128), 1)
    row = lax.broadcasted_iota(jnp.int32, (4, 128), 0)
    for k in range(2):
        for pr in range(2):
            other = k if pr == 0 else k + 2
            there = (2 * g + k > 0) if pr == 0 else (2 * g + k < ha_count - 1)
            upright = ((lane < 64) if pr == 0 else (lane >= 64)) & there

            def edge(j, pr=pr, k=k, other=other, upright=upright):
                mine = jnp.broadcast_to(held(k + 1, j, 12 + pr, 1), (4, 128))
                theirs = jnp.broadcast_to(held(other, j, 14, 1), (4, 128))
                return mine + jnp.where(upright, theirs, 0.0)

            for j in range(8):
                total = held(k + 1, j, pr * 4, 4)
                total = total + jnp.where(upright, held(other, j, 8, 4), 0.0)
                if j > 0:
                    total = total + jnp.where((row == 0) & (lane % 64 < 32), edge(j - 1), 0.0)
                if j < 7:
                    total = total + jnp.where((row == 3) & (lane % 64 >= 32), edge(j + 1), 0.0)
                sums[pl.ds((2 * k + pr) * 32 + j * 4, 4)] = total + bias[pl.ds(0, 1), :]
    out[...] = sums[...].astype(BF16)


def shape(*dims, dtype=BF16):
    return jax.ShapeDtypeStruct(dims, dtype)


def near(*dims, dtype=BF16):
    return pltpu.VMEM(dims, dtype)


def far(array):
    return pltpu.with_memory_space_constraint(array, pltpu.HBM)


def kernel(body, outs, ins, scratch, limit, name, flops=0, moved=0):
    return pl.pallas_call(
        body,
        out_shape=outs,
        in_specs=ins,
        out_specs=[VM] * len(outs),
        scratch_shapes=scratch,
        compiler_params=pltpu.CompilerParams(vmem_limit_bytes=limit * 2**20),
        cost_estimate=pl.CostEstimate(flops=flops, bytes_accessed=moved, transcendentals=0),
        name=name,
    )


def around(axis, step):
    count = lax.axis_size(axis)
    return [(n, (n + step) % count) for n in range(count)]


def local(
    features, cache_first, cache_second, cache_head, gain_first, gain_second, gain_head,
    conv_first, conv_second, conv_head, bias_first, bias_second, bias_head,
):
    own, plain, lo, hi, cfw, csw, chw, vec, bias = kernel(
        first_kernel,
        [near(32, F, C), near(3, F * R * Q, 128, dtype=F32), near(MSG, F, C), near(MSG, F, C)]
        + [near(3, 64, 128, dtype=F32)] * 3 + [near(8, C, dtype=F32), near(8, 128, dtype=F32)],
        [ANY] * 10,
        [
            pltpu.VMEM((F, R, Q, C), BF16),
            pltpu.VMEM((3, 2, R, Q, C), BF16),
        ]
        + [pltpu.VMEM((C,), F32)] * 5
        + [
            pltpu.VMEM((32,), F32),
            pltpu.VMEM((3, F * R * Q, 128), F32),
            pltpu.SemaphoreType.DMA((13,)),
        ],
        12, "act_first",
    )(*[far(v) for v in (features, cache_first, cache_second, cache_head, gain_first, gain_second, gain_head,
                         bias_first, bias_second, bias_head)])
    top = lax.ppermute(hi, "ha", around("ha", 1))
    bot = lax.ppermute(lo, "ha", around("ha", -1))
    cell_flops = 2 * F * 27 * C * C
    own1, inner2, w1v, w2v, wy, raw = kernel(
        inner_kernel,
        [near(R, Q, F, 3 * C), near(2, 6, F, 3 * C), near(3, 9, C, C), near(3, 9, C, C), near(3 * 128, 3 * C),
         near(32, F, C)],
        [VM] * 5 + [ANY] * 3,
        [pltpu.VMEM((12 * F, C), F32), pltpu.SemaphoreType.DMA((7,))],
        8, "inner", 12 * cell_flops, 17 * 2**20,
    )(own, plain, cfw, csw, vec, far(conv_first), far(conv_second), far(jnp.swapaxes(conv_head, 3, 4)))
    to_left, to_right = kernel(
        pack_kernel,
        [near(MSG, F, C)] * 2,
        [VM] * 5,
        [pltpu.VMEM((3, 128, 128), F32)] * 2,
        4, "pack_columns",
    )(own, top, bot, cfw, csw)
    left = lax.ppermute(to_right, "wa", around("wa", 1))
    right = lax.ppermute(to_left, "wa", around("wa", -1))
    s1, rows2 = kernel(
        rows_kernel,
        [near(8, Q, F, 3 * C), near(4, 6, F, 3 * C)],
        [VM] * 6,
        [pltpu.VMEM((24 * F, C), F32)],
        8, "rows", 24 * cell_flops, 10 * 2**20,
    )(top, bot, own1, csw, vec, w1v)
    (slots,) = kernel(
        finish_kernel,
        [shape(F, 8, 16, 128)],
        [VM] * 14,
        [
            pltpu.VMEM((8, 2, 4, F, 3 * C), BF16),
            pltpu.VMEM((R + 2, Q + 2, F, 3 * C), BF16),
            pltpu.VMEM((R * Q, F, 3 * C), BF16),
            pltpu.VMEM((24 * F, C), F32),
            pltpu.VMEM((R * Q * F, C), F32),
            pltpu.VMEM((16 * F, 128), F32),
            pltpu.VMEM((2, 32, C), F32),
            pltpu.VMEM((2, 16, C), F32),
        ],
        20, "finish", 60 * cell_flops, 20 * 2**20,
    )(left, right, top, bot, s1, inner2, rows2, raw, csw, chw, vec, w1v, w2v, wy)
    arrived = lax.all_to_all(slots.reshape(F * 8, 16, 128), ("ha", "wa"), 0, 0, tiled=True)
    return pl.pallas_call(
        last_kernel,
        out_shape=shape(128, 128),
        in_specs=[VM] * 2,
        out_specs=VM,
        scratch_shapes=[pltpu.VMEM((128, 128), F32)],
        compiler_params=pltpu.CompilerParams(vmem_limit_bytes=4 * 2**20),
        name="sum_patches",
    )(arrived, bias)


def solution(mesh):
    tile = P(None, "ha", "wa", None)
    return jax.shard_map(
        local,
        mesh=mesh,
        in_specs=(tile,) * 4 + (P(),) * 9,
        out_specs=P(("ha", "wa"), None),
        check_vma=False,
    )
```

```python
import jax
import jax.numpy as jnp
from jax import lax
from jax.experimental import pallas as pl
from jax.experimental.pallas import tpu as pltpu
from jax.sharding import PartitionSpec as P

BF16 = jnp.bfloat16
F32 = jnp.float32
F, R, Q, C = 16, 4, 8, 384
MSG = 19
VM = pl.BlockSpec(memory_space=pltpu.VMEM)
ANY = pl.BlockSpec(memory_space=pl.ANY)


def act(wide, half_gain):
    scale = lax.rsqrt(jnp.mean(wide * wide, axis=-1, keepdims=True) + 1e-06)
    h = wide * scale * half_gain
    return h + h * jnp.tanh(h)


def line(ref):
    return ref[...].reshape(1, -1)


def put_rows(ref, start, value):
    for n in range(3):
        ref[n, pl.ds(start, value.shape[0])] = value[:, n * 128 : (n + 1) * 128]


def rows_at(ref, start, count, stride):
    where = pl.ds(start, count, stride=stride) if stride > 1 else pl.ds(start, count)
    return jnp.concatenate([ref[n, where, :] for n in range(3)], axis=-1)


def stack(now, c0, c1):
    row = lax.broadcasted_iota(jnp.int32, now.shape, 0) % F
    c0, c1 = (jnp.concatenate([jnp.broadcast_to(c, (F, C)) for c in cs], axis=0) for cs in (c0, c1))
    one = jnp.where(row == 0, c1, pltpu.roll(now, 1, 0))
    two = jnp.where(row == 0, c0, jnp.where(row == 1, c1, pltpu.roll(now, 2, 0)))
    return two.astype(BF16), one.astype(BF16), now.astype(BF16)


def put(dst, where, now, c0, c1, valid=None):
    if valid is not None:
        keep = jnp.where(valid, 1.0, 0.0).astype(F32)
        now, c0, c1 = now * keep, [c * keep for c in c0], [c * keep for c in c1]
    for n, part in enumerate(stack(now, c0, c1)):
        dst[where + (slice(None), pl.ds(n * C, C))] = part.reshape(-1, F, C)


def bring(pairs, sems):
    copies = [pltpu.make_async_copy(src, dst, sems.at[n]) for n, (src, dst) in enumerate(pairs)]
    for copy in copies:
        copy.start()
    return copies


def first_kernel(
    feat_h, cf_h, cs_h, ch_h, g1_h, g2_h, gh_h, b1_h, b2_h, b3_h, own, plain, lo, hi, cfw, csw, chw, vec, bias,
    feat, caches, g1, g2, gh, b1, b2, b3, wide, sems,
):
    parts = [pl.ds(4 * n, 4) for n in range(4)]
    copies = bring(
        [(g1_h, g1)] + [(feat_h.at[part], feat.at[part]) for part in parts]
        + [(cf_h, caches.at[0]), (cs_h, caches.at[1]), (ch_h, caches.at[2]),
           (g2_h, g2), (gh_h, gh), (b1_h, b1), (b2_h, b2), (b3_h, b3)], sems
    )
    copies[0].wait()
    half = 0.5 * line(g1)
    for n, part in enumerate(parts):
        copies[1 + n].wait()
        x = feat[part].astype(F32).reshape(4 * R * Q, C)
        put_rows(plain, n * 4 * R * Q, x)
        put_rows(wide, n * 4 * R * Q, act(x, half))
    for k in range(R * Q):
        cell = rows_at(wide, k, F, R * Q).astype(BF16)
        own[k] = cell
        if k < 16:
            lo[k] = cell
        else:
            hi[k - 16] = cell
    for copy in copies[5:]:
        copy.wait()
    for n, value in enumerate((0.5 * line(g2), 0.5 * line(gh), line(b1), line(b2))):
        vec[pl.ds(n, 1)] = value
    bias[pl.ds(0, 1)] = jnp.concatenate([line(b3)] * 4, axis=-1)
    for n, out in enumerate((cfw, csw, chw)):
        for h in range(R):
            for f in range(2):
                put_rows(out, h * 16 + f * 8, caches[n, f, h].astype(F32))
    for n in range(2):
        lo[16 + n] = rows_at(cfw, n * 16, 16, 1).astype(BF16)
        hi[16 + n] = rows_at(cfw, (2 + n) * 16, 16, 1).astype(BF16)
    lo[18] = rows_at(csw, 0, 16, 1).astype(BF16)
    hi[18] = rows_at(csw, 48, 16, 1).astype(BF16)


def pack_kernel(own, top, bot, cfw, csw, after, left, right, wide_f, wide_s):
    del after
    for n in range(2):
        put_rows(wide_f, n * 16, top[16 + n].astype(F32))
        put_rows(wide_f, (6 + n) * 16, bot[16 + n].astype(F32))
    put_rows(wide_s, 0, top[18].astype(F32))
    put_rows(wide_s, 5 * 16, bot[18].astype(F32))
    for n in range(3):
        wide_f[n, pl.ds(32, 64)] = cfw[n]
        wide_s[n, pl.ds(16, 64)] = csw[n]
        wide_s[n, pl.ds(96, 32)] = jnp.zeros((32, 128), F32)
    for out, base, edge in ((left, 0, 0), (right, 6, 7)):
        for c in range(2):
            for h in range(8):
                w = base + c
                if h < 2:
                    cell = top[h * Q + w]
                elif h < 6:
                    cell = own[(h - 2) * Q + w]
                else:
                    cell = bot[(h - 6) * Q + w]
                out[h * 2 + c] = cell
            out[16 + c] = rows_at(wide_f, base + c, 16, 8).astype(BF16)
        out[18] = rows_at(wide_s, edge, 16, 8).astype(BF16)


def cached_row(ref, base, w0, count):
    return [[rows_at(ref, base + 8 * f + w0 + w, 1, 1) for w in range(count)] for f in range(2)]


def cached_msg(block, count=Q):
    block = block.astype(F32)
    return [[block[8 * f + w : 8 * f + w + 1] for w in range(count)] for f in range(2)]


def three(weight, a):
    return jnp.concatenate([weight[a, 3 * b : 3 * b + 3].reshape(3 * C, C) for b in range(3)], axis=-1)


def hidden(dst, where, total, vec, cached, valid=None):
    wide = (total + vec[pl.ds(2, 1), :]).astype(BF16).astype(F32)
    put(dst, where, act(wide, vec[pl.ds(0, 1), :]), cached[0], cached[1], valid)


def place():
    ha, wa = lax.axis_index("ha"), lax.axis_index("wa")
    return ha > 0, ha < lax.axis_size("ha") - 1, wa > 0, wa < lax.axis_size("wa") - 1


def inner_kernel(own, plain, cfw, csw, vec, w1, w2, wh, acc, s2, w1v, w2v, wy, raw, s1, sems):
    def group(src, dst, a, sem):
        return [
            pltpu.make_async_copy(src.at[t, a, b], dst.at[a, b * 3 + t], sem) for b in range(3) for t in range(3)
        ]

    first = [group(w1, w1v, a, sems.at[a]) for a in range(3)]
    later = [copy for a in range(3) for copy in group(w2, w2v, a, sems.at[3 + a])]
    for t in range(3):
        for a in range(3):
            for b in range(3):
                later.append(
                    pltpu.make_async_copy(
                        wh.at[t, a, b], wy.at[pl.ds(a * 128 + b * 32, 32), pl.ds(t * C, C)], sems.at[6]
                    )
                )
    for copies in first[:2]:
        for copy in copies:
            copy.start()
    for a in range(3):
        wy[pl.ds(a * 128 + 96, 32)] = jnp.zeros((32, 3 * C), BF16)
    acc[...] = jnp.zeros_like(acc)

    def cells(h, _):
        c0, c1 = cached_row(cfw, h * 16, 0, Q)
        put(s1, (pl.ds(h * Q, Q),), own[pl.ds(h * Q, Q)].reshape(Q * F, C).astype(F32), c0, c1)
        return 0

    lax.fori_loop(0, R, cells, 0)
    for a in range(3):
        for copy in first[a]:
            copy.wait()
        for copy in (first[2], later, ())[a]:
            copy.start()
        part = jnp.dot(s1[...].reshape(R * Q * F, 3 * C), three(w1v, a), preferred_element_type=F32)
        for b in range(3):
            acc[2 - a : 2 - a + R, 2 - b : 2 - b + Q] += part[:, b * C : (b + 1) * C].reshape(R, Q, F, C)
    for h in range(2):
        hidden(s2, (h, pl.ds(0, 6)), acc[2 + h, 2:8].reshape(6 * F, C), vec, cached_row(csw, (1 + h) * 16, 1, 6))
    for k in range(R * Q):
        raw[k] = rows_at(plain, k, F, R * Q).astype(BF16)
    for copy in later:
        copy.wait()


def rows_kernel(top, bot, acc, csw, vec, w1v, sides, s2, s1, add):
    up, down, _, _ = place()
    for msg, h0, valid in ((top, 0, up), (bot, 2, down)):
        for h in range(2):
            c0, c1 = cached_msg(msg[16 + h])
            put(s1, (h0 + h, pl.ds(0, Q)), msg[pl.ds(h * Q, Q)].reshape(Q * F, C).astype(F32), c0, c1, valid)
    add[0:2] = acc[0:2]
    add[2:4] = acc[4:6]
    for a, (low, targets) in enumerate(((0, (0, 1)), (1, (0, 3)), (2, (2, 3)))):
        part = jnp.dot(s1[low : low + 2].reshape(2 * Q * F, 3 * C), three(w1v, a), preferred_element_type=F32)
        for n, row in enumerate(targets):
            for b in range(3):
                block = part[n * Q * F : (n + 1) * Q * F, b * C : (b + 1) * C]
                add[row, 2 - b : 2 - b + Q] += block.reshape(Q, F, C)
    for n, cached, valid in (
        (0, [c[1:7] for c in cached_msg(top[18])], up),
        (1, cached_row(csw, 0, 1, 6), None),
        (2, cached_row(csw, 48, 1, 6), None),
        (3, [c[1:7] for c in cached_msg(bot[18])], down),
    ):
        hidden(s2, (n, pl.ds(0, 6)), add[n, 2:8].reshape(6 * F, C), vec, cached, valid)
    for n, col in enumerate((0, 8)):
        sides[0:2, 2 * n : 2 * n + 2] = add[0:2, col : col + 2]
        sides[2:4, 2 * n : 2 * n + 2] = acc[2:4, col : col + 2]
        sides[4:6, 2 * n : 2 * n + 2] = add[2:4, col : col + 2]


def finish_kernel(
    left, right, top, bot, sides, inner2, rows2, raw, csw, chw, vec, w1v, w2v, wy, out,
    s1, acc1, s2, s3, acc2, acch, side_f, side_s,
):
    up, down, west, east = place()
    for n, msg in enumerate((left, right)):
        for c in range(2):
            side_f[n, pl.ds(c * 16, 16)] = msg[16 + c].astype(F32)
        side_s[n] = msg[18].astype(F32)
    for n, (msg, side) in enumerate(((left, west), (right, east))):
        def cells(h, _, n=n, msg=msg, side=side):
            for k in range(2):
                hh = h * 2 + k
                put(
                    s1, (hh, pl.ds(2 * n, 2)), msg[pl.ds(hh * 2, 2)].reshape(2 * F, C).astype(F32),
                    [side_f[n, pl.ds(c * 16 + hh * 2, 1), :] for c in range(2)],
                    [side_f[n, pl.ds(c * 16 + hh * 2 + 1, 1), :] for c in range(2)],
                    side & (up | (hh >= 2)) & (down | (hh < 6)),
                )
            return 0

        lax.fori_loop(0, 4, cells, 0)

    acc1[...] = sides[...]
    for b, targets in enumerate(((0, 1), (0, 3), (2, 3))):
        taken = jnp.concatenate([s1[a : a + 6, b : b + 2].reshape(12 * F, 3 * C) for a in range(3)], axis=-1)
        weight = jnp.concatenate([w1v[a, 3 * b : 3 * b + 3].reshape(3 * C, C) for a in range(3)], axis=0)
        part = jnp.dot(taken, weight, preferred_element_type=F32).reshape(6, 2, F, C)
        for n, col in enumerate(targets):
            acc1[:, col] += part[:, n]
    s2[2:4, 2:8] = inner2[...]
    s2[0:2, 2:8] = rows2[0:2]
    s2[4:6, 2:8] = rows2[2:4]
    for h in range(6):
        inside = up if h == 0 else down if h == 5 else True
        if h == 0:
            c0, c1 = cached_msg(top[18])
        elif h == 5:
            c0, c1 = cached_msg(bot[18])
        else:
            c0, c1 = cached_row(csw, (h - 1) * 16, 0, Q)
        for n, side in enumerate((west, east)):
            first = [side_s[n, pl.ds(h * 2 + f, 1), :] for f in range(2)]
            keep = jnp.where(side, 1.0, 0.0).astype(F32)
            total = acc1[h, 2 * n : 2 * n + 2].reshape(2 * F, C)
            wide = (total + vec[pl.ds(2, 1), :]).astype(BF16).astype(F32)
            now = act(wide, vec[pl.ds(0, 1), :])
            own_w = 0 if n == 0 else Q - 1
            pair = [now[:F], now[F:]]
            pair[n] = pair[n] * keep
            now = jnp.concatenate(pair, axis=0)
            olds = []
            for f, c in enumerate((c0, c1)):
                two = [first[f] * keep, c[own_w]]
                olds.append(two if n == 0 else two[::-1])
            put(s2, (h, pl.ds(8 * n, 2)), now, olds[0], olds[1], None if inside is True else inside)

    def window(a, rows):
        return jnp.concatenate([s2[a : a + rows, b : b + Q].reshape(rows * Q * F, 3 * C) for b in range(3)], axis=-1)

    for a in range(3):
        part = jnp.dot(window(a, R), w2v[a, :, :, 0:256].reshape(9 * C, 256), preferred_element_type=F32)
        if a == 0:
            acc2[:, 0:256] = part
        else:
            acc2[:, 0:256] += part
    side = [w2v[a, :, :, 256:384].reshape(9 * C, 128) for a in range(3)]
    pair = jnp.dot(window(0, R + 1), jnp.concatenate(side[:2], axis=-1), preferred_element_type=F32)
    acc2[:, 256:384] = (
        pair[: R * Q * F, :128] + pair[Q * F :, 128:]
        + jnp.dot(window(2, R), side[2], preferred_element_type=F32)
    )

    def last(h, _):
        wide = acc2[pl.ds(h * Q * F, Q * F)] + vec[pl.ds(3, 1), :]
        wide = wide + raw[pl.ds(h * Q, Q)].reshape(Q * F, C).astype(F32)
        c0, c1 = cached_row(chw, h * 16, 0, Q)
        put(s3, (pl.ds(h * Q, Q),), act(wide.astype(BF16).astype(F32), vec[pl.ds(1, 1), :]), c0, c1)
        return 0

    lax.fori_loop(0, R, last, 0)
    part = lax.dot_general(
        s3[...].reshape(R * Q * F, 3 * C), wy[...], (((1,), (1,)), ((), ())), preferred_element_type=F32
    )
    lane = lax.broadcasted_iota(jnp.int32, (F, 128), 1)
    sums = {}
    for h in range(R):
        for w in range(Q):
            k = h * Q + w
            for a in range(3):
                block = part[k * F : (k + 1) * F, a * 128 : (a + 1) * 128]
                for b in range(3):
                    row, col = h + 1 - a, w + 1 - b
                    pp, qq = (row // 2) % 3, (col // 2) % 5
                    slot = pp * 4 + qq if qq < 4 else 12 + pp
                    low = (2 * (row % 2) + col % 2) * 32
                    shift = (low - 32 * b) % 128
                    moved = pltpu.roll(block, shift, 1) if shift else block
                    term = jnp.where((lane >= low) & (lane < low + 32), moved, 0.0)
                    sums[slot] = sums[slot] + term if slot in sums else term
    for slot, total in sums.items():
        acch[pl.ds(slot * F, F)] = total
    acch[pl.ds(15 * F, F)] = jnp.zeros((F, 128), F32)

    for f in range(F):
        patches = acch[pl.ds(f, 16, stride=F), :].astype(BF16)
        for g in range(8):
            out[f, g] = patches


def last_kernel(slots, bias, out, sums):
    ha_count = 16
    g = lax.axis_index("wa")
    first = [jnp.clip(2 * g - 1 + k, 0, ha_count - 1) * 8 for k in range(4)]

    def held(k, j, low, count):
        return slots[first[k] + j, pl.ds(low, count)].astype(F32)

    lane = lax.broadcasted_iota(jnp.int32, (4, 128), 1)
    row = lax.broadcasted_iota(jnp.int32, (4, 128), 0)
    for k in range(2):
        for pr in range(2):
            other = k if pr == 0 else k + 2
            there = (2 * g + k > 0) if pr == 0 else (2 * g + k < ha_count - 1)
            upright = ((lane < 64) if pr == 0 else (lane >= 64)) & there

            def edge(j, pr=pr, k=k, other=other, upright=upright):
                mine = jnp.broadcast_to(held(k + 1, j, 12 + pr, 1), (4, 128))
                theirs = jnp.broadcast_to(held(other, j, 14, 1), (4, 128))
                return mine + jnp.where(upright, theirs, 0.0)

            for j in range(8):
                total = held(k + 1, j, pr * 4, 4)
                total = total + jnp.where(upright, held(other, j, 8, 4), 0.0)
                if j > 0:
                    total = total + jnp.where((row == 0) & (lane % 64 < 32), edge(j - 1), 0.0)
                if j < 7:
                    total = total + jnp.where((row == 3) & (lane % 64 >= 32), edge(j + 1), 0.0)
                sums[pl.ds((2 * k + pr) * 32 + j * 4, 4)] = total + bias[pl.ds(0, 1), :]
    out[...] = sums[...].astype(BF16)


def shape(*dims, dtype=BF16):
    return jax.ShapeDtypeStruct(dims, dtype)


def near(*dims, dtype=BF16):
    return pltpu.VMEM(dims, dtype)


def far(array):
    return pltpu.with_memory_space_constraint(array, pltpu.HBM)


def kernel(body, outs, ins, scratch, limit, name, flops=0, moved=0):
    return pl.pallas_call(
        body,
        out_shape=outs,
        in_specs=ins,
        out_specs=[VM] * len(outs),
        scratch_shapes=scratch,
        compiler_params=pltpu.CompilerParams(vmem_limit_bytes=limit * 2**20),
        cost_estimate=pl.CostEstimate(flops=flops, bytes_accessed=moved, transcendentals=0),
        name=name,
    )


def around(axis, step):
    count = lax.axis_size(axis)
    return [(n, (n + step) % count) for n in range(count)]


def local(
    features, cache_first, cache_second, cache_head, gain_first, gain_second, gain_head,
    conv_first, conv_second, conv_head, bias_first, bias_second, bias_head,
):
    own, plain, lo, hi, cfw, csw, chw, vec, bias = kernel(
        first_kernel,
        [near(32, F, C), near(3, F * R * Q, 128, dtype=F32), near(MSG, F, C), near(MSG, F, C)]
        + [near(3, 64, 128, dtype=F32)] * 3 + [near(8, C, dtype=F32), near(8, 128, dtype=F32)],
        [ANY] * 10,
        [
            pltpu.VMEM((F, R, Q, C), BF16),
            pltpu.VMEM((3, 2, R, Q, C), BF16),
        ]
        + [pltpu.VMEM((C,), F32)] * 5
        + [
            pltpu.VMEM((32,), F32),
            pltpu.VMEM((3, F * R * Q, 128), F32),
            pltpu.SemaphoreType.DMA((13,)),
        ],
        12, "act_first",
    )(*[far(v) for v in (features, cache_first, cache_second, cache_head, gain_first, gain_second, gain_head,
                         bias_first, bias_second, bias_head)])
    top = lax.ppermute(hi, "ha", around("ha", 1))
    bot = lax.ppermute(lo, "ha", around("ha", -1))
    cell_flops = 2 * F * 27 * C * C
    sums1, inner2, w1v, w2v, wy, raw = kernel(
        inner_kernel,
        [near(R + 2, Q + 2, F, C, dtype=F32), near(2, 6, F, 3 * C), near(3, 9, C, C), near(3, 9, C, C), near(3 * 128, 3 * C),
         near(32, F, C)],
        [VM] * 5 + [ANY] * 3,
        [pltpu.VMEM((R * Q, F, 3 * C), BF16), pltpu.SemaphoreType.DMA((7,))],
        12, "inner", 32 * cell_flops, 17 * 2**20,
    )(own, plain, cfw, csw, vec, far(conv_first), far(conv_second), far(jnp.swapaxes(conv_head, 3, 4)))
    to_left, to_right = kernel(
        pack_kernel,
        [near(MSG, F, C)] * 2,
        [VM] * 6,
        [pltpu.VMEM((3, 128, 128), F32)] * 2,
        4, "pack_columns",
    )(own, top, bot, cfw, csw, inner2)
    left = lax.ppermute(to_right, "wa", around("wa", 1))
    right = lax.ppermute(to_left, "wa", around("wa", -1))
    sides, rows2 = kernel(
        rows_kernel,
        [near(R + 2, 4, F, C, dtype=F32), near(4, 6, F, 3 * C)],
        [VM] * 6,
        [pltpu.VMEM((4, Q, F, 3 * C), BF16), pltpu.VMEM((4, Q + 2, F, C), F32)],
        10, "rows", 16 * cell_flops, 10 * 2**20,
    )(top, bot, sums1, csw, vec, w1v)
    (slots,) = kernel(
        finish_kernel,
        [shape(F, 8, 16, 128)],
        [VM] * 14,
        [
            pltpu.VMEM((8, 4, F, 3 * C), BF16),
            pltpu.VMEM((R + 2, 4, F, C), F32),
            pltpu.VMEM((R + 2, Q + 2, F, 3 * C), BF16),
            pltpu.VMEM((R * Q, F, 3 * C), BF16),
            pltpu.VMEM((R * Q * F, C), F32),
            pltpu.VMEM((16 * F, 128), F32),
            pltpu.VMEM((2, 32, C), F32),
            pltpu.VMEM((2, 16, C), F32),
        ],
        20, "finish", 48 * cell_flops, 20 * 2**20,
    )(left, right, top, bot, sides, inner2, rows2, raw, csw, chw, vec, w1v, w2v, wy)
    arrived = lax.all_to_all(slots.reshape(F * 8, 16, 128), ("ha", "wa"), 0, 0, tiled=True)
    return pl.pallas_call(
        last_kernel,
        out_shape=shape(128, 128),
        in_specs=[VM] * 2,
        out_specs=VM,
        scratch_shapes=[pltpu.VMEM((128, 128), F32)],
        compiler_params=pltpu.CompilerParams(vmem_limit_bytes=4 * 2**20),
        name="sum_patches",
    )(arrived, bias)


def solution(mesh):
    tile = P(None, "ha", "wa", None)
    return jax.shard_map(
        local,
        mesh=mesh,
        in_specs=(tile,) * 4 + (P(),) * 9,
        out_specs=P(("ha", "wa"), None),
        check_vma=False,
    )
```

```python
import jax
import jax.numpy as jnp
from jax import lax
from jax.experimental import pallas as pl
from jax.experimental.pallas import tpu as pltpu
from jax.sharding import PartitionSpec as P

BF16 = jnp.bfloat16
F32 = jnp.float32
F, R, Q, C = 16, 4, 8, 384
MSG = 19
VM = pl.BlockSpec(memory_space=pltpu.VMEM)
ANY = pl.BlockSpec(memory_space=pl.ANY)


def act(wide, half_gain):
    scale = lax.rsqrt(jnp.mean(wide * wide, axis=-1, keepdims=True) + 1e-06)
    h = wide * scale * half_gain
    return h + h * jnp.tanh(h)


def line(ref):
    return ref[...].reshape(1, -1)


def put_rows(ref, start, value):
    for n in range(3):
        ref[n, pl.ds(start, value.shape[0])] = value[:, n * 128 : (n + 1) * 128]


def rows_at(ref, start, count, stride):
    where = pl.ds(start, count, stride=stride) if stride > 1 else pl.ds(start, count)
    return jnp.concatenate([ref[n, where, :] for n in range(3)], axis=-1)


def stack(now, c0, c1):
    row = lax.broadcasted_iota(jnp.int32, now.shape, 0) % F
    c0, c1 = (jnp.concatenate([jnp.broadcast_to(c, (F, C)) for c in cs], axis=0) for cs in (c0, c1))
    one = jnp.where(row == 0, c1, pltpu.roll(now, 1, 0))
    two = jnp.where(row == 0, c0, jnp.where(row == 1, c1, pltpu.roll(now, 2, 0)))
    return two.astype(BF16), one.astype(BF16), now.astype(BF16)


def put(dst, where, now, c0, c1, valid=None):
    if valid is not None:
        keep = jnp.where(valid, 1.0, 0.0).astype(F32)
        now, c0, c1 = now * keep, [c * keep for c in c0], [c * keep for c in c1]
    for n, part in enumerate(stack(now, c0, c1)):
        dst[where + (slice(None), pl.ds(n * C, C))] = part.reshape(-1, F, C)


def bring(pairs, sems):
    copies = [pltpu.make_async_copy(src, dst, sems.at[n]) for n, (src, dst) in enumerate(pairs)]
    for copy in copies:
        copy.start()
    return copies


def first_kernel(
    feat_h, cf_h, cs_h, ch_h, g1_h, g2_h, gh_h, b1_h, b2_h, b3_h, own, plain, lo, hi, cfw, csw, chw, vec, bias,
    feat, caches, g1, g2, gh, b1, b2, b3, wide, sems,
):
    parts = [pl.ds(4 * n, 4) for n in range(4)]
    copies = bring(
        [(g1_h, g1)] + [(feat_h.at[part], feat.at[part]) for part in parts]
        + [(cf_h, caches.at[0]), (cs_h, caches.at[1]), (ch_h, caches.at[2]),
           (g2_h, g2), (gh_h, gh), (b1_h, b1), (b2_h, b2), (b3_h, b3)], sems
    )
    copies[0].wait()
    half = 0.5 * line(g1)
    for n, part in enumerate(parts):
        copies[1 + n].wait()
        x = feat[part].astype(F32).reshape(4 * R * Q, C)
        put_rows(plain, n * 4 * R * Q, x)
        put_rows(wide, n * 4 * R * Q, act(x, half))
    for k in range(R * Q):
        cell = rows_at(wide, k, F, R * Q).astype(BF16)
        own[k] = cell
        if k < 16:
            lo[k] = cell
        else:
            hi[k - 16] = cell
    for copy in copies[5:]:
        copy.wait()
    for n, value in enumerate((0.5 * line(g2), 0.5 * line(gh), line(b1), line(b2))):
        vec[pl.ds(n, 1)] = value
    bias[pl.ds(0, 1)] = jnp.concatenate([line(b3)] * 4, axis=-1)
    for n, out in enumerate((cfw, csw, chw)):
        for h in range(R):
            for f in range(2):
                put_rows(out, h * 16 + f * 8, caches[n, f, h].astype(F32))
    for n in range(2):
        lo[16 + n] = rows_at(cfw, n * 16, 16, 1).astype(BF16)
        hi[16 + n] = rows_at(cfw, (2 + n) * 16, 16, 1).astype(BF16)
    lo[18] = rows_at(csw, 0, 16, 1).astype(BF16)
    hi[18] = rows_at(csw, 48, 16, 1).astype(BF16)


def pack_kernel(own, top, bot, cfw, csw, after, left, right, wide_f, wide_s):
    del after
    for n in range(2):
        put_rows(wide_f, n * 16, top[16 + n].astype(F32))
        put_rows(wide_f, (6 + n) * 16, bot[16 + n].astype(F32))
    put_rows(wide_s, 0, top[18].astype(F32))
    put_rows(wide_s, 5 * 16, bot[18].astype(F32))
    for n in range(3):
        wide_f[n, pl.ds(32, 64)] = cfw[n]
        wide_s[n, pl.ds(16, 64)] = csw[n]
        wide_s[n, pl.ds(96, 32)] = jnp.zeros((32, 128), F32)
    for out, base, edge in ((left, 0, 0), (right, 6, 7)):
        for c in range(2):
            for h in range(8):
                w = base + c
                if h < 2:
                    cell = top[h * Q + w]
                elif h < 6:
                    cell = own[(h - 2) * Q + w]
                else:
                    cell = bot[(h - 6) * Q + w]
                out[h * 2 + c] = cell
            out[16 + c] = rows_at(wide_f, base + c, 16, 8).astype(BF16)
        out[18] = rows_at(wide_s, edge, 16, 8).astype(BF16)


def cached_row(ref, base, w0, count):
    return [[rows_at(ref, base + 8 * f + w0 + w, 1, 1) for w in range(count)] for f in range(2)]


def cached_msg(block, count=Q):
    block = block.astype(F32)
    return [[block[8 * f + w : 8 * f + w + 1] for w in range(count)] for f in range(2)]


def three(weight, a):
    return jnp.concatenate([weight[a, 3 * b : 3 * b + 3].reshape(3 * C, C) for b in range(3)], axis=-1)


def hidden(dst, where, total, vec, cached, valid=None):
    wide = (total + vec[pl.ds(2, 1), :]).astype(BF16).astype(F32)
    put(dst, where, act(wide, vec[pl.ds(0, 1), :]), cached[0], cached[1], valid)


def place():
    ha, wa = lax.axis_index("ha"), lax.axis_index("wa")
    return ha > 0, ha < lax.axis_size("ha") - 1, wa > 0, wa < lax.axis_size("wa") - 1


def inner_kernel(own, cfw, w1, w2, wh, acc, w1v, w2v, wy, s1, sems):
    def group(src, dst, a, sem):
        return [
            pltpu.make_async_copy(src.at[t, a, b], dst.at[a, b * 3 + t], sem) for b in range(3) for t in range(3)
        ]

    first = [group(w1, w1v, a, sems.at[a]) for a in range(3)]
    later = [copy for a in range(3) for copy in group(w2, w2v, a, sems.at[3 + a])]
    for t in range(3):
        for a in range(3):
            for b in range(3):
                later.append(
                    pltpu.make_async_copy(
                        wh.at[t, a, b], wy.at[pl.ds(a * 128 + b * 32, 32), pl.ds(t * C, C)], sems.at[6]
                    )
                )
    for copies in first[:2]:
        for copy in copies:
            copy.start()
    for a in range(3):
        wy[pl.ds(a * 128 + 96, 32)] = jnp.zeros((32, 3 * C), BF16)
    acc[...] = jnp.zeros_like(acc)

    def cells(h, _):
        c0, c1 = cached_row(cfw, h * 16, 0, Q)
        put(s1, (pl.ds(h * Q, Q),), own[pl.ds(h * Q, Q)].reshape(Q * F, C).astype(F32), c0, c1)
        return 0

    lax.fori_loop(0, R, cells, 0)
    for a in range(3):
        for copy in first[a]:
            copy.wait()
        for copy in (first[2], later, ())[a]:
            copy.start()
        part = jnp.dot(s1[...].reshape(R * Q * F, 3 * C), three(w1v, a), preferred_element_type=F32)
        for b in range(3):
            acc[2 - a : 2 - a + R, 2 - b : 2 - b + Q] += part[:, b * C : (b + 1) * C].reshape(R, Q, F, C)
    for copy in later:
        copy.wait()


def rows_kernel(top, bot, acc, plain, csw, vec, w1v, sides, s2, raw, s1, add):
    up, down, _, _ = place()
    for msg, h0, valid in ((top, 0, up), (bot, 2, down)):
        for h in range(2):
            c0, c1 = cached_msg(msg[16 + h])
            put(s1, (h0 + h, pl.ds(0, Q)), msg[pl.ds(h * Q, Q)].reshape(Q * F, C).astype(F32), c0, c1, valid)
    add[0:2] = acc[0:2]
    add[2:4] = acc[4:6]
    for a, (low, targets) in enumerate(((0, (0, 1)), (1, (0, 3)), (2, (2, 3)))):
        part = jnp.dot(s1[low : low + 2].reshape(2 * Q * F, 3 * C), three(w1v, a), preferred_element_type=F32)
        for n, row in enumerate(targets):
            for b in range(3):
                block = part[n * Q * F : (n + 1) * Q * F, b * C : (b + 1) * C]
                add[row, 2 - b : 2 - b + Q] += block.reshape(Q, F, C)
    for n, cached, valid in (
        (0, [c[1:7] for c in cached_msg(top[18])], up),
        (1, cached_row(csw, 0, 1, 6), None),
        (2, cached_row(csw, 16, 1, 6), None),
        (3, cached_row(csw, 32, 1, 6), None),
        (4, cached_row(csw, 48, 1, 6), None),
        (5, [c[1:7] for c in cached_msg(bot[18])], down),
    ):
        total = acc[n, 2:8] if 2 <= n < 4 else add[n if n < 2 else n - 2, 2:8]
        hidden(s2, (n, pl.ds(0, 6)), total.reshape(6 * F, C), vec, cached, valid)
    for k in range(R * Q):
        raw[k] = rows_at(plain, k, F, R * Q).astype(BF16)
    for n, col in enumerate((0, 8)):
        sides[0:2, 2 * n : 2 * n + 2] = add[0:2, col : col + 2]
        sides[2:4, 2 * n : 2 * n + 2] = acc[2:4, col : col + 2]
        sides[4:6, 2 * n : 2 * n + 2] = add[2:4, col : col + 2]


def finish_kernel(
    left, right, top, bot, sides, rows2, raw, csw, chw, vec, w1v, w2v, wy, out,
    s1, acc1, s2, s3, acc2, acch, side_f, side_s,
):
    up, down, west, east = place()
    for n, msg in enumerate((left, right)):
        for c in range(2):
            side_f[n, pl.ds(c * 16, 16)] = msg[16 + c].astype(F32)
        side_s[n] = msg[18].astype(F32)
    for n, (msg, side) in enumerate(((left, west), (right, east))):
        def cells(h, _, n=n, msg=msg, side=side):
            for k in range(2):
                hh = h * 2 + k
                put(
                    s1, (hh, pl.ds(2 * n, 2)), msg[pl.ds(hh * 2, 2)].reshape(2 * F, C).astype(F32),
                    [side_f[n, pl.ds(c * 16 + hh * 2, 1), :] for c in range(2)],
                    [side_f[n, pl.ds(c * 16 + hh * 2 + 1, 1), :] for c in range(2)],
                    side & (up | (hh >= 2)) & (down | (hh < 6)),
                )
            return 0

        lax.fori_loop(0, 4, cells, 0)

    acc1[...] = sides[...]
    for b, targets in enumerate(((0, 1), (0, 3), (2, 3))):
        taken = jnp.concatenate([s1[a : a + 6, b : b + 2].reshape(12 * F, 3 * C) for a in range(3)], axis=-1)
        weight = jnp.concatenate([w1v[a, 3 * b : 3 * b + 3].reshape(3 * C, C) for a in range(3)], axis=0)
        part = jnp.dot(taken, weight, preferred_element_type=F32).reshape(6, 2, F, C)
        for n, col in enumerate(targets):
            acc1[:, col] += part[:, n]
    s2[:, 2:8] = rows2[...]
    for h in range(6):
        inside = up if h == 0 else down if h == 5 else True
        if h == 0:
            c0, c1 = cached_msg(top[18])
        elif h == 5:
            c0, c1 = cached_msg(bot[18])
        else:
            c0, c1 = cached_row(csw, (h - 1) * 16, 0, Q)
        for n, side in enumerate((west, east)):
            first = [side_s[n, pl.ds(h * 2 + f, 1), :] for f in range(2)]
            keep = jnp.where(side, 1.0, 0.0).astype(F32)
            total = acc1[h, 2 * n : 2 * n + 2].reshape(2 * F, C)
            wide = (total + vec[pl.ds(2, 1), :]).astype(BF16).astype(F32)
            now = act(wide, vec[pl.ds(0, 1), :])
            own_w = 0 if n == 0 else Q - 1
            pair = [now[:F], now[F:]]
            pair[n] = pair[n] * keep
            now = jnp.concatenate(pair, axis=0)
            olds = []
            for f, c in enumerate((c0, c1)):
                two = [first[f] * keep, c[own_w]]
                olds.append(two if n == 0 else two[::-1])
            put(s2, (h, pl.ds(8 * n, 2)), now, olds[0], olds[1], None if inside is True else inside)

    def window(a, rows):
        return jnp.concatenate([s2[a : a + rows, b : b + Q].reshape(rows * Q * F, 3 * C) for b in range(3)], axis=-1)

    for a in range(3):
        part = jnp.dot(window(a, R), w2v[a, :, :, 0:256].reshape(9 * C, 256), preferred_element_type=F32)
        if a == 0:
            acc2[:, 0:256] = part
        else:
            acc2[:, 0:256] += part
    side = [w2v[a, :, :, 256:384].reshape(9 * C, 128) for a in range(3)]
    pair = jnp.dot(window(0, R + 1), jnp.concatenate(side[:2], axis=-1), preferred_element_type=F32)
    acc2[:, 256:384] = (
        pair[: R * Q * F, :128] + pair[Q * F :, 128:]
        + jnp.dot(window(2, R), side[2], preferred_element_type=F32)
    )

    def last(h, _):
        wide = acc2[pl.ds(h * Q * F, Q * F)] + vec[pl.ds(3, 1), :]
        wide = wide + raw[pl.ds(h * Q, Q)].reshape(Q * F, C).astype(F32)
        c0, c1 = cached_row(chw, h * 16, 0, Q)
        put(s3, (pl.ds(h * Q, Q),), act(wide.astype(BF16).astype(F32), vec[pl.ds(1, 1), :]), c0, c1)
        return 0

    lax.fori_loop(0, R, last, 0)
    part = lax.dot_general(
        s3[...].reshape(R * Q * F, 3 * C), wy[...], (((1,), (1,)), ((), ())), preferred_element_type=F32
    )
    lane = lax.broadcasted_iota(jnp.int32, (F, 128), 1)
    sums = {}
    for h in range(R):
        for w in range(Q):
            k = h * Q + w
            for a in range(3):
                block = part[k * F : (k + 1) * F, a * 128 : (a + 1) * 128]
                for b in range(3):
                    row, col = h + 1 - a, w + 1 - b
                    pp, qq = (row // 2) % 3, (col // 2) % 5
                    slot = pp * 4 + qq if qq < 4 else 12 + pp
                    low = (2 * (row % 2) + col % 2) * 32
                    shift = (low - 32 * b) % 128
                    moved = pltpu.roll(block, shift, 1) if shift else block
                    term = jnp.where((lane >= low) & (lane < low + 32), moved, 0.0)
                    sums[slot] = sums[slot] + term if slot in sums else term
    for slot, total in sums.items():
        acch[pl.ds(slot * F, F)] = total
    acch[pl.ds(15 * F, F)] = jnp.zeros((F, 128), F32)

    for f in range(F):
        patches = acch[pl.ds(f, 16, stride=F), :].astype(BF16)
        for g in range(8):
            out[f, g] = patches


def last_kernel(slots, bias, out, sums):
    ha_count = 16
    g = lax.axis_index("wa")
    first = [jnp.clip(2 * g - 1 + k, 0, ha_count - 1) * 8 for k in range(4)]

    def held(k, j, low, count):
        return slots[first[k] + j, pl.ds(low, count)].astype(F32)

    lane = lax.broadcasted_iota(jnp.int32, (4, 128), 1)
    row = lax.broadcasted_iota(jnp.int32, (4, 128), 0)
    for k in range(2):
        for pr in range(2):
            other = k if pr == 0 else k + 2
            there = (2 * g + k > 0) if pr == 0 else (2 * g + k < ha_count - 1)
            upright = ((lane < 64) if pr == 0 else (lane >= 64)) & there

            def edge(j, pr=pr, k=k, other=other, upright=upright):
                mine = jnp.broadcast_to(held(k + 1, j, 12 + pr, 1), (4, 128))
                theirs = jnp.broadcast_to(held(other, j, 14, 1), (4, 128))
                return mine + jnp.where(upright, theirs, 0.0)

            for j in range(8):
                total = held(k + 1, j, pr * 4, 4)
                total = total + jnp.where(upright, held(other, j, 8, 4), 0.0)
                if j > 0:
                    total = total + jnp.where((row == 0) & (lane % 64 < 32), edge(j - 1), 0.0)
                if j < 7:
                    total = total + jnp.where((row == 3) & (lane % 64 >= 32), edge(j + 1), 0.0)
                sums[pl.ds((2 * k + pr) * 32 + j * 4, 4)] = total + bias[pl.ds(0, 1), :]
    out[...] = sums[...].astype(BF16)


def shape(*dims, dtype=BF16):
    return jax.ShapeDtypeStruct(dims, dtype)


def near(*dims, dtype=BF16):
    return pltpu.VMEM(dims, dtype)


def far(array):
    return pltpu.with_memory_space_constraint(array, pltpu.HBM)


def kernel(body, outs, ins, scratch, limit, name, flops=0, moved=0):
    return pl.pallas_call(
        body,
        out_shape=outs,
        in_specs=ins,
        out_specs=[VM] * len(outs),
        scratch_shapes=scratch,
        compiler_params=pltpu.CompilerParams(vmem_limit_bytes=limit * 2**20),
        cost_estimate=pl.CostEstimate(flops=flops, bytes_accessed=moved, transcendentals=0),
        name=name,
    )


def around(axis, step):
    count = lax.axis_size(axis)
    return [(n, (n + step) % count) for n in range(count)]


def local(
    features, cache_first, cache_second, cache_head, gain_first, gain_second, gain_head,
    conv_first, conv_second, conv_head, bias_first, bias_second, bias_head,
):
    own, plain, lo, hi, cfw, csw, chw, vec, bias = kernel(
        first_kernel,
        [near(32, F, C), near(3, F * R * Q, 128, dtype=F32), near(MSG, F, C), near(MSG, F, C)]
        + [near(3, 64, 128, dtype=F32)] * 3 + [near(8, C, dtype=F32), near(8, 128, dtype=F32)],
        [ANY] * 10,
        [
            pltpu.VMEM((F, R, Q, C), BF16),
            pltpu.VMEM((3, 2, R, Q, C), BF16),
        ]
        + [pltpu.VMEM((C,), F32)] * 5
        + [
            pltpu.VMEM((32,), F32),
            pltpu.VMEM((3, F * R * Q, 128), F32),
            pltpu.SemaphoreType.DMA((13,)),
        ],
        12, "act_first",
    )(*[far(v) for v in (features, cache_first, cache_second, cache_head, gain_first, gain_second, gain_head,
                         bias_first, bias_second, bias_head)])
    top = lax.ppermute(hi, "ha", around("ha", 1))
    bot = lax.ppermute(lo, "ha", around("ha", -1))
    cell_flops = 2 * F * 27 * C * C
    sums1, w1v, w2v, wy = kernel(
        inner_kernel,
        [near(R + 2, Q + 2, F, C, dtype=F32), near(3, 9, C, C), near(3, 9, C, C), near(3 * 128, 3 * C)],
        [VM] * 2 + [ANY] * 3,
        [pltpu.VMEM((R * Q, F, 3 * C), BF16), pltpu.SemaphoreType.DMA((7,))],
        12, "inner", 32 * cell_flops, 17 * 2**20,
    )(own, cfw, far(conv_first), far(conv_second), far(jnp.swapaxes(conv_head, 3, 4)))
    to_left, to_right = kernel(
        pack_kernel,
        [near(MSG, F, C)] * 2,
        [VM] * 6,
        [pltpu.VMEM((3, 128, 128), F32)] * 2,
        4, "pack_columns",
    )(own, top, bot, cfw, csw, wy)
    left = lax.ppermute(to_right, "wa", around("wa", 1))
    right = lax.ppermute(to_left, "wa", around("wa", -1))
    sides, rows2, raw = kernel(
        rows_kernel,
        [near(R + 2, 4, F, C, dtype=F32), near(R + 2, 6, F, 3 * C), near(32, F, C)],
        [VM] * 7,
        [pltpu.VMEM((4, Q, F, 3 * C), BF16), pltpu.VMEM((4, Q + 2, F, C), F32)],
        10, "rows", 16 * cell_flops, 10 * 2**20,
    )(top, bot, sums1, plain, csw, vec, w1v)
    (slots,) = kernel(
        finish_kernel,
        [shape(F, 8, 16, 128)],
        [VM] * 13,
        [
            pltpu.VMEM((8, 4, F, 3 * C), BF16),
            pltpu.VMEM((R + 2, 4, F, C), F32),
            pltpu.VMEM((R + 2, Q + 2, F, 3 * C), BF16),
            pltpu.VMEM((R * Q, F, 3 * C), BF16),
            pltpu.VMEM((R * Q * F, C), F32),
            pltpu.VMEM((16 * F, 128), F32),
            pltpu.VMEM((2, 32, C), F32),
            pltpu.VMEM((2, 16, C), F32),
        ],
        20, "finish", 48 * cell_flops, 20 * 2**20,
    )(left, right, top, bot, sides, rows2, raw, csw, chw, vec, w1v, w2v, wy)
    arrived = lax.all_to_all(slots.reshape(F * 8, 16, 128), ("ha", "wa"), 0, 0, tiled=True)
    return pl.pallas_call(
        last_kernel,
        out_shape=shape(128, 128),
        in_specs=[VM] * 2,
        out_specs=VM,
        scratch_shapes=[pltpu.VMEM((128, 128), F32)],
        compiler_params=pltpu.CompilerParams(vmem_limit_bytes=4 * 2**20),
        name="sum_patches",
    )(arrived, bias)


def solution(mesh):
    tile = P(None, "ha", "wa", None)
    return jax.shard_map(
        local,
        mesh=mesh,
        in_specs=(tile,) * 4 + (P(),) * 9,
        out_specs=P(("ha", "wa"), None),
        check_vma=False,
    )
```

```python
import jax
import jax.numpy as jnp
from jax import lax
from jax.experimental import pallas as pl
from jax.experimental.pallas import tpu as pltpu
from jax.sharding import PartitionSpec as P

BF16 = jnp.bfloat16
F32 = jnp.float32
F, R, Q, C = 16, 4, 8, 384
MSG = 19
VM = pl.BlockSpec(memory_space=pltpu.VMEM)
ANY = pl.BlockSpec(memory_space=pl.ANY)


def act(wide, half_gain):
    scale = lax.rsqrt(jnp.mean(wide * wide, axis=-1, keepdims=True) + 1e-06)
    h = wide * scale * half_gain
    return h + h * jnp.tanh(h)


def line(ref):
    return ref[...].reshape(1, -1)


def put_rows(ref, start, value):
    for n in range(3):
        ref[n, pl.ds(start, value.shape[0])] = value[:, n * 128 : (n + 1) * 128]


def rows_at(ref, start, count, stride):
    where = pl.ds(start, count, stride=stride) if stride > 1 else pl.ds(start, count)
    return jnp.concatenate([ref[n, where, :] for n in range(3)], axis=-1)


def stack(now, c0, c1):
    row = lax.broadcasted_iota(jnp.int32, now.shape, 0) % F
    c0, c1 = (jnp.concatenate([jnp.broadcast_to(c, (F, C)) for c in cs], axis=0) for cs in (c0, c1))
    one = jnp.where(row == 0, c1, pltpu.roll(now, 1, 0))
    two = jnp.where(row == 0, c0, jnp.where(row == 1, c1, pltpu.roll(now, 2, 0)))
    return two.astype(BF16), one.astype(BF16), now.astype(BF16)


def put(dst, where, now, c0, c1, valid=None):
    if valid is not None:
        keep = jnp.where(valid, 1.0, 0.0).astype(F32)
        now, c0, c1 = now * keep, [c * keep for c in c0], [c * keep for c in c1]
    for n, part in enumerate(stack(now, c0, c1)):
        dst[where + (slice(None), pl.ds(n * C, C))] = part.reshape(-1, F, C)


def bring(pairs, sems):
    copies = [pltpu.make_async_copy(src, dst, sems.at[n]) for n, (src, dst) in enumerate(pairs)]
    for copy in copies:
        copy.start()
    return copies


def first_kernel(
    feat_h, cf_h, cs_h, ch_h, g1_h, g2_h, gh_h, b1_h, b2_h, b3_h, own, plain, lo, hi, cfw, csw, chw, vec, bias,
    feat, caches, g1, g2, gh, b1, b2, b3, wide, sems,
):
    parts = [pl.ds(4 * n, 4) for n in range(4)]
    copies = bring(
        [(g1_h, g1)] + [(feat_h.at[part], feat.at[part]) for part in parts]
        + [(cf_h, caches.at[0]), (cs_h, caches.at[1]), (ch_h, caches.at[2]),
           (g2_h, g2), (gh_h, gh), (b1_h, b1), (b2_h, b2), (b3_h, b3)], sems
    )
    copies[0].wait()
    half = 0.5 * line(g1)
    for n, part in enumerate(parts):
        copies[1 + n].wait()
        x = feat[part].astype(F32).reshape(4 * R * Q, C)
        put_rows(plain, n * 4 * R * Q, x)
        put_rows(wide, n * 4 * R * Q, act(x, half))
    for k in range(R * Q):
        cell = rows_at(wide, k, F, R * Q).astype(BF16)
        own[k] = cell
        if k < 16:
            lo[k] = cell
        else:
            hi[k - 16] = cell
    for copy in copies[5:]:
        copy.wait()
    for n, value in enumerate((0.5 * line(g2), 0.5 * line(gh), line(b1), line(b2))):
        vec[pl.ds(n, 1)] = value
    bias[pl.ds(0, 1)] = jnp.concatenate([line(b3)] * 4, axis=-1)
    for n, out in enumerate((cfw, csw, chw)):
        for h in range(R):
            for f in range(2):
                put_rows(out, h * 16 + f * 8, caches[n, f, h].astype(F32))
    for n in range(2):
        lo[16 + n] = rows_at(cfw, n * 16, 16, 1).astype(BF16)
        hi[16 + n] = rows_at(cfw, (2 + n) * 16, 16, 1).astype(BF16)
    lo[18] = rows_at(csw, 0, 16, 1).astype(BF16)
    hi[18] = rows_at(csw, 48, 16, 1).astype(BF16)


def pack_kernel(own, top, bot, cfw, csw, after, left, right, wide_f, wide_s):
    del after
    for n in range(2):
        put_rows(wide_f, n * 16, top[16 + n].astype(F32))
        put_rows(wide_f, (6 + n) * 16, bot[16 + n].astype(F32))
    put_rows(wide_s, 0, top[18].astype(F32))
    put_rows(wide_s, 5 * 16, bot[18].astype(F32))
    for n in range(3):
        wide_f[n, pl.ds(32, 64)] = cfw[n]
        wide_s[n, pl.ds(16, 64)] = csw[n]
        wide_s[n, pl.ds(96, 32)] = jnp.zeros((32, 128), F32)
    for out, base, edge in ((left, 0, 0), (right, 6, 7)):
        for c in range(2):
            for h in range(8):
                w = base + c
                if h < 2:
                    cell = top[h * Q + w]
                elif h < 6:
                    cell = own[(h - 2) * Q + w]
                else:
                    cell = bot[(h - 6) * Q + w]
                out[h * 2 + c] = cell
            out[16 + c] = rows_at(wide_f, base + c, 16, 8).astype(BF16)
        out[18] = rows_at(wide_s, edge, 16, 8).astype(BF16)


def cached_row(ref, base, w0, count):
    return [[rows_at(ref, base + 8 * f + w0 + w, 1, 1) for w in range(count)] for f in range(2)]


def cached_msg(block, count=Q):
    block = block.astype(F32)
    return [[block[8 * f + w : 8 * f + w + 1] for w in range(count)] for f in range(2)]


def three(weight, a):
    return jnp.concatenate([weight[a, 3 * b : 3 * b + 3].reshape(3 * C, C) for b in range(3)], axis=-1)


def hidden(dst, where, total, vec, cached, valid=None):
    wide = (total + vec[pl.ds(2, 1), :]).astype(BF16).astype(F32)
    put(dst, where, act(wide, vec[pl.ds(0, 1), :]), cached[0], cached[1], valid)


def place():
    ha, wa = lax.axis_index("ha"), lax.axis_index("wa")
    return ha > 0, ha < lax.axis_size("ha") - 1, wa > 0, wa < lax.axis_size("wa") - 1


def reach(rh, rw):
    return [
        (2 * (rh - 1 + m) + r, 2 * (rw - 1 + n) + s)
        for m in range(2) for n in range(2) for r in range(2) for s in range(2)
    ]


def inner_kernel(own, cfw, w1, w2, wh, acc, w1v, w2v, wy, s1, sems):
    def group(src, dst, a, sem):
        return [
            pltpu.make_async_copy(src.at[t, a, b], dst.at[a, b * 3 + t], sem) for b in range(3) for t in range(3)
        ]

    first = [group(w1, w1v, a, sems.at[a]) for a in range(3)]
    later = [copy for a in range(3) for copy in group(w2, w2v, a, sems.at[3 + a])]
    empty = []
    for rh in range(2):
        for rw in range(2):
            for k, (row, col) in enumerate(reach(rh, rw)):
                a, b = rh + 1 - row, rw + 1 - col
                where = pl.ds(k * 32, 32)
                if 0 <= a <= 2 and 0 <= b <= 2:
                    for t in range(3):
                        later.append(
                            pltpu.make_async_copy(
                                wh.at[t, a, b], wy.at[rh * 2 + rw, where, pl.ds(t * C, C)], sems.at[6]
                            )
                        )
                else:
                    empty.append((rh * 2 + rw, where))
    for copies in first[:2]:
        for copy in copies:
            copy.start()
    for where in empty:
        wy[where] = jnp.zeros((32, 3 * C), BF16)
    acc[...] = jnp.zeros_like(acc)

    def cells(h, _):
        c0, c1 = cached_row(cfw, h * 16, 0, Q)
        put(s1, (pl.ds(h * Q, Q),), own[pl.ds(h * Q, Q)].reshape(Q * F, C).astype(F32), c0, c1)
        return 0

    lax.fori_loop(0, R, cells, 0)
    for a in range(3):
        for copy in first[a]:
            copy.wait()
        for copy in (first[2], later, ())[a]:
            copy.start()
        part = jnp.dot(s1[...].reshape(R * Q * F, 3 * C), three(w1v, a), preferred_element_type=F32)
        for b in range(3):
            acc[2 - a : 2 - a + R, 2 - b : 2 - b + Q] += part[:, b * C : (b + 1) * C].reshape(R, Q, F, C)
    for copy in later:
        copy.wait()


def rows_kernel(top, bot, acc, plain, csw, vec, w1v, sides, s2, raw, s1, add):
    up, down, _, _ = place()
    for msg, h0, valid in ((top, 0, up), (bot, 2, down)):
        for h in range(2):
            c0, c1 = cached_msg(msg[16 + h])
            put(s1, (h0 + h, pl.ds(0, Q)), msg[pl.ds(h * Q, Q)].reshape(Q * F, C).astype(F32), c0, c1, valid)
    add[0:2] = acc[0:2]
    add[2:4] = acc[4:6]
    for a, (low, targets) in enumerate(((0, (0, 1)), (1, (0, 3)), (2, (2, 3)))):
        part = jnp.dot(s1[low : low + 2].reshape(2 * Q * F, 3 * C), three(w1v, a), preferred_element_type=F32)
        for n, row in enumerate(targets):
            for b in range(3):
                block = part[n * Q * F : (n + 1) * Q * F, b * C : (b + 1) * C]
                add[row, 2 - b : 2 - b + Q] += block.reshape(Q, F, C)
    for n, cached, valid in (
        (0, [c[1:7] for c in cached_msg(top[18])], up),
        (1, cached_row(csw, 0, 1, 6), None),
        (2, cached_row(csw, 16, 1, 6), None),
        (3, cached_row(csw, 32, 1, 6), None),
        (4, cached_row(csw, 48, 1, 6), None),
        (5, [c[1:7] for c in cached_msg(bot[18])], down),
    ):
        total = acc[n, 2:8] if 2 <= n < 4 else add[n if n < 2 else n - 2, 2:8]
        hidden(s2, (n, pl.ds(0, 6)), total.reshape(6 * F, C), vec, cached, valid)
    for k in range(R * Q):
        raw[k] = rows_at(plain, k, F, R * Q).astype(BF16)
    for n, col in enumerate((0, 8)):
        sides[0:2, 2 * n : 2 * n + 2] = add[0:2, col : col + 2]
        sides[2:4, 2 * n : 2 * n + 2] = acc[2:4, col : col + 2]
        sides[4:6, 2 * n : 2 * n + 2] = add[2:4, col : col + 2]


def finish_kernel(
    left, right, top, bot, sides, rows2, raw, csw, chw, vec, w1v, w2v, wy, out,
    s1, acc1, s2, s3, acc2, acch, side_f, side_s,
):
    up, down, west, east = place()
    for n, msg in enumerate((left, right)):
        for c in range(2):
            side_f[n, pl.ds(c * 16, 16)] = msg[16 + c].astype(F32)
        side_s[n] = msg[18].astype(F32)
    for n, (msg, side) in enumerate(((left, west), (right, east))):
        for h in range(8):
            valid = side & up if h < 2 else side & down if h >= 6 else side
            put(
                s1, (h, pl.ds(2 * n, 2)), msg[pl.ds(h * 2, 2)].reshape(2 * F, C).astype(F32),
                [side_f[n, pl.ds(c * 16 + h * 2, 1), :] for c in range(2)],
                [side_f[n, pl.ds(c * 16 + h * 2 + 1, 1), :] for c in range(2)], valid,
            )

    acc1[...] = sides[...]
    for b, targets in enumerate(((0, 1), (0, 3), (2, 3))):
        taken = jnp.concatenate([s1[a : a + 6, b : b + 2].reshape(12 * F, 3 * C) for a in range(3)], axis=-1)
        weight = jnp.concatenate([w1v[a, 3 * b : 3 * b + 3].reshape(3 * C, C) for a in range(3)], axis=0)
        part = jnp.dot(taken, weight, preferred_element_type=F32).reshape(6, 2, F, C)
        for n, col in enumerate(targets):
            acc1[:, col] += part[:, n]
    s2[:, 2:8] = rows2[...]
    for h in range(6):
        inside = up if h == 0 else down if h == 5 else True
        if h == 0:
            c0, c1 = cached_msg(top[18])
        elif h == 5:
            c0, c1 = cached_msg(bot[18])
        else:
            c0, c1 = cached_row(csw, (h - 1) * 16, 0, Q)
        for n, side in enumerate((west, east)):
            first = [side_s[n, pl.ds(h * 2 + f, 1), :] for f in range(2)]
            keep = jnp.where(side, 1.0, 0.0).astype(F32)
            total = acc1[h, 2 * n : 2 * n + 2].reshape(2 * F, C)
            wide = (total + vec[pl.ds(2, 1), :]).astype(BF16).astype(F32)
            now = act(wide, vec[pl.ds(0, 1), :])
            own_w = 0 if n == 0 else Q - 1
            pair = [now[:F], now[F:]]
            pair[n] = pair[n] * keep
            now = jnp.concatenate(pair, axis=0)
            olds = []
            for f, c in enumerate((c0, c1)):
                two = [first[f] * keep, c[own_w]]
                olds.append(two if n == 0 else two[::-1])
            put(s2, (h, pl.ds(8 * n, 2)), now, olds[0], olds[1], None if inside is True else inside)

    def window(a, rows):
        return jnp.concatenate([s2[a : a + rows, b : b + Q].reshape(rows * Q * F, 3 * C) for b in range(3)], axis=-1)

    for a in range(3):
        part = jnp.dot(window(a, R), w2v[a, :, :, 0:256].reshape(9 * C, 256), preferred_element_type=F32)
        if a == 0:
            acc2[:, 0:256] = part
        else:
            acc2[:, 0:256] += part
    side = [w2v[a, :, :, 256:384].reshape(9 * C, 128) for a in range(3)]
    pair = jnp.dot(window(0, R + 1), jnp.concatenate(side[:2], axis=-1), preferred_element_type=F32)
    acc2[:, 256:384] = (
        pair[: R * Q * F, :128] + pair[Q * F :, 128:]
        + jnp.dot(window(2, R), side[2], preferred_element_type=F32)
    )

    for h in range(R):
        wide = acc2[pl.ds(h * Q * F, Q * F)] + vec[pl.ds(3, 1), :]
        wide = wide + raw[pl.ds(h * Q, Q)].reshape(Q * F, C).astype(F32)
        c0, c1 = cached_row(chw, h * 16, 0, Q)
        now = act(wide.astype(BF16).astype(F32), vec[pl.ds(1, 1), :])
        for n, part in enumerate(stack(now, c0, c1)):
            part = part.reshape(Q, F, C)
            for w in range(Q):
                s3[h % 2 * 2 + w % 2, h // 2 * 4 + w // 2, :, pl.ds(n * C, C)] = part[w]
    sums = {}
    for rh in range(2):
        for rw in range(2):
            part = lax.dot_general(
                s3[rh * 2 + rw].reshape(8 * F, 3 * C), wy[rh * 2 + rw], (((1,), (1,)), ((), ())),
                preferred_element_type=F32,
            )
            for k in range(8):
                for m in range(2):
                    for n in range(2):
                        pp, qq = (k // 4 + rh - 1 + m) % 3, (k % 4 + rw - 1 + n) % 5
                        slot = pp * 4 + qq if qq < 4 else 12 + pp
                        term = part[k * F : (k + 1) * F, (m * 2 + n) * 128 : (m * 2 + n + 1) * 128]
                        sums[slot] = sums[slot] + term if slot in sums else term
    for slot, total in sums.items():
        acch[pl.ds(slot * F, F)] = total
    acch[pl.ds(15 * F, F)] = jnp.zeros((F, 128), F32)

    for f in range(F):
        patches = acch[pl.ds(f, 16, stride=F), :].astype(BF16)
        for g in range(8):
            out[f, g] = patches


def last_kernel(slots, bias, out, sums):
    ha_count = 16
    g = lax.axis_index("wa")
    first = [jnp.clip(2 * g - 1 + k, 0, ha_count - 1) * 8 for k in range(4)]

    def held(k, j, low, count):
        return slots[first[k] + j, pl.ds(low, count)].astype(F32)

    lane = lax.broadcasted_iota(jnp.int32, (4, 128), 1)
    row = lax.broadcasted_iota(jnp.int32, (4, 128), 0)
    for k in range(2):
        for pr in range(2):
            other = k if pr == 0 else k + 2
            there = (2 * g + k > 0) if pr == 0 else (2 * g + k < ha_count - 1)
            upright = ((lane < 64) if pr == 0 else (lane >= 64)) & there

            def edge(j, pr=pr, k=k, other=other, upright=upright):
                mine = jnp.broadcast_to(held(k + 1, j, 12 + pr, 1), (4, 128))
                theirs = jnp.broadcast_to(held(other, j, 14, 1), (4, 128))
                return mine + jnp.where(upright, theirs, 0.0)

            for j in range(8):
                total = held(k + 1, j, pr * 4, 4)
                total = total + jnp.where(upright, held(other, j, 8, 4), 0.0)
                if j > 0:
                    total = total + jnp.where((row == 0) & (lane % 64 < 32), edge(j - 1), 0.0)
                if j < 7:
                    total = total + jnp.where((row == 3) & (lane % 64 >= 32), edge(j + 1), 0.0)
                sums[pl.ds((2 * k + pr) * 32 + j * 4, 4)] = total + bias[pl.ds(0, 1), :]
    out[...] = sums[...].astype(BF16)


def shape(*dims, dtype=BF16):
    return jax.ShapeDtypeStruct(dims, dtype)


def near(*dims, dtype=BF16):
    return pltpu.VMEM(dims, dtype)


def far(array):
    return pltpu.with_memory_space_constraint(array, pltpu.HBM)


def kernel(body, outs, ins, scratch, limit, name, flops=0, moved=0):
    return pl.pallas_call(
        body,
        out_shape=outs,
        in_specs=ins,
        out_specs=[VM] * len(outs),
        scratch_shapes=scratch,
        compiler_params=pltpu.CompilerParams(vmem_limit_bytes=limit * 2**20),
        cost_estimate=pl.CostEstimate(flops=flops, bytes_accessed=moved, transcendentals=0),
        name=name,
    )


def around(axis, step):
    count = lax.axis_size(axis)
    return [(n, (n + step) % count) for n in range(count)]


def local(
    features, cache_first, cache_second, cache_head, gain_first, gain_second, gain_head,
    conv_first, conv_second, conv_head, bias_first, bias_second, bias_head,
):
    own, plain, lo, hi, cfw, csw, chw, vec, bias = kernel(
        first_kernel,
        [near(32, F, C), near(3, F * R * Q, 128, dtype=F32), near(MSG, F, C), near(MSG, F, C)]
        + [near(3, 64, 128, dtype=F32)] * 3 + [near(8, C, dtype=F32), near(8, 128, dtype=F32)],
        [ANY] * 10,
        [
            pltpu.VMEM((F, R, Q, C), BF16),
            pltpu.VMEM((3, 2, R, Q, C), BF16),
        ]
        + [pltpu.VMEM((C,), F32)] * 5
        + [
            pltpu.VMEM((32,), F32),
            pltpu.VMEM((3, F * R * Q, 128), F32),
            pltpu.SemaphoreType.DMA((13,)),
        ],
        12, "act_first",
    )(*[far(v) for v in (features, cache_first, cache_second, cache_head, gain_first, gain_second, gain_head,
                         bias_first, bias_second, bias_head)])
    top = lax.ppermute(hi, "ha", around("ha", 1))
    bot = lax.ppermute(lo, "ha", around("ha", -1))
    cell_flops = 2 * F * 27 * C * C
    sums1, w1v, w2v, wy = kernel(
        inner_kernel,
        [near(R + 2, Q + 2, F, C, dtype=F32), near(3, 9, C, C), near(3, 9, C, C), near(4, 512, 3 * C)],
        [VM] * 2 + [ANY] * 3,
        [pltpu.VMEM((R * Q, F, 3 * C), BF16), pltpu.SemaphoreType.DMA((7,))],
        12, "inner", 32 * cell_flops, 17 * 2**20,
    )(own, cfw, far(conv_first), far(conv_second), far(jnp.swapaxes(conv_head, 3, 4)))
    to_left, to_right = kernel(
        pack_kernel,
        [near(MSG, F, C)] * 2,
        [VM] * 6,
        [pltpu.VMEM((3, 128, 128), F32)] * 2,
        4, "pack_columns",
    )(own, top, bot, cfw, csw, wy)
    left = lax.ppermute(to_right, "wa", around("wa", 1))
    right = lax.ppermute(to_left, "wa", around("wa", -1))
    sides, rows2, raw = kernel(
        rows_kernel,
        [near(R + 2, 4, F, C, dtype=F32), near(R + 2, 6, F, 3 * C), near(32, F, C)],
        [VM] * 7,
        [pltpu.VMEM((4, Q, F, 3 * C), BF16), pltpu.VMEM((4, Q + 2, F, C), F32)],
        10, "rows", 16 * cell_flops, 10 * 2**20,
    )(top, bot, sums1, plain, csw, vec, w1v)
    (slots,) = kernel(
        finish_kernel,
        [shape(F, 8, 16, 128)],
        [VM] * 13,
        [
            pltpu.VMEM((8, 4, F, 3 * C), BF16),
            pltpu.VMEM((R + 2, 4, F, C), F32),
            pltpu.VMEM((R + 2, Q + 2, F, 3 * C), BF16),
            pltpu.VMEM((4, 8, F, 3 * C), BF16),
            pltpu.VMEM((R * Q * F, C), F32),
            pltpu.VMEM((16 * F, 128), F32),
            pltpu.VMEM((2, 32, C), F32),
            pltpu.VMEM((2, 16, C), F32),
        ],
        20, "finish", 48 * cell_flops, 20 * 2**20,
    )(left, right, top, bot, sides, rows2, raw, csw, chw, vec, w1v, w2v, wy)
    arrived = lax.all_to_all(slots.reshape(F * 8, 16, 128), ("ha", "wa"), 0, 0, tiled=True)
    return pl.pallas_call(
        last_kernel,
        out_shape=shape(128, 128),
        in_specs=[VM] * 2,
        out_specs=VM,
        scratch_shapes=[pltpu.VMEM((128, 128), F32)],
        compiler_params=pltpu.CompilerParams(vmem_limit_bytes=4 * 2**20),
        name="sum_patches",
    )(arrived, bias)


def solution(mesh):
    tile = P(None, "ha", "wa", None)
    return jax.shard_map(
        local,
        mesh=mesh,
        in_specs=(tile,) * 4 + (P(),) * 9,
        out_specs=P(("ha", "wa"), None),
        check_vma=False,
    )
```

```python
import jax
import jax.numpy as jnp
from jax import lax
from jax.experimental import pallas as pl
from jax.experimental.pallas import tpu as pltpu
from jax.sharding import PartitionSpec as P

BF16 = jnp.bfloat16
F32 = jnp.float32
F, R, Q, C = 16, 4, 8, 384
MSG = 19
VM = pl.BlockSpec(memory_space=pltpu.VMEM)
ANY = pl.BlockSpec(memory_space=pl.ANY)


def act(wide, half_gain):
    scale = lax.rsqrt(jnp.mean(wide * wide, axis=-1, keepdims=True) + 1e-06)
    h = wide * scale * half_gain
    return h + h * jnp.tanh(h)


def line(ref):
    return ref[...].reshape(1, -1)


def put_rows(ref, start, value):
    for n in range(3):
        ref[n, pl.ds(start, value.shape[0])] = value[:, n * 128 : (n + 1) * 128]


def rows_at(ref, start, count, stride):
    where = pl.ds(start, count, stride=stride) if stride > 1 else pl.ds(start, count)
    return jnp.concatenate([ref[n, where, :] for n in range(3)], axis=-1)


def stack(now, c0, c1):
    row = lax.broadcasted_iota(jnp.int32, now.shape, 0) % F
    c0, c1 = (jnp.concatenate([jnp.broadcast_to(c, (F, C)) for c in cs], axis=0) for cs in (c0, c1))
    one = jnp.where(row == 0, c1, pltpu.roll(now, 1, 0))
    two = jnp.where(row == 0, c0, jnp.where(row == 1, c1, pltpu.roll(now, 2, 0)))
    return two.astype(BF16), one.astype(BF16), now.astype(BF16)


def put(dst, where, now, c0, c1, valid=None):
    if valid is not None:
        keep = jnp.where(valid, 1.0, 0.0).astype(F32)
        now, c0, c1 = now * keep, [c * keep for c in c0], [c * keep for c in c1]
    for n, part in enumerate(stack(now, c0, c1)):
        dst[where + (slice(None), pl.ds(n * C, C))] = part.reshape(-1, F, C)


def bring(pairs, sems):
    copies = [pltpu.make_async_copy(src, dst, sems.at[n]) for n, (src, dst) in enumerate(pairs)]
    for copy in copies:
        copy.start()
    return copies


def first_kernel(
    feat_h, cf_h, cs_h, ch_h, g1_h, g2_h, gh_h, b1_h, b2_h, b3_h, own, plain, lo, hi, cfw, csw, chw, vec, bias,
    feat, caches, g1, g2, gh, b1, b2, b3, wide, sems,
):
    parts = [pl.ds(4 * n, 4) for n in range(4)]
    copies = bring(
        [(g1_h, g1)] + [(feat_h.at[part], feat.at[part]) for part in parts]
        + [(cf_h, caches.at[0]), (cs_h, caches.at[1]), (ch_h, caches.at[2]),
           (g2_h, g2), (gh_h, gh), (b1_h, b1), (b2_h, b2), (b3_h, b3)], sems
    )
    copies[0].wait()
    half = 0.5 * line(g1)
    for n, part in enumerate(parts):
        copies[1 + n].wait()
        x = feat[part].astype(F32).reshape(4 * R * Q, C)
        put_rows(plain, n * 4 * R * Q, x)
        put_rows(wide, n * 4 * R * Q, act(x, half))
    for k in range(R * Q):
        cell = rows_at(wide, k, F, R * Q).astype(BF16)
        own[k] = cell
        if k < 16:
            lo[k] = cell
        else:
            hi[k - 16] = cell
    for copy in copies[5:]:
        copy.wait()
    for n, value in enumerate((0.5 * line(g2), 0.5 * line(gh), line(b1), line(b2))):
        vec[pl.ds(n, 1)] = value
    bias[pl.ds(0, 1)] = jnp.concatenate([line(b3)] * 4, axis=-1)
    for n, out in enumerate((cfw, csw, chw)):
        for h in range(R):
            for f in range(2):
                put_rows(out, h * 16 + f * 8, caches[n, f, h].astype(F32))
    for n in range(2):
        lo[16 + n] = rows_at(cfw, n * 16, 16, 1).astype(BF16)
        hi[16 + n] = rows_at(cfw, (2 + n) * 16, 16, 1).astype(BF16)
    lo[18] = rows_at(csw, 0, 16, 1).astype(BF16)
    hi[18] = rows_at(csw, 48, 16, 1).astype(BF16)


def pack_kernel(own, top, bot, cfw, csw, after, left, right, wide_f, wide_s):
    del after
    for n in range(2):
        put_rows(wide_f, n * 16, top[16 + n].astype(F32))
        put_rows(wide_f, (6 + n) * 16, bot[16 + n].astype(F32))
    put_rows(wide_s, 0, top[18].astype(F32))
    put_rows(wide_s, 5 * 16, bot[18].astype(F32))
    for n in range(3):
        wide_f[n, pl.ds(32, 64)] = cfw[n]
        wide_s[n, pl.ds(16, 64)] = csw[n]
        wide_s[n, pl.ds(96, 32)] = jnp.zeros((32, 128), F32)
    for out, base, edge in ((left, 0, 0), (right, 6, 7)):
        for c in range(2):
            for h in range(8):
                w = base + c
                if h < 2:
                    cell = top[h * Q + w]
                elif h < 6:
                    cell = own[(h - 2) * Q + w]
                else:
                    cell = bot[(h - 6) * Q + w]
                out[h * 2 + c] = cell
            out[16 + c] = rows_at(wide_f, base + c, 16, 8).astype(BF16)
        out[18] = rows_at(wide_s, edge, 16, 8).astype(BF16)


def cached_row(ref, base, w0, count):
    return [[rows_at(ref, base + 8 * f + w0 + w, 1, 1) for w in range(count)] for f in range(2)]


def cached_msg(block, count=Q):
    block = block.astype(F32)
    return [[block[8 * f + w : 8 * f + w + 1] for w in range(count)] for f in range(2)]


def three(weight, a):
    return jnp.concatenate([weight[a, 3 * b : 3 * b + 3].reshape(3 * C, C) for b in range(3)], axis=-1)


def hidden(dst, where, total, vec, cached, valid=None):
    wide = (total + vec[pl.ds(2, 1), :]).astype(BF16).astype(F32)
    put(dst, where, act(wide, vec[pl.ds(0, 1), :]), cached[0], cached[1], valid)


def place():
    ha, wa = lax.axis_index("ha"), lax.axis_index("wa")
    return ha > 0, ha < lax.axis_size("ha") - 1, wa > 0, wa < lax.axis_size("wa") - 1


def reach(rh, rw):
    return [
        (2 * (rh - 1 + m) + r, 2 * (rw - 1 + n) + s)
        for m in range(2) for n in range(2) for r in range(2) for s in range(2)
    ]


def inner_kernel(own, cfw, w1, w2, wh, acc, w1v, w2v, wy, s1, sems):
    def group(src, dst, a, sem):
        return [
            pltpu.make_async_copy(src.at[t, a, b], dst.at[a, b * 3 + t], sem) for b in range(3) for t in range(3)
        ]

    first = [group(w1, w1v, a, sems.at[a]) for a in range(3)]
    later = [copy for a in range(3) for copy in group(w2, w2v, a, sems.at[3 + a])]
    empty = []
    for rh in range(2):
        for rw in range(2):
            for k, (row, col) in enumerate(reach(rh, rw)):
                a, b = rh + 1 - row, rw + 1 - col
                where = pl.ds(k * 32, 32)
                if 0 <= a <= 2 and 0 <= b <= 2:
                    for t in range(3):
                        later.append(
                            pltpu.make_async_copy(
                                wh.at[t, a, b], wy.at[rh * 2 + rw, where, pl.ds(t * C, C)], sems.at[6]
                            )
                        )
                else:
                    empty.append((rh * 2 + rw, where))
    for copies in first[:2]:
        for copy in copies:
            copy.start()
    for where in empty:
        wy[where] = jnp.zeros((32, 3 * C), BF16)
    acc[...] = jnp.zeros_like(acc)

    def cells(h, _):
        c0, c1 = cached_row(cfw, h * 16, 0, Q)
        put(s1, (pl.ds(h * Q, Q),), own[pl.ds(h * Q, Q)].reshape(Q * F, C).astype(F32), c0, c1)
        return 0

    lax.fori_loop(0, R, cells, 0)
    for a in range(3):
        for copy in first[a]:
            copy.wait()
        for copy in (first[2], later, ())[a]:
            copy.start()
        part = jnp.dot(s1[...].reshape(R * Q * F, 3 * C), three(w1v, a), preferred_element_type=F32)
        for b in range(3):
            acc[2 - a : 2 - a + R, 2 - b : 2 - b + Q] += part[:, b * C : (b + 1) * C].reshape(R, Q, F, C)
    for copy in later:
        copy.wait()


def rows_kernel(top, bot, acc, plain, csw, vec, w1v, sides, s2, raw, s1, add):
    up, down, _, _ = place()
    for msg, h0, valid in ((top, 0, up), (bot, 2, down)):
        for h in range(2):
            c0, c1 = cached_msg(msg[16 + h])
            put(s1, (h0 + h, pl.ds(0, Q)), msg[pl.ds(h * Q, Q)].reshape(Q * F, C).astype(F32), c0, c1, valid)
    add[0:2] = acc[0:2]
    add[2:4] = acc[4:6]
    for a, (low, targets) in enumerate(((0, (0, 1)), (1, (0, 3)), (2, (2, 3)))):
        part = jnp.dot(s1[low : low + 2].reshape(2 * Q * F, 3 * C), three(w1v, a), preferred_element_type=F32)
        for n, row in enumerate(targets):
            for b in range(3):
                block = part[n * Q * F : (n + 1) * Q * F, b * C : (b + 1) * C]
                add[row, 2 - b : 2 - b + Q] += block.reshape(Q, F, C)
    for n, cached, valid in (
        (0, [c[1:7] for c in cached_msg(top[18])], up),
        (1, cached_row(csw, 0, 1, 6), None),
        (2, cached_row(csw, 16, 1, 6), None),
        (3, cached_row(csw, 32, 1, 6), None),
        (4, cached_row(csw, 48, 1, 6), None),
        (5, [c[1:7] for c in cached_msg(bot[18])], down),
    ):
        total = acc[n, 2:8] if 2 <= n < 4 else add[n if n < 2 else n - 2, 2:8]
        hidden(s2, (n, pl.ds(0, 6)), total.reshape(6 * F, C), vec, cached, valid)
    for k in range(R * Q):
        raw[k] = rows_at(plain, k, F, R * Q).astype(BF16)
    for n, col in enumerate((0, 8)):
        sides[0:2, 2 * n : 2 * n + 2] = add[0:2, col : col + 2]
        sides[2:4, 2 * n : 2 * n + 2] = acc[2:4, col : col + 2]
        sides[4:6, 2 * n : 2 * n + 2] = add[2:4, col : col + 2]


def finish_kernel(
    left, right, top, bot, sides, rows2, raw, csw, chw, vec, w1v, w2v, wy, out,
    s1, acc1, s2, s3, acc2, acch, side_f, side_s,
):
    up, down, west, east = place()
    for n, msg in enumerate((left, right)):
        for c in range(2):
            side_f[n, pl.ds(c * 16, 16)] = msg[16 + c].astype(F32)
        side_s[n] = msg[18].astype(F32)
    for n, (msg, side) in enumerate(((left, west), (right, east))):
        for h in range(8):
            valid = side & up if h < 2 else side & down if h >= 6 else side
            put(
                s1, (h, pl.ds(2 * n, 2)), msg[pl.ds(h * 2, 2)].reshape(2 * F, C).astype(F32),
                [side_f[n, pl.ds(c * 16 + h * 2, 1), :] for c in range(2)],
                [side_f[n, pl.ds(c * 16 + h * 2 + 1, 1), :] for c in range(2)], valid,
            )

    acc1[...] = sides[...]
    def columns(first):
        return jnp.concatenate([s1[a : a + 6, first : first + 2].reshape(12 * F, 3 * C) for a in range(3)], axis=-1)

    def column_tap(b, low, high):
        return jnp.concatenate([w1v[a, 3 * b : 3 * b + 3, :, low:high].reshape(3 * C, high - low) for a in range(3)], axis=0)

    for b, targets in enumerate(((0, 1), (0, 3), (2, 3))):
        part = jnp.dot(columns(b), column_tap(b, 0, 256), preferred_element_type=F32).reshape(6, 2, F, 256)
        for n, col in enumerate(targets):
            acc1[:, col, :, 0:256] += part[:, n]
    for b, moves in ((0, ((0, 0, 0), (1, 0, 1), (1, 1, 0))), (1, ((0, 0, 3), (0, 1, 2), (1, 1, 3)))):
        weight = jnp.concatenate([column_tap(b, 256, 384), column_tap(b + 1, 256, 384)], axis=-1)
        part = jnp.dot(columns(2 * b), weight, preferred_element_type=F32).reshape(6, 2, F, 256)
        for n, tap, col in moves:
            acc1[:, col, :, 256:384] += part[:, n, :, tap * 128 : (tap + 1) * 128]
    s2[:, 2:8] = rows2[...]
    for h in range(6):
        inside = up if h == 0 else down if h == 5 else True
        if h == 0:
            c0, c1 = cached_msg(top[18])
        elif h == 5:
            c0, c1 = cached_msg(bot[18])
        else:
            c0, c1 = cached_row(csw, (h - 1) * 16, 0, Q)
        for n, side in enumerate((west, east)):
            first = [side_s[n, pl.ds(h * 2 + f, 1), :] for f in range(2)]
            keep = jnp.where(side, 1.0, 0.0).astype(F32)
            total = acc1[h, 2 * n : 2 * n + 2].reshape(2 * F, C)
            wide = (total + vec[pl.ds(2, 1), :]).astype(BF16).astype(F32)
            now = act(wide, vec[pl.ds(0, 1), :])
            own_w = 0 if n == 0 else Q - 1
            pair = [now[:F], now[F:]]
            pair[n] = pair[n] * keep
            now = jnp.concatenate(pair, axis=0)
            olds = []
            for f, c in enumerate((c0, c1)):
                two = [first[f] * keep, c[own_w]]
                olds.append(two if n == 0 else two[::-1])
            put(s2, (h, pl.ds(8 * n, 2)), now, olds[0], olds[1], None if inside is True else inside)

    def window(a, rows):
        return jnp.concatenate([s2[a : a + rows, b : b + Q].reshape(rows * Q * F, 3 * C) for b in range(3)], axis=-1)

    for a in range(3):
        part = jnp.dot(window(a, R), w2v[a, :, :, 0:256].reshape(9 * C, 256), preferred_element_type=F32)
        if a == 0:
            acc2[:, 0:256] = part
        else:
            acc2[:, 0:256] += part
    side = [w2v[a, :, :, 256:384].reshape(9 * C, 128) for a in range(2)]
    pair = jnp.dot(window(0, R + 1), jnp.concatenate(side, axis=-1), preferred_element_type=F32)
    def one(b):
        return w2v[2, 3 * b : 3 * b + 3, :, 256:384].reshape(3 * C, 128)

    wider = s2[2 : 2 + R, 0 : Q + 1].reshape(R * (Q + 1) * F, 3 * C)
    two = jnp.dot(wider, jnp.concatenate([one(0), one(1)], axis=-1), preferred_element_type=F32)
    two = two.reshape(R, Q + 1, F, 256)
    last_tap = jnp.dot(s2[2 : 2 + R, 2 : 2 + Q].reshape(R * Q * F, 3 * C), one(2), preferred_element_type=F32)
    acc2[:, 256:384] = (
        pair[: R * Q * F, :128] + pair[Q * F :, 128:] + last_tap
        + (two[:, :Q, :, :128] + two[:, 1:, :, 128:]).reshape(R * Q * F, 128)
    )

    for h in range(R):
        wide = acc2[pl.ds(h * Q * F, Q * F)] + vec[pl.ds(3, 1), :]
        wide = wide + raw[pl.ds(h * Q, Q)].reshape(Q * F, C).astype(F32)
        c0, c1 = cached_row(chw, h * 16, 0, Q)
        now = act(wide.astype(BF16).astype(F32), vec[pl.ds(1, 1), :])
        for n, part in enumerate(stack(now, c0, c1)):
            part = part.reshape(Q, F, C)
            for w in range(Q):
                s3[h % 2 * 2 + w % 2, h // 2 * 4 + w // 2, :, pl.ds(n * C, C)] = part[w]
    sums = {}
    for rh in range(2):
        for rw in range(2):
            part = lax.dot_general(
                s3[rh * 2 + rw].reshape(8 * F, 3 * C), wy[rh * 2 + rw], (((1,), (1,)), ((), ())),
                preferred_element_type=F32,
            )
            for k in range(8):
                for m in range(2):
                    for n in range(2):
                        pp, qq = (k // 4 + rh - 1 + m) % 3, (k % 4 + rw - 1 + n) % 5
                        slot = pp * 4 + qq if qq < 4 else 12 + pp
                        term = part[k * F : (k + 1) * F, (m * 2 + n) * 128 : (m * 2 + n + 1) * 128]
                        sums[slot] = sums[slot] + term if slot in sums else term
    for slot, total in sums.items():
        acch[pl.ds(slot * F, F)] = total
    acch[pl.ds(15 * F, F)] = jnp.zeros((F, 128), F32)

    for f in range(F):
        patches = acch[pl.ds(f, 16, stride=F), :].astype(BF16)
        for g in range(8):
            out[f, g] = patches[8 * (g % 2) : 8 * (g % 2) + 8]


def last_kernel(mine, theirs, bias, out, sums):
    ha_count = 16
    g = lax.axis_index("wa")
    even = g % 2 == 0
    first = [jnp.clip(2 * g - 1 + k, 0, ha_count - 1) * 8 for k in range(4)]

    def held(k, j, low, count):
        where = (first[k] + j, pl.ds(low % 8, count))
        here, there = mine[where].astype(F32), theirs[where].astype(F32)
        return jnp.where(even == (low < 8), here, there)

    lane = lax.broadcasted_iota(jnp.int32, (4, 128), 1)
    row = lax.broadcasted_iota(jnp.int32, (4, 128), 0)
    for k in range(2):
        for pr in range(2):
            other = k if pr == 0 else k + 2
            there = (2 * g + k > 0) if pr == 0 else (2 * g + k < ha_count - 1)
            upright = ((lane < 64) if pr == 0 else (lane >= 64)) & there

            def edge(j, pr=pr, k=k, other=other, upright=upright):
                mine = jnp.broadcast_to(held(k + 1, j, 12 + pr, 1), (4, 128))
                theirs = jnp.broadcast_to(held(other, j, 14, 1), (4, 128))
                return mine + jnp.where(upright, theirs, 0.0)

            for j in range(8):
                total = held(k + 1, j, pr * 4, 4)
                total = total + jnp.where(upright, held(other, j, 8, 4), 0.0)
                if j > 0:
                    total = total + jnp.where((row == 0) & (lane % 64 < 32), edge(j - 1), 0.0)
                if j < 7:
                    total = total + jnp.where((row == 3) & (lane % 64 >= 32), edge(j + 1), 0.0)
                sums[pl.ds((2 * k + pr) * 32 + j * 4, 4)] = total + bias[pl.ds(0, 1), :]
    out[...] = sums[...].astype(BF16)


def shape(*dims, dtype=BF16):
    return jax.ShapeDtypeStruct(dims, dtype)


def near(*dims, dtype=BF16):
    return pltpu.VMEM(dims, dtype)


def far(array):
    return pltpu.with_memory_space_constraint(array, pltpu.HBM)


def kernel(body, outs, ins, scratch, limit, name, flops=0, moved=0):
    return pl.pallas_call(
        body,
        out_shape=outs,
        in_specs=ins,
        out_specs=[VM] * len(outs),
        scratch_shapes=scratch,
        compiler_params=pltpu.CompilerParams(vmem_limit_bytes=limit * 2**20),
        cost_estimate=pl.CostEstimate(flops=flops, bytes_accessed=moved, transcendentals=0),
        name=name,
    )


def around(axis, step):
    count = lax.axis_size(axis)
    return [(n, (n + step) % count) for n in range(count)]


def local(
    features, cache_first, cache_second, cache_head, gain_first, gain_second, gain_head,
    conv_first, conv_second, conv_head, bias_first, bias_second, bias_head,
):
    own, plain, lo, hi, cfw, csw, chw, vec, bias = kernel(
        first_kernel,
        [near(32, F, C), near(3, F * R * Q, 128, dtype=F32), near(MSG, F, C), near(MSG, F, C)]
        + [near(3, 64, 128, dtype=F32)] * 3 + [near(8, C, dtype=F32), near(8, 128, dtype=F32)],
        [ANY] * 10,
        [
            pltpu.VMEM((F, R, Q, C), BF16),
            pltpu.VMEM((3, 2, R, Q, C), BF16),
        ]
        + [pltpu.VMEM((C,), F32)] * 5
        + [
            pltpu.VMEM((32,), F32),
            pltpu.VMEM((3, F * R * Q, 128), F32),
            pltpu.SemaphoreType.DMA((13,)),
        ],
        12, "act_first",
    )(*[far(v) for v in (features, cache_first, cache_second, cache_head, gain_first, gain_second, gain_head,
                         bias_first, bias_second, bias_head)])
    top = lax.ppermute(hi, "ha", around("ha", 1))
    bot = lax.ppermute(lo, "ha", around("ha", -1))
    cell_flops = 2 * F * 27 * C * C
    sums1, w1v, w2v, wy = kernel(
        inner_kernel,
        [near(R + 2, Q + 2, F, C, dtype=F32), near(3, 9, C, C), near(3, 9, C, C), near(4, 512, 3 * C)],
        [VM] * 2 + [ANY] * 3,
        [pltpu.VMEM((R * Q, F, 3 * C), BF16), pltpu.SemaphoreType.DMA((7,))],
        12, "inner", 32 * cell_flops, 17 * 2**20,
    )(own, cfw, far(conv_first), far(conv_second), far(jnp.swapaxes(conv_head, 3, 4)))
    to_left, to_right = kernel(
        pack_kernel,
        [near(MSG, F, C)] * 2,
        [VM] * 6,
        [pltpu.VMEM((3, 128, 128), F32)] * 2,
        4, "pack_columns",
    )(own, top, bot, cfw, csw, wy)
    left = lax.ppermute(to_right, "wa", around("wa", 1))
    right = lax.ppermute(to_left, "wa", around("wa", -1))
    sides, rows2, raw = kernel(
        rows_kernel,
        [near(R + 2, 4, F, C, dtype=F32), near(R + 2, 6, F, 3 * C), near(32, F, C)],
        [VM] * 7,
        [pltpu.VMEM((4, Q, F, 3 * C), BF16), pltpu.VMEM((4, Q + 2, F, C), F32)],
        10, "rows", 16 * cell_flops, 10 * 2**20,
    )(top, bot, sums1, plain, csw, vec, w1v)
    (slots,) = kernel(
        finish_kernel,
        [shape(F, 8, 8, 128)],
        [VM] * 13,
        [
            pltpu.VMEM((8, 4, F, 3 * C), BF16),
            pltpu.VMEM((R + 2, 4, F, C), F32),
            pltpu.VMEM((R + 2, Q + 2, F, 3 * C), BF16),
            pltpu.VMEM((4, 8, F, 3 * C), BF16),
            pltpu.VMEM((R * Q * F, C), F32),
            pltpu.VMEM((16 * F, 128), F32),
            pltpu.VMEM((2, 32, C), F32),
            pltpu.VMEM((2, 16, C), F32),
        ],
        20, "finish", 48 * cell_flops, 20 * 2**20,
    )(left, right, top, bot, sides, rows2, raw, csw, chw, vec, w1v, w2v, wy)
    arrived = lax.all_to_all(slots.reshape(F * 8, 8, 128), ("ha", "wa"), 0, 0, tiled=True)
    pairs = [(n, n ^ 1) for n in range(lax.axis_size("wa"))]
    swapped = lax.ppermute(arrived, "wa", pairs)
    return pl.pallas_call(
        last_kernel,
        out_shape=shape(128, 128),
        in_specs=[VM] * 3,
        out_specs=VM,
        scratch_shapes=[pltpu.VMEM((128, 128), F32)],
        compiler_params=pltpu.CompilerParams(vmem_limit_bytes=4 * 2**20),
        name="sum_patches",
    )(arrived, swapped, bias)


def solution(mesh):
    tile = P(None, "ha", "wa", None)
    return jax.shard_map(
        local,
        mesh=mesh,
        in_specs=(tile,) * 4 + (P(),) * 9,
        out_specs=P(("ha", "wa"), None),
        check_vma=False,
    )
```

```python
import jax
import jax.numpy as jnp
from jax import lax
from jax.experimental import pallas as pl
from jax.experimental.pallas import tpu as pltpu
from jax.sharding import PartitionSpec as P

BF16 = jnp.bfloat16
F32 = jnp.float32
F, R, Q, C = 16, 4, 8, 384
MSG = 19
VM = pl.BlockSpec(memory_space=pltpu.VMEM)
ANY = pl.BlockSpec(memory_space=pl.ANY)


def act(wide, half_gain):
    scale = lax.rsqrt(jnp.mean(wide * wide, axis=-1, keepdims=True) + 1e-06)
    h = wide * scale * half_gain
    return h + h * jnp.tanh(h)


def line(ref):
    return ref[...].reshape(1, -1)


def put_rows(ref, start, value):
    for n in range(3):
        ref[n, pl.ds(start, value.shape[0])] = value[:, n * 128 : (n + 1) * 128]


def rows_at(ref, start, count, stride):
    where = pl.ds(start, count, stride=stride) if stride > 1 else pl.ds(start, count)
    return jnp.concatenate([ref[n, where, :] for n in range(3)], axis=-1)


def stack(now, c0, c1):
    row = lax.broadcasted_iota(jnp.int32, now.shape, 0) % F
    c0, c1 = (jnp.concatenate([jnp.broadcast_to(c, (F, C)) for c in cs], axis=0) for cs in (c0, c1))
    one = jnp.where(row == 0, c1, pltpu.roll(now, 1, 0))
    two = jnp.where(row == 0, c0, jnp.where(row == 1, c1, pltpu.roll(now, 2, 0)))
    return two.astype(BF16), one.astype(BF16), now.astype(BF16)


def put(dst, where, now, c0, c1, valid=None):
    if valid is not None:
        keep = jnp.where(valid, 1.0, 0.0).astype(F32)
        now, c0, c1 = now * keep, [c * keep for c in c0], [c * keep for c in c1]
    for n, part in enumerate(stack(now, c0, c1)):
        dst[where + (slice(None), pl.ds(n * C, C))] = part.reshape(-1, F, C)


def bring(pairs, sems):
    copies = [pltpu.make_async_copy(src, dst, sems.at[n]) for n, (src, dst) in enumerate(pairs)]
    for copy in copies:
        copy.start()
    return copies


def first_kernel(
    feat_h, cf_h, cs_h, ch_h, g1_h, g2_h, gh_h, b1_h, b2_h, b3_h, own, plain, pair_a, pair_b, cfw, csw, chw, vec, bias,
    feat, caches, g1, g2, gh, b1, b2, b3, wide, sems,
):
    parts = [pl.ds(4 * n, 4) for n in range(4)]
    copies = bring(
        [(g1_h, g1)] + [(feat_h.at[part], feat.at[part]) for part in parts]
        + [(cf_h, caches.at[0]), (cs_h, caches.at[1]), (ch_h, caches.at[2]),
           (g2_h, g2), (gh_h, gh), (b1_h, b1), (b2_h, b2), (b3_h, b3)], sems
    )
    even = lax.axis_index("ha") % 2 == 0

    def send(k, low, high):
        pair_a[k] = jnp.where(even, high, low).astype(BF16)
        pair_b[k] = jnp.where(even, low, high).astype(BF16)

    for n in (0, 5, 6, 7, 8, 9, 10, 11, 12):
        copies[n].wait()
    for n, out in enumerate((cfw, csw, chw)):
        for h in range(R):
            for f in range(2):
                put_rows(out, h * 16 + f * 8, caches[n, f, h].astype(F32))
    for n in range(2):
        send(16 + n, rows_at(cfw, n * 16, 16, 1), rows_at(cfw, (2 + n) * 16, 16, 1))
    send(18, rows_at(csw, 0, 16, 1), rows_at(csw, 48, 16, 1))
    for n, value in enumerate((0.5 * line(g2), 0.5 * line(gh), line(b1), line(b2))):
        vec[pl.ds(n, 1)] = value
    bias[pl.ds(0, 1)] = jnp.concatenate([line(b3)] * 4, axis=-1)
    half = 0.5 * line(g1)
    for n, part in enumerate(parts):
        copies[1 + n].wait()
        x = feat[part].astype(F32).reshape(4 * R * Q, C)
        put_rows(plain, n * 4 * R * Q, x)
        put_rows(wide, n * 4 * R * Q, act(x, half))
    for k in range(16):
        low, high = rows_at(wide, k, F, R * Q), rows_at(wide, k + 16, F, R * Q)
        own[k] = low.astype(BF16)
        own[k + 16] = high.astype(BF16)
        send(k, low, high)


def pack_kernel(own, got_a, got_b, cfw, csw, after, top, bot, pair_a, pair_b, wide_f, wide_s):
    del after
    even_h, even_w = lax.axis_index("ha") % 2 == 0, lax.axis_index("wa") % 2 == 0

    def choose(first, one, other):
        return jnp.where(first, one.astype(F32), other.astype(F32))

    for k in range(MSG):
        above, below = choose(even_h, got_b[k], got_a[k]), choose(even_h, got_a[k], got_b[k])
        top[k], bot[k] = above.astype(BF16), below.astype(BF16)
        if k in (16, 17):
            put_rows(wide_f, (k - 16) * 16, above)
            put_rows(wide_f, (k - 10) * 16, below)
        elif k == 18:
            put_rows(wide_s, 0, above)
            put_rows(wide_s, 5 * 16, below)
    for n in range(3):
        wide_f[n, pl.ds(32, 64)] = cfw[n]
        wide_s[n, pl.ds(16, 64)] = csw[n]
        wide_s[n, pl.ds(96, 32)] = jnp.zeros((32, 128), F32)

    def send(k, left, right):
        pair_a[k] = choose(even_w, right, left).astype(BF16)
        pair_b[k] = choose(even_w, left, right).astype(BF16)

    for c in range(2):
        for h in range(8):
            cells = []
            for w in (c, 6 + c):
                if h < 2:
                    cells.append(top[h * Q + w])
                elif h < 6:
                    cells.append(own[(h - 2) * Q + w])
                else:
                    cells.append(bot[(h - 6) * Q + w])
            send(h * 2 + c, *cells)
        send(16 + c, rows_at(wide_f, c, 16, 8), rows_at(wide_f, 6 + c, 16, 8))
    send(18, rows_at(wide_s, 0, 16, 8), rows_at(wide_s, 7, 16, 8))


def cached_row(ref, base, w0, count):
    return [[rows_at(ref, base + 8 * f + w0 + w, 1, 1) for w in range(count)] for f in range(2)]


def cached_msg(block, count=Q):
    block = block.astype(F32)
    return [[block[8 * f + w : 8 * f + w + 1] for w in range(count)] for f in range(2)]


def three(weight, a):
    return jnp.concatenate([weight[a, 3 * b : 3 * b + 3].reshape(3 * C, C) for b in range(3)], axis=-1)


def hidden(dst, where, total, vec, cached, valid=None):
    wide = (total + vec[pl.ds(2, 1), :]).astype(BF16).astype(F32)
    put(dst, where, act(wide, vec[pl.ds(0, 1), :]), cached[0], cached[1], valid)


def place():
    ha, wa = lax.axis_index("ha"), lax.axis_index("wa")
    return ha > 0, ha < lax.axis_size("ha") - 1, wa > 0, wa < lax.axis_size("wa") - 1


def reach(rh, rw):
    return [
        (2 * (rh - 1 + m) + r, 2 * (rw - 1 + n) + s)
        for m in range(2) for n in range(2) for r in range(2) for s in range(2)
    ]


def inner_kernel(own, cfw, w1, w2, wh, acc, w1v, w2v, wy, s1, sems):
    def group(src, dst, a, sem):
        return [
            pltpu.make_async_copy(src.at[t, a, b], dst.at[a, b * 3 + t], sem) for b in range(3) for t in range(3)
        ]

    first = [group(w1, w1v, a, sems.at[a]) for a in range(3)]
    later = [copy for a in range(3) for copy in group(w2, w2v, a, sems.at[3 + a])]
    empty = []
    for rh in range(2):
        for rw in range(2):
            for k, (row, col) in enumerate(reach(rh, rw)):
                a, b = rh + 1 - row, rw + 1 - col
                where = pl.ds(k * 32, 32)
                if 0 <= a <= 2 and 0 <= b <= 2:
                    for t in range(3):
                        later.append(
                            pltpu.make_async_copy(
                                wh.at[t, a, b], wy.at[rh * 2 + rw, where, pl.ds(t * C, C)], sems.at[6]
                            )
                        )
                else:
                    empty.append((rh * 2 + rw, where))
    for copies in first[:2]:
        for copy in copies:
            copy.start()
    for where in empty:
        wy[where] = jnp.zeros((32, 3 * C), BF16)
    for col in (0, Q + 1):
        acc[:, col] = jnp.zeros((R + 2, F, C), F32)

    def cells(h, _):
        c0, c1 = cached_row(cfw, h * 16, 0, Q)
        put(s1, (pl.ds(h * Q, Q),), own[pl.ds(h * Q, Q)].reshape(Q * F, C).astype(F32), c0, c1)
        return 0

    lax.fori_loop(0, R, cells, 0)
    for a in range(3):
        for copy in first[a]:
            copy.wait()
        for copy in (first[2], later, ())[a]:
            copy.start()
        part = jnp.dot(s1[...].reshape(R * Q * F, 3 * C), three(w1v, a), preferred_element_type=F32)
        part = part.reshape(R, Q, F, 3 * C)
        fresh = R if a == 0 else 1
        acc[2 - a : 2 - a + fresh, 1 : 1 + Q] = part[:fresh, :, :, C : 2 * C]
        if a > 0:
            acc[3 - a : 2 - a + R, 1 : 1 + Q] += part[1:, :, :, C : 2 * C]
        for b in (0, 2):
            acc[2 - a : 2 - a + R, 2 - b : 2 - b + Q] += part[:, :, :, b * C : (b + 1) * C]
    for copy in later:
        copy.wait()


def rows_kernel(top, bot, acc, plain, csw, vec, w1v, sides, s2, raw, s1, add):
    up, down, _, _ = place()
    for msg, h0, valid in ((top, 0, up), (bot, 2, down)):
        for h in range(2):
            c0, c1 = cached_msg(msg[16 + h])
            put(s1, (h0 + h, pl.ds(0, Q)), msg[pl.ds(h * Q, Q)].reshape(Q * F, C).astype(F32), c0, c1, valid)
    add[0:2] = acc[0:2]
    add[2:4] = acc[4:6]
    for a, (low, targets) in enumerate(((0, (0, 1)), (1, (0, 3)), (2, (2, 3)))):
        part = jnp.dot(s1[low : low + 2].reshape(2 * Q * F, 3 * C), three(w1v, a), preferred_element_type=F32)
        for n, row in enumerate(targets):
            for b in range(3):
                block = part[n * Q * F : (n + 1) * Q * F, b * C : (b + 1) * C]
                add[row, 2 - b : 2 - b + Q] += block.reshape(Q, F, C)
    for n, cached, valid in (
        (0, [c[1:7] for c in cached_msg(top[18])], up),
        (1, cached_row(csw, 0, 1, 6), None),
        (2, cached_row(csw, 16, 1, 6), None),
        (3, cached_row(csw, 32, 1, 6), None),
        (4, cached_row(csw, 48, 1, 6), None),
        (5, [c[1:7] for c in cached_msg(bot[18])], down),
    ):
        total = acc[n, 2:8] if 2 <= n < 4 else add[n if n < 2 else n - 2, 2:8]
        hidden(s2, (n, pl.ds(0, 6)), total.reshape(6 * F, C), vec, cached, valid)
    for k in range(R * Q):
        raw[k] = rows_at(plain, k, F, R * Q).astype(BF16)
    for n, col in enumerate((0, 8)):
        sides[0:2, 2 * n : 2 * n + 2] = add[0:2, col : col + 2]
        sides[2:4, 2 * n : 2 * n + 2] = acc[2:4, col : col + 2]
        sides[4:6, 2 * n : 2 * n + 2] = add[2:4, col : col + 2]


def finish_kernel(
    got_a, got_b, top, bot, sides, rows2, raw, csw, chw, vec, w1v, w2v, wy, out,
    s1, acc1, s2, s3, acc2, acch, side_f, side_s,
):
    up, down, west, east = place()
    even = lax.axis_index("wa") % 2 == 0

    def arrived(n, k):
        one, other = got_a[k].astype(F32), got_b[k].astype(F32)
        return jnp.where(even, other, one) if n == 0 else jnp.where(even, one, other)

    for n in range(2):
        for c in range(2):
            side_f[n, pl.ds(c * 16, 16)] = arrived(n, 16 + c)
        side_s[n] = arrived(n, 18)
    for n, side in enumerate((west, east)):
        for h in range(8):
            valid = side & up if h < 2 else side & down if h >= 6 else side
            put(
                s1, (h, pl.ds(2 * n, 2)), arrived(n, pl.ds(h * 2, 2)).reshape(2 * F, C),
                [side_f[n, pl.ds(c * 16 + h * 2, 1), :] for c in range(2)],
                [side_f[n, pl.ds(c * 16 + h * 2 + 1, 1), :] for c in range(2)], valid,
            )

    acc1[...] = sides[...]
    def columns(first):
        return jnp.concatenate([s1[a : a + 6, first : first + 2].reshape(12 * F, 3 * C) for a in range(3)], axis=-1)

    def column_tap(b, low, high):
        return jnp.concatenate([w1v[a, 3 * b : 3 * b + 3, :, low:high].reshape(3 * C, high - low) for a in range(3)], axis=0)

    for b, targets in enumerate(((0, 1), (0, 3), (2, 3))):
        part = jnp.dot(columns(b), column_tap(b, 0, 256), preferred_element_type=F32).reshape(6, 2, F, 256)
        for n, col in enumerate(targets):
            acc1[:, col, :, 0:256] += part[:, n]
    for b, moves in ((0, ((0, 0, 0), (1, 0, 1), (1, 1, 0))), (1, ((0, 0, 3), (0, 1, 2), (1, 1, 3)))):
        weight = jnp.concatenate([column_tap(b, 256, 384), column_tap(b + 1, 256, 384)], axis=-1)
        part = jnp.dot(columns(2 * b), weight, preferred_element_type=F32).reshape(6, 2, F, 256)
        for n, tap, col in moves:
            acc1[:, col, :, 256:384] += part[:, n, :, tap * 128 : (tap + 1) * 128]
    s2[:, 2:8] = rows2[...]
    for h in range(6):
        inside = up if h == 0 else down if h == 5 else True
        if h == 0:
            c0, c1 = cached_msg(top[18])
        elif h == 5:
            c0, c1 = cached_msg(bot[18])
        else:
            c0, c1 = cached_row(csw, (h - 1) * 16, 0, Q)
        for n, side in enumerate((west, east)):
            first = [side_s[n, pl.ds(h * 2 + f, 1), :] for f in range(2)]
            keep = jnp.where(side, 1.0, 0.0).astype(F32)
            total = acc1[h, 2 * n : 2 * n + 2].reshape(2 * F, C)
            wide = (total + vec[pl.ds(2, 1), :]).astype(BF16).astype(F32)
            now = act(wide, vec[pl.ds(0, 1), :])
            own_w = 0 if n == 0 else Q - 1
            pair = [now[:F], now[F:]]
            pair[n] = pair[n] * keep
            now = jnp.concatenate(pair, axis=0)
            olds = []
            for f, c in enumerate((c0, c1)):
                two = [first[f] * keep, c[own_w]]
                olds.append(two if n == 0 else two[::-1])
            put(s2, (h, pl.ds(8 * n, 2)), now, olds[0], olds[1], None if inside is True else inside)

    def window(a, rows):
        return jnp.concatenate([s2[a : a + rows, b : b + Q].reshape(rows * Q * F, 3 * C) for b in range(3)], axis=-1)

    for a in range(3):
        part = jnp.dot(window(a, R), w2v[a, :, :, 0:256].reshape(9 * C, 256), preferred_element_type=F32)
        if a == 0:
            acc2[:, 0:256] = part
        else:
            acc2[:, 0:256] += part
    side = [w2v[a, :, :, 256:384].reshape(9 * C, 128) for a in range(2)]
    pair = jnp.dot(window(0, R + 1), jnp.concatenate(side, axis=-1), preferred_element_type=F32)
    def one(b):
        return w2v[2, 3 * b : 3 * b + 3, :, 256:384].reshape(3 * C, 128)

    wider = s2[2 : 2 + R, 0 : Q + 1].reshape(R * (Q + 1) * F, 3 * C)
    two = jnp.dot(wider, jnp.concatenate([one(0), one(1)], axis=-1), preferred_element_type=F32)
    two = two.reshape(R, Q + 1, F, 256)
    last_tap = jnp.dot(s2[2 : 2 + R, 2 : 2 + Q].reshape(R * Q * F, 3 * C), one(2), preferred_element_type=F32)
    acc2[:, 256:384] = (
        pair[: R * Q * F, :128] + pair[Q * F :, 128:] + last_tap
        + (two[:, :Q, :, :128] + two[:, 1:, :, 128:]).reshape(R * Q * F, 128)
    )

    for h in range(R):
        wide = acc2[pl.ds(h * Q * F, Q * F)] + vec[pl.ds(3, 1), :]
        wide = wide + raw[pl.ds(h * Q, Q)].reshape(Q * F, C).astype(F32)
        c0, c1 = cached_row(chw, h * 16, 0, Q)
        now = act(wide.astype(BF16).astype(F32), vec[pl.ds(1, 1), :])
        for n, part in enumerate(stack(now, c0, c1)):
            part = part.reshape(Q, F, C)
            for w in range(Q):
                s3[h % 2 * 2 + w % 2, h // 2 * 4 + w // 2, :, pl.ds(n * C, C)] = part[w]
    sums = {}
    for rh in range(2):
        for rw in range(2):
            part = lax.dot_general(
                s3[rh * 2 + rw].reshape(8 * F, 3 * C), wy[rh * 2 + rw], (((1,), (1,)), ((), ())),
                preferred_element_type=F32,
            )
            for k in range(8):
                for m in range(2):
                    for n in range(2):
                        pp, qq = (k // 4 + rh - 1 + m) % 3, (k % 4 + rw - 1 + n) % 5
                        slot = pp * 4 + qq if qq < 4 else 12 + pp
                        term = part[k * F : (k + 1) * F, (m * 2 + n) * 128 : (m * 2 + n + 1) * 128]
                        sums[slot] = sums[slot] + term if slot in sums else term
    for slot, total in sums.items():
        acch[pl.ds(slot * F, F)] = total
    acch[pl.ds(15 * F, F)] = jnp.zeros((F, 128), F32)

    for f in range(F):
        patches = acch[pl.ds(f, 16, stride=F), :].astype(BF16)
        for g in range(8):
            out[f, g] = patches[8 * (g % 2) : 8 * (g % 2) + 8]


def last_kernel(mine, theirs, bias, out, sums):
    ha_count = 16
    g = lax.axis_index("wa")
    even = g % 2 == 0
    first = [jnp.clip(2 * g - 1 + k, 0, ha_count - 1) * 8 for k in range(4)]

    def held(k, j, low, count):
        where = (first[k] + j, pl.ds(low % 8, count))
        here, there = mine[where].astype(F32), theirs[where].astype(F32)
        return jnp.where(even == (low < 8), here, there)

    lane = lax.broadcasted_iota(jnp.int32, (4, 128), 1)
    row = lax.broadcasted_iota(jnp.int32, (4, 128), 0)
    for k in range(2):
        for pr in range(2):
            other = k if pr == 0 else k + 2
            there = (2 * g + k > 0) if pr == 0 else (2 * g + k < ha_count - 1)
            upright = ((lane < 64) if pr == 0 else (lane >= 64)) & there

            def edge(j, pr=pr, k=k, other=other, upright=upright):
                mine = jnp.broadcast_to(held(k + 1, j, 12 + pr, 1), (4, 128))
                theirs = jnp.broadcast_to(held(other, j, 14, 1), (4, 128))
                return mine + jnp.where(upright, theirs, 0.0)

            for j in range(8):
                total = held(k + 1, j, pr * 4, 4)
                total = total + jnp.where(upright, held(other, j, 8, 4), 0.0)
                if j > 0:
                    total = total + jnp.where((row == 0) & (lane % 64 < 32), edge(j - 1), 0.0)
                if j < 7:
                    total = total + jnp.where((row == 3) & (lane % 64 >= 32), edge(j + 1), 0.0)
                sums[pl.ds((2 * k + pr) * 32 + j * 4, 4)] = total + bias[pl.ds(0, 1), :]
    out[...] = sums[...].astype(BF16)


def shape(*dims, dtype=BF16):
    return jax.ShapeDtypeStruct(dims, dtype)


def near(*dims, dtype=BF16):
    return pltpu.VMEM(dims, dtype)


def far(array):
    return pltpu.with_memory_space_constraint(array, pltpu.HBM)


def kernel(body, outs, ins, scratch, limit, name, flops=0, moved=0):
    return pl.pallas_call(
        body,
        out_shape=outs,
        in_specs=ins,
        out_specs=[VM] * len(outs),
        scratch_shapes=scratch,
        compiler_params=pltpu.CompilerParams(vmem_limit_bytes=limit * 2**20),
        cost_estimate=pl.CostEstimate(flops=flops, bytes_accessed=moved, transcendentals=0),
        name=name,
    )


def neighbours(axis, first):
    count = lax.axis_size(axis)
    pairs = [(n, (n + 1) % count) for n in range(first, count, 2)]
    return sorted(pairs + [(b, a) for a, b in pairs])


def local(
    features, cache_first, cache_second, cache_head, gain_first, gain_second, gain_head,
    conv_first, conv_second, conv_head, bias_first, bias_second, bias_head,
):
    own, plain, rows_a, rows_b, cfw, csw, chw, vec, bias = kernel(
        first_kernel,
        [near(32, F, C), near(3, F * R * Q, 128, dtype=F32), near(MSG, F, C), near(MSG, F, C)]
        + [near(3, 64, 128, dtype=F32)] * 3 + [near(8, C, dtype=F32), near(8, 128, dtype=F32)],
        [ANY] * 10,
        [
            pltpu.VMEM((F, R, Q, C), BF16),
            pltpu.VMEM((3, 2, R, Q, C), BF16),
        ]
        + [pltpu.VMEM((C,), F32)] * 5
        + [
            pltpu.VMEM((32,), F32),
            pltpu.VMEM((3, F * R * Q, 128), F32),
            pltpu.SemaphoreType.DMA((13,)),
        ],
        12, "act_first",
    )(*[far(v) for v in (features, cache_first, cache_second, cache_head, gain_first, gain_second, gain_head,
                         bias_first, bias_second, bias_head)])
    got_a = lax.ppermute(rows_a, "ha", neighbours("ha", 0))
    got_b = lax.ppermute(rows_b, "ha", neighbours("ha", 1))
    cell_flops = 2 * F * 27 * C * C
    sums1, w1v, w2v, wy = kernel(
        inner_kernel,
        [near(R + 2, Q + 2, F, C, dtype=F32), near(3, 9, C, C), near(3, 9, C, C), near(4, 512, 3 * C)],
        [VM] * 2 + [ANY] * 3,
        [pltpu.VMEM((R * Q, F, 3 * C), BF16), pltpu.SemaphoreType.DMA((7,))],
        12, "inner", 32 * cell_flops, 17 * 2**20,
    )(own, cfw, far(conv_first), far(conv_second), far(jnp.swapaxes(conv_head, 3, 4)))
    top, bot, columns_a, columns_b = kernel(
        pack_kernel,
        [near(MSG, F, C)] * 4,
        [VM] * 6,
        [pltpu.VMEM((3, 128, 128), F32)] * 2,
        4, "pack_columns",
    )(own, got_a, got_b, cfw, csw, wy)
    side_a = lax.ppermute(columns_a, "wa", neighbours("wa", 0))
    side_b = lax.ppermute(columns_b, "wa", neighbours("wa", 1))
    sides, rows2, raw = kernel(
        rows_kernel,
        [near(R + 2, 4, F, C, dtype=F32), near(R + 2, 6, F, 3 * C), near(32, F, C)],
        [VM] * 7,
        [pltpu.VMEM((4, Q, F, 3 * C), BF16), pltpu.VMEM((4, Q + 2, F, C), F32)],
        10, "rows", 16 * cell_flops, 10 * 2**20,
    )(top, bot, sums1, plain, csw, vec, w1v)
    (slots,) = kernel(
        finish_kernel,
        [shape(F, 8, 8, 128)],
        [VM] * 13,
        [
            pltpu.VMEM((8, 4, F, 3 * C), BF16),
            pltpu.VMEM((R + 2, 4, F, C), F32),
            pltpu.VMEM((R + 2, Q + 2, F, 3 * C), BF16),
            pltpu.VMEM((4, 8, F, 3 * C), BF16),
            pltpu.VMEM((R * Q * F, C), F32),
            pltpu.VMEM((16 * F, 128), F32),
            pltpu.VMEM((2, 32, C), F32),
            pltpu.VMEM((2, 16, C), F32),
        ],
        20, "finish", 48 * cell_flops, 20 * 2**20,
    )(side_a, side_b, top, bot, sides, rows2, raw, csw, chw, vec, w1v, w2v, wy)
    arrived = lax.all_to_all(slots.reshape(F * 8, 8, 128), ("ha", "wa"), 0, 0, tiled=True)
    swapped = lax.ppermute(arrived, "wa", neighbours("wa", 0))
    return pl.pallas_call(
        last_kernel,
        out_shape=shape(128, 128),
        in_specs=[VM] * 3,
        out_specs=VM,
        scratch_shapes=[pltpu.VMEM((128, 128), F32)],
        compiler_params=pltpu.CompilerParams(vmem_limit_bytes=4 * 2**20),
        name="sum_patches",
    )(arrived, swapped, bias)


def solution(mesh):
    tile = P(None, "ha", "wa", None)
    return jax.shard_map(
        local,
        mesh=mesh,
        in_specs=(tile,) * 4 + (P(),) * 9,
        out_specs=P(("ha", "wa"), None),
        check_vma=False,
    )
```

```python
import jax
import jax.numpy as jnp
from jax import lax
from jax.experimental import pallas as pl
from jax.experimental.pallas import tpu as pltpu
from jax.sharding import PartitionSpec as P

BF16 = jnp.bfloat16
F32 = jnp.float32
F, R, Q, C = 16, 4, 8, 384
MSG = 19
PITCH = 40
VM = pl.BlockSpec(memory_space=pltpu.VMEM)
ANY = pl.BlockSpec(memory_space=pl.ANY)


def act(wide, half_gain):
    scale = lax.rsqrt(jnp.mean(wide * wide, axis=-1, keepdims=True) + 1e-06)
    h = wide * scale * half_gain
    return h + h * jnp.tanh(h)


def line(ref):
    return ref[...].reshape(1, -1)


def put_rows(ref, start, value):
    for n in range(3):
        ref[n, pl.ds(start, value.shape[0])] = value[:, n * 128 : (n + 1) * 128]


def rows_at(ref, start, count, stride):
    where = pl.ds(start, count, stride=stride) if stride > 1 else pl.ds(start, count)
    return jnp.concatenate([ref[n, where, :] for n in range(3)], axis=-1)


def stack(now, c0, c1):
    row = lax.broadcasted_iota(jnp.int32, now.shape, 0) % F
    c0, c1 = (jnp.concatenate([jnp.broadcast_to(c, (F, C)) for c in cs], axis=0) for cs in (c0, c1))
    one = jnp.where(row == 0, c1, pltpu.roll(now, 1, 0))
    two = jnp.where(row == 0, c0, jnp.where(row == 1, c1, pltpu.roll(now, 2, 0)))
    return two.astype(BF16), one.astype(BF16), now.astype(BF16)


def put(dst, where, now, c0, c1, valid=None):
    if valid is not None:
        keep = jnp.where(valid, 1.0, 0.0).astype(F32)
        now, c0, c1 = now * keep, [c * keep for c in c0], [c * keep for c in c1]
    for n, part in enumerate(stack(now, c0, c1)):
        dst[where + (slice(None), pl.ds(n * C, C))] = part.reshape(-1, F, C)


def bring(pairs, sems):
    copies = [pltpu.make_async_copy(src, dst, sems.at[n]) for n, (src, dst) in enumerate(pairs)]
    for copy in copies:
        copy.start()
    return copies


def first_kernel(
    feat_h, cf_h, cs_h, ch_h, g1_h, g2_h, gh_h, b1_h, b2_h, b3_h, own, plain, lo, hi, cfw, csw, chw, vec, bias,
    feat, caches, g1, g2, gh, b1, b2, b3, wide, sems,
):
    parts = [pl.ds(4 * n, 4) for n in range(4)]
    copies = bring(
        [(g1_h, g1)] + [(feat_h.at[part], feat.at[part]) for part in parts]
        + [(cf_h, caches.at[0]), (cs_h, caches.at[1]), (ch_h, caches.at[2]),
           (g2_h, g2), (gh_h, gh), (b1_h, b1), (b2_h, b2), (b3_h, b3)], sems
    )
    copies[0].wait()
    half = 0.5 * line(g1)
    for n, part in enumerate(parts):
        copies[1 + n].wait()
        x = feat[part].astype(F32).reshape(4 * R * Q, C)
        y = act(x, half)
        for m in range(4):
            put_rows(plain, (n * 4 + m) * PITCH, x[m * R * Q : (m + 1) * R * Q])
            put_rows(wide, (n * 4 + m) * PITCH, y[m * R * Q : (m + 1) * R * Q])
    for k in range(R * Q):
        cell = rows_at(wide, k, F, PITCH).astype(BF16)
        own[k] = cell
        if k < 16:
            lo[k] = cell
        else:
            hi[k - 16] = cell
    for copy in copies[5:]:
        copy.wait()
    for n, value in enumerate((0.5 * line(g2), 0.5 * line(gh), line(b1), line(b2))):
        vec[pl.ds(n, 1)] = value
    bias[pl.ds(0, 1)] = jnp.concatenate([line(b3)] * 4, axis=-1)
    for n, out in enumerate((cfw, csw, chw)):
        for h in range(R):
            for f in range(2):
                put_rows(out, h * 16 + f * 8, caches[n, f, h].astype(F32))
    for n in range(2):
        lo[16 + n] = rows_at(cfw, n * 16, 16, 1).astype(BF16)
        hi[16 + n] = rows_at(cfw, (2 + n) * 16, 16, 1).astype(BF16)
    lo[18] = rows_at(csw, 0, 16, 1).astype(BF16)
    hi[18] = rows_at(csw, 48, 16, 1).astype(BF16)


def pack_kernel(own, top, bot, cfw, csw, after, left, right, wide_f, wide_s):
    del after
    for n in range(2):
        put_rows(wide_f, n * 16, top[16 + n].astype(F32))
        put_rows(wide_f, (6 + n) * 16, bot[16 + n].astype(F32))
    put_rows(wide_s, 0, top[18].astype(F32))
    put_rows(wide_s, 5 * 16, bot[18].astype(F32))
    for n in range(3):
        wide_f[n, pl.ds(32, 64)] = cfw[n]
        wide_s[n, pl.ds(16, 64)] = csw[n]
        wide_s[n, pl.ds(96, 32)] = jnp.zeros((32, 128), F32)
    for out, base, edge in ((left, 0, 0), (right, 6, 7)):
        for c in range(2):
            for h in range(8):
                w = base + c
                if h < 2:
                    cell = top[h * Q + w]
                elif h < 6:
                    cell = own[(h - 2) * Q + w]
                else:
                    cell = bot[(h - 6) * Q + w]
                out[h * 2 + c] = cell
            out[16 + c] = rows_at(wide_f, base + c, 16, 8).astype(BF16)
        out[18] = rows_at(wide_s, edge, 16, 8).astype(BF16)


def cached_row(ref, base, w0, count):
    return [[rows_at(ref, base + 8 * f + w0 + w, 1, 1) for w in range(count)] for f in range(2)]


def cached_msg(block, count=Q):
    block = block.astype(F32)
    return [[block[8 * f + w : 8 * f + w + 1] for w in range(count)] for f in range(2)]


def three(weight, a):
    return jnp.concatenate([weight[a, 3 * b : 3 * b + 3].reshape(3 * C, C) for b in range(3)], axis=-1)


def hidden(dst, where, total, vec, cached, valid=None):
    wide = (total + vec[pl.ds(2, 1), :]).astype(BF16).astype(F32)
    put(dst, where, act(wide, vec[pl.ds(0, 1), :]), cached[0], cached[1], valid)


def place():
    ha, wa = lax.axis_index("ha"), lax.axis_index("wa")
    return ha > 0, ha < lax.axis_size("ha") - 1, wa > 0, wa < lax.axis_size("wa") - 1


def reach(rh, rw):
    return [
        (2 * (rh - 1 + m) + r, 2 * (rw - 1 + n) + s)
        for m in range(2) for n in range(2) for r in range(2) for s in range(2)
    ]


def inner_kernel(own, cfw, w1, w2, wh, acc, w1v, w2v, wy, s1, sems):
    def group(src, dst, a, sem):
        return [
            pltpu.make_async_copy(src.at[t, a, b], dst.at[a, b * 3 + t], sem) for b in range(3) for t in range(3)
        ]

    first = [group(w1, w1v, a, sems.at[a]) for a in range(3)]
    later = [copy for a in range(3) for copy in group(w2, w2v, a, sems.at[3 + a])]
    empty = []
    for rh in range(2):
        for rw in range(2):
            for k, (row, col) in enumerate(reach(rh, rw)):
                a, b = rh + 1 - row, rw + 1 - col
                where = pl.ds(k * 32, 32)
                if 0 <= a <= 2 and 0 <= b <= 2:
                    for t in range(3):
                        later.append(
                            pltpu.make_async_copy(
                                wh.at[t, a, b], wy.at[rh * 2 + rw, where, pl.ds(t * C, C)], sems.at[6]
                            )
                        )
                else:
                    empty.append((rh * 2 + rw, where))
    for copies in first[:2]:
        for copy in copies:
            copy.start()
    for where in empty:
        wy[where] = jnp.zeros((32, 3 * C), BF16)
    acc[...] = jnp.zeros_like(acc)

    def cells(h, _):
        c0, c1 = cached_row(cfw, h * 16, 0, Q)
        put(s1, (pl.ds(h * Q, Q),), own[pl.ds(h * Q, Q)].reshape(Q * F, C).astype(F32), c0, c1)
        return 0

    lax.fori_loop(0, R, cells, 0)
    for a in range(3):
        for copy in first[a]:
            copy.wait()
        for copy in (first[2], later, ())[a]:
            copy.start()
        part = jnp.dot(s1[...].reshape(R * Q * F, 3 * C), three(w1v, a), preferred_element_type=F32)
        for b in range(3):
            acc[2 - a : 2 - a + R, 2 - b : 2 - b + Q] += part[:, b * C : (b + 1) * C].reshape(R, Q, F, C)
    for copy in later:
        copy.wait()


def rows_kernel(top, bot, acc, plain, csw, vec, w1v, sides, s2, raw, s1, add):
    up, down, _, _ = place()
    for msg, h0, valid in ((top, 0, up), (bot, 2, down)):
        for h in range(2):
            c0, c1 = cached_msg(msg[16 + h])
            put(s1, (h0 + h, pl.ds(0, Q)), msg[pl.ds(h * Q, Q)].reshape(Q * F, C).astype(F32), c0, c1, valid)
    add[0:2] = acc[0:2]
    add[2:4] = acc[4:6]
    for a, (low, targets) in enumerate(((0, (0, 1)), (1, (0, 3)), (2, (2, 3)))):
        part = jnp.dot(s1[low : low + 2].reshape(2 * Q * F, 3 * C), three(w1v, a), preferred_element_type=F32)
        for n, row in enumerate(targets):
            for b in range(3):
                block = part[n * Q * F : (n + 1) * Q * F, b * C : (b + 1) * C]
                add[row, 2 - b : 2 - b + Q] += block.reshape(Q, F, C)
    for n, cached, valid in (
        (0, [c[1:7] for c in cached_msg(top[18])], up),
        (1, cached_row(csw, 0, 1, 6), None),
        (2, cached_row(csw, 16, 1, 6), None),
        (3, cached_row(csw, 32, 1, 6), None),
        (4, cached_row(csw, 48, 1, 6), None),
        (5, [c[1:7] for c in cached_msg(bot[18])], down),
    ):
        total = acc[n, 2:8] if 2 <= n < 4 else add[n if n < 2 else n - 2, 2:8]
        hidden(s2, (n, pl.ds(0, 6)), total.reshape(6 * F, C), vec, cached, valid)
    for k in range(R * Q):
        raw[k] = rows_at(plain, k, F, PITCH).astype(BF16)
    for n, col in enumerate((0, 8)):
        sides[0:2, 2 * n : 2 * n + 2] = add[0:2, col : col + 2]
        sides[2:4, 2 * n : 2 * n + 2] = acc[2:4, col : col + 2]
        sides[4:6, 2 * n : 2 * n + 2] = add[2:4, col : col + 2]


def finish_kernel(
    left, right, top, bot, sides, rows2, raw, csw, chw, vec, w1v, w2v, wy, out,
    s1, acc1, s2, s3, acc2, acch, side_f, side_s,
):
    up, down, west, east = place()
    for n, msg in enumerate((left, right)):
        for c in range(2):
            side_f[n, pl.ds(c * 16, 16)] = msg[16 + c].astype(F32)
        side_s[n] = msg[18].astype(F32)
    for n, (msg, side) in enumerate(((left, west), (right, east))):
        for h in range(8):
            valid = side & up if h < 2 else side & down if h >= 6 else side
            put(
                s1, (h, pl.ds(2 * n, 2)), msg[pl.ds(h * 2, 2)].reshape(2 * F, C).astype(F32),
                [side_f[n, pl.ds(c * 16 + h * 2, 1), :] for c in range(2)],
                [side_f[n, pl.ds(c * 16 + h * 2 + 1, 1), :] for c in range(2)], valid,
            )

    acc1[...] = sides[...]
    def columns(first):
        return jnp.concatenate([s1[a : a + 6, first : first + 2].reshape(12 * F, 3 * C) for a in range(3)], axis=-1)

    def column_tap(b, low, high):
        return jnp.concatenate([w1v[a, 3 * b : 3 * b + 3, :, low:high].reshape(3 * C, high - low) for a in range(3)], axis=0)

    for b, targets in enumerate(((0, 1), (0, 3), (2, 3))):
        part = jnp.dot(columns(b), column_tap(b, 0, 256), preferred_element_type=F32).reshape(6, 2, F, 256)
        for n, col in enumerate(targets):
            acc1[:, col, :, 0:256] += part[:, n]
    for b, moves in ((0, ((0, 0, 0), (1, 0, 1), (1, 1, 0))), (1, ((0, 0, 3), (0, 1, 2), (1, 1, 3)))):
        weight = jnp.concatenate([column_tap(b, 256, 384), column_tap(b + 1, 256, 384)], axis=-1)
        part = jnp.dot(columns(2 * b), weight, preferred_element_type=F32).reshape(6, 2, F, 256)
        for n, tap, col in moves:
            acc1[:, col, :, 256:384] += part[:, n, :, tap * 128 : (tap + 1) * 128]
    s2[:, 2:8] = rows2[...]
    for h in range(6):
        inside = up if h == 0 else down if h == 5 else True
        if h == 0:
            c0, c1 = cached_msg(top[18])
        elif h == 5:
            c0, c1 = cached_msg(bot[18])
        else:
            c0, c1 = cached_row(csw, (h - 1) * 16, 0, Q)
        for n, side in enumerate((west, east)):
            first = [side_s[n, pl.ds(h * 2 + f, 1), :] for f in range(2)]
            keep = jnp.where(side, 1.0, 0.0).astype(F32)
            total = acc1[h, 2 * n : 2 * n + 2].reshape(2 * F, C)
            wide = (total + vec[pl.ds(2, 1), :]).astype(BF16).astype(F32)
            now = act(wide, vec[pl.ds(0, 1), :])
            own_w = 0 if n == 0 else Q - 1
            pair = [now[:F], now[F:]]
            pair[n] = pair[n] * keep
            now = jnp.concatenate(pair, axis=0)
            olds = []
            for f, c in enumerate((c0, c1)):
                two = [first[f] * keep, c[own_w]]
                olds.append(two if n == 0 else two[::-1])
            put(s2, (h, pl.ds(8 * n, 2)), now, olds[0], olds[1], None if inside is True else inside)

    def window(row, rows):
        return jnp.concatenate(
            [s2[row : row + rows, b : b + Q].reshape(rows * Q * F, 3 * C) for b in range(3)], axis=-1
        )

    def one(b):
        return w2v[2, 3 * b : 3 * b + 3, :, 256:384].reshape(3 * C, 128)

    half = R // 2
    size = half * Q * F
    side = [w2v[a, :, :, 256:384].reshape(9 * C, 128) for a in range(2)]
    for top_row in range(0, R, half):
        rows = pl.ds(top_row * Q * F, size)
        for a in range(3):
            part = jnp.dot(
                window(top_row + a, half), w2v[a, :, :, 0:256].reshape(9 * C, 256), preferred_element_type=F32
            )
            if a == 0:
                acc2[rows, 0:256] = part
            else:
                acc2[rows, 0:256] += part
        pair = jnp.dot(window(top_row, half + 1), jnp.concatenate(side, axis=-1), preferred_element_type=F32)
        wider = s2[top_row + 2 : top_row + 2 + half, 0 : Q + 1].reshape(half * (Q + 1) * F, 3 * C)
        two = jnp.dot(wider, jnp.concatenate([one(0), one(1)], axis=-1), preferred_element_type=F32)
        two = two.reshape(half, Q + 1, F, 256)
        last_tap = jnp.dot(
            s2[top_row + 2 : top_row + 2 + half, 2 : 2 + Q].reshape(size, 3 * C), one(2), preferred_element_type=F32
        )
        acc2[rows, 256:384] = (
            pair[:size, :128] + pair[Q * F :, 128:] + last_tap
            + (two[:, :Q, :, :128] + two[:, 1:, :, 128:]).reshape(size, 128)
        )
        for h in range(top_row, top_row + half):
            wide = acc2[pl.ds(h * Q * F, Q * F)] + vec[pl.ds(3, 1), :]
            wide = wide + raw[pl.ds(h * Q, Q)].reshape(Q * F, C).astype(F32)
            c0, c1 = cached_row(chw, h * 16, 0, Q)
            now = act(wide.astype(BF16).astype(F32), vec[pl.ds(1, 1), :])
            for n, part in enumerate(stack(now, c0, c1)):
                part = part.reshape(Q, F, C)
                for w in range(Q):
                    s3[h % 2 * 2 + w % 2, h // 2 * 4 + w // 2, :, pl.ds(n * C, C)] = part[w]
    sums = {}
    for rh in range(2):
        for rw in range(2):
            part = lax.dot_general(
                s3[rh * 2 + rw].reshape(8 * F, 3 * C), wy[rh * 2 + rw], (((1,), (1,)), ((), ())),
                preferred_element_type=F32,
            )
            for k in range(8):
                for m in range(2):
                    for n in range(2):
                        pp, qq = (k // 4 + rh - 1 + m) % 3, (k % 4 + rw - 1 + n) % 5
                        slot = pp * 4 + qq if qq < 4 else 12 + pp
                        term = part[k * F : (k + 1) * F, (m * 2 + n) * 128 : (m * 2 + n + 1) * 128]
                        sums[slot] = sums[slot] + term if slot in sums else term
    for slot, total in sums.items():
        acch[pl.ds(slot * F, F)] = total
    acch[pl.ds(15 * F, F)] = jnp.zeros((F, 128), F32)

    for f in range(F):
        patches = acch[pl.ds(f, 16, stride=F), :].astype(BF16)
        for g in range(8):
            out[f, g] = patches[8 * (g % 2) : 8 * (g % 2) + 8]


def last_kernel(mine, theirs, bias, out, sums):
    ha_count = 16
    g = lax.axis_index("wa")
    even = g % 2 == 0
    first = [jnp.clip(2 * g - 1 + k, 0, ha_count - 1) * 8 for k in range(4)]

    def held(k, j, low, count):
        where = (first[k] + j, pl.ds(low % 8, count))
        here, there = mine[where].astype(F32), theirs[where].astype(F32)
        return jnp.where(even == (low < 8), here, there)

    lane = lax.broadcasted_iota(jnp.int32, (4, 128), 1)
    row = lax.broadcasted_iota(jnp.int32, (4, 128), 0)
    for k in range(2):
        for pr in range(2):
            other = k if pr == 0 else k + 2
            there = (2 * g + k > 0) if pr == 0 else (2 * g + k < ha_count - 1)
            upright = ((lane < 64) if pr == 0 else (lane >= 64)) & there

            def edge(j, pr=pr, k=k, other=other, upright=upright):
                mine = jnp.broadcast_to(held(k + 1, j, 12 + pr, 1), (4, 128))
                theirs = jnp.broadcast_to(held(other, j, 14, 1), (4, 128))
                return mine + jnp.where(upright, theirs, 0.0)

            for j in range(8):
                total = held(k + 1, j, pr * 4, 4)
                total = total + jnp.where(upright, held(other, j, 8, 4), 0.0)
                if j > 0:
                    total = total + jnp.where((row == 0) & (lane % 64 < 32), edge(j - 1), 0.0)
                if j < 7:
                    total = total + jnp.where((row == 3) & (lane % 64 >= 32), edge(j + 1), 0.0)
                sums[pl.ds((2 * k + pr) * 32 + j * 4, 4)] = total + bias[pl.ds(0, 1), :]
    out[...] = sums[...].astype(BF16)


def shape(*dims, dtype=BF16):
    return jax.ShapeDtypeStruct(dims, dtype)


def near(*dims, dtype=BF16):
    return pltpu.VMEM(dims, dtype)


def far(array):
    return pltpu.with_memory_space_constraint(array, pltpu.HBM)


def kernel(body, outs, ins, scratch, limit, name, flops=0, moved=0):
    return pl.pallas_call(
        body,
        out_shape=outs,
        in_specs=ins,
        out_specs=[VM] * len(outs),
        scratch_shapes=scratch,
        compiler_params=pltpu.CompilerParams(vmem_limit_bytes=limit * 2**20),
        cost_estimate=pl.CostEstimate(flops=flops, bytes_accessed=moved, transcendentals=0),
        name=name,
    )


def around(axis, step):
    count = lax.axis_size(axis)
    return [(n, (n + step) % count) for n in range(count)]


def local(
    features, cache_first, cache_second, cache_head, gain_first, gain_second, gain_head,
    conv_first, conv_second, conv_head, bias_first, bias_second, bias_head,
):
    own, plain, lo, hi, cfw, csw, chw, vec, bias = kernel(
        first_kernel,
        [near(32, F, C), near(3, F * PITCH, 128, dtype=F32), near(MSG, F, C), near(MSG, F, C)]
        + [near(3, 64, 128, dtype=F32)] * 3 + [near(8, C, dtype=F32), near(8, 128, dtype=F32)],
        [ANY] * 10,
        [
            pltpu.VMEM((F, R, Q, C), BF16),
            pltpu.VMEM((3, 2, R, Q, C), BF16),
        ]
        + [pltpu.VMEM((C,), F32)] * 5
        + [
            pltpu.VMEM((32,), F32),
            pltpu.VMEM((3, F * PITCH, 128), F32),
            pltpu.SemaphoreType.DMA((13,)),
        ],
        12, "act_first",
    )(*[far(v) for v in (features, cache_first, cache_second, cache_head, gain_first, gain_second, gain_head,
                         bias_first, bias_second, bias_head)])
    top = lax.ppermute(hi, "ha", around("ha", 1))
    bot = lax.ppermute(lo, "ha", around("ha", -1))
    cell_flops = 2 * F * 27 * C * C
    sums1, w1v, w2v, wy = kernel(
        inner_kernel,
        [near(R + 2, Q + 2, F, C, dtype=F32), near(3, 9, C, C), near(3, 9, C, C), near(4, 512, 3 * C)],
        [VM] * 2 + [ANY] * 3,
        [pltpu.VMEM((R * Q, F, 3 * C), BF16), pltpu.SemaphoreType.DMA((7,))],
        12, "inner", 32 * cell_flops, 17 * 2**20,
    )(own, cfw, far(conv_first), far(conv_second), far(jnp.swapaxes(conv_head, 3, 4)))
    to_left, to_right = kernel(
        pack_kernel,
        [near(MSG, F, C)] * 2,
        [VM] * 6,
        [pltpu.VMEM((3, 128, 128), F32)] * 2,
        4, "pack_columns",
    )(own, top, bot, cfw, csw, wy)
    left = lax.ppermute(to_right, "wa", around("wa", 1))
    right = lax.ppermute(to_left, "wa", around("wa", -1))
    sides, rows2, raw = kernel(
        rows_kernel,
        [near(R + 2, 4, F, C, dtype=F32), near(R + 2, 6, F, 3 * C), near(32, F, C)],
        [VM] * 7,
        [pltpu.VMEM((4, Q, F, 3 * C), BF16), pltpu.VMEM((4, Q + 2, F, C), F32)],
        10, "rows", 16 * cell_flops, 10 * 2**20,
    )(top, bot, sums1, plain, csw, vec, w1v)
    (slots,) = kernel(
        finish_kernel,
        [shape(F, 8, 8, 128)],
        [VM] * 13,
        [
            pltpu.VMEM((8, 4, F, 3 * C), BF16),
            pltpu.VMEM((R + 2, 4, F, C), F32),
            pltpu.VMEM((R + 2, Q + 2, F, 3 * C), BF16),
            pltpu.VMEM((4, 8, F, 3 * C), BF16),
            pltpu.VMEM((R * Q * F, C), F32),
            pltpu.VMEM((16 * F, 128), F32),
            pltpu.VMEM((2, 32, C), F32),
            pltpu.VMEM((2, 16, C), F32),
        ],
        20, "finish", 48 * cell_flops, 20 * 2**20,
    )(left, right, top, bot, sides, rows2, raw, csw, chw, vec, w1v, w2v, wy)
    arrived = lax.all_to_all(slots.reshape(F * 8, 8, 128), ("ha", "wa"), 0, 0, tiled=True)
    pairs = [(n, n ^ 1) for n in range(lax.axis_size("wa"))]
    swapped = lax.ppermute(arrived, "wa", pairs)
    return pl.pallas_call(
        last_kernel,
        out_shape=shape(128, 128),
        in_specs=[VM] * 3,
        out_specs=VM,
        scratch_shapes=[pltpu.VMEM((128, 128), F32)],
        compiler_params=pltpu.CompilerParams(vmem_limit_bytes=4 * 2**20),
        name="sum_patches",
    )(arrived, swapped, bias)


def solution(mesh):
    tile = P(None, "ha", "wa", None)
    return jax.shard_map(
        local,
        mesh=mesh,
        in_specs=(tile,) * 4 + (P(),) * 9,
        out_specs=P(("ha", "wa"), None),
        check_vma=False,
    )
```

```python
import jax
import jax.numpy as jnp
from jax import lax
from jax.experimental import pallas as pl
from jax.experimental.pallas import tpu as pltpu
from jax.sharding import PartitionSpec as P

BF16 = jnp.bfloat16
F32 = jnp.float32
F, R, Q, C = 16, 4, 8, 384
MSG = 19
PITCH = 40
VM = pl.BlockSpec(memory_space=pltpu.VMEM)
ANY = pl.BlockSpec(memory_space=pl.ANY)


def act(wide, half_gain):
    scale = lax.rsqrt(jnp.mean(wide * wide, axis=-1, keepdims=True) + 1e-06)
    h = wide * scale * half_gain
    return h + h * jnp.tanh(h)


def line(ref):
    return ref[...].reshape(1, -1)


def put_rows(ref, start, value):
    for n in range(3):
        ref[n, pl.ds(start, value.shape[0])] = value[:, n * 128 : (n + 1) * 128]


def rows_at(ref, start, count, stride):
    where = pl.ds(start, count, stride=stride) if stride > 1 else pl.ds(start, count)
    return jnp.concatenate([ref[n, where, :] for n in range(3)], axis=-1)


def stack(now, c0, c1):
    row = lax.broadcasted_iota(jnp.int32, now.shape, 0) % F
    c0, c1 = (jnp.concatenate([jnp.broadcast_to(c, (F, C)) for c in cs], axis=0) for cs in (c0, c1))
    one = jnp.where(row == 0, c1, pltpu.roll(now, 1, 0))
    two = jnp.where(row == 0, c0, jnp.where(row == 1, c1, pltpu.roll(now, 2, 0)))
    return two.astype(BF16), one.astype(BF16), now.astype(BF16)


def put(dst, where, now, c0, c1, valid=None):
    if valid is not None:
        keep = jnp.where(valid, 1.0, 0.0).astype(F32)
        now, c0, c1 = now * keep, [c * keep for c in c0], [c * keep for c in c1]
    for n, part in enumerate(stack(now, c0, c1)):
        dst[where + (slice(None), pl.ds(n * C, C))] = part.reshape(-1, F, C)


def bring(pairs, sems):
    copies = [pltpu.make_async_copy(src, dst, sems.at[n]) for n, (src, dst) in enumerate(pairs)]
    for copy in copies:
        copy.start()
    return copies


def first_kernel(
    feat_h, cf_h, cs_h, ch_h, g1_h, g2_h, gh_h, b1_h, b2_h, b3_h, own, plain, lo, hi, cfw, csw, chw, vec, bias,
    feat, caches, g1, g2, gh, b1, b2, b3, wide, sems,
):
    parts = [pl.ds(4 * n, 4) for n in range(4)]
    copies = bring(
        [(g1_h, g1)] + [(feat_h.at[part], feat.at[part]) for part in parts]
        + [(cf_h, caches.at[0]), (cs_h, caches.at[1]), (ch_h, caches.at[2]),
           (g2_h, g2), (gh_h, gh), (b1_h, b1), (b2_h, b2), (b3_h, b3)], sems
    )
    copies[0].wait()
    half = 0.5 * line(g1)
    for n, part in enumerate(parts):
        copies[1 + n].wait()
        x = feat[part].astype(F32).reshape(4 * R * Q, C)
        y = act(x, half)
        for m in range(4):
            put_rows(plain, (n * 4 + m) * PITCH, x[m * R * Q : (m + 1) * R * Q])
            put_rows(wide, (n * 4 + m) * PITCH, y[m * R * Q : (m + 1) * R * Q])
    for k in range(R * Q):
        cell = rows_at(wide, k, F, PITCH).astype(BF16)
        own[k] = cell
        if k < 16:
            lo[k] = cell
        else:
            hi[k - 16] = cell
    for copy in copies[5:]:
        copy.wait()
    for n, value in enumerate((0.5 * line(g2), 0.5 * line(gh), line(b1), line(b2))):
        vec[pl.ds(n, 1)] = value
    bias[pl.ds(0, 1)] = jnp.concatenate([line(b3)] * 4, axis=-1)
    for n, out in enumerate((cfw, csw, chw)):
        for h in range(R):
            for f in range(2):
                put_rows(out, h * 16 + f * 8, caches[n, f, h].astype(F32))
    for n in range(2):
        lo[16 + n] = rows_at(cfw, n * 16, 16, 1).astype(BF16)
        hi[16 + n] = rows_at(cfw, (2 + n) * 16, 16, 1).astype(BF16)
    lo[18] = rows_at(csw, 0, 16, 1).astype(BF16)
    hi[18] = rows_at(csw, 48, 16, 1).astype(BF16)


def pack_kernel(own, top, bot, cfw, csw, after, left, right, wide_f, wide_s):
    del after
    for n in range(2):
        put_rows(wide_f, n * 16, top[16 + n].astype(F32))
        put_rows(wide_f, (6 + n) * 16, bot[16 + n].astype(F32))
    put_rows(wide_s, 0, top[18].astype(F32))
    put_rows(wide_s, 5 * 16, bot[18].astype(F32))
    for n in range(3):
        wide_f[n, pl.ds(32, 64)] = cfw[n]
        wide_s[n, pl.ds(16, 64)] = csw[n]
        wide_s[n, pl.ds(96, 32)] = jnp.zeros((32, 128), F32)
    for out, base, edge in ((left, 0, 0), (right, 6, 7)):
        for c in range(2):
            for h in range(8):
                w = base + c
                if h < 2:
                    cell = top[h * Q + w]
                elif h < 6:
                    cell = own[(h - 2) * Q + w]
                else:
                    cell = bot[(h - 6) * Q + w]
                out[h * 2 + c] = cell
            out[16 + c] = rows_at(wide_f, base + c, 16, 8).astype(BF16)
        out[18] = rows_at(wide_s, edge, 16, 8).astype(BF16)


def cached_row(ref, base, w0, count):
    return [[rows_at(ref, base + 8 * f + w0 + w, 1, 1) for w in range(count)] for f in range(2)]


def cached_msg(block, count=Q):
    block = block.astype(F32)
    return [[block[8 * f + w : 8 * f + w + 1] for w in range(count)] for f in range(2)]


def three(weight, a):
    return jnp.concatenate([weight[a, 3 * b : 3 * b + 3].reshape(3 * C, C) for b in range(3)], axis=-1)


def hidden(dst, where, total, vec, cached, valid=None):
    wide = (total + vec[pl.ds(2, 1), :]).astype(BF16).astype(F32)
    put(dst, where, act(wide, vec[pl.ds(0, 1), :]), cached[0], cached[1], valid)


def place():
    ha, wa = lax.axis_index("ha"), lax.axis_index("wa")
    return ha > 0, ha < lax.axis_size("ha") - 1, wa > 0, wa < lax.axis_size("wa") - 1


def reach(rh, rw):
    return [
        (2 * (rh - 1 + m) + r, 2 * (rw - 1 + n) + s)
        for m in range(2) for n in range(2) for r in range(2) for s in range(2)
    ]


def inner_kernel(own, cfw, w1, w2, wh, acc, w1v, w2v, flat, s1, sems):
    def group(src, dst, a, sem):
        return [
            pltpu.make_async_copy(src.at[t, a, b], dst.at[a, b * 3 + t], sem) for b in range(3) for t in range(3)
        ]

    first = [group(w1, w1v, a, sems.at[a]) for a in range(3)]
    later = [copy for a in range(3) for copy in group(w2, w2v, a, sems.at[3 + a])]
    for t in range(3):
        for a in range(3):
            for b in range(3):
                later.append(
                    pltpu.make_async_copy(
                        wh.at[t, a, b], flat.at[pl.ds((a * 3 + b) * 32, 32), pl.ds(t * C, C)], sems.at[6]
                    )
                )
    for copies in first[:2]:
        for copy in copies:
            copy.start()
    acc[...] = jnp.zeros_like(acc)

    def cells(h, _):
        c0, c1 = cached_row(cfw, h * 16, 0, Q)
        put(s1, (pl.ds(h * Q, Q),), own[pl.ds(h * Q, Q)].reshape(Q * F, C).astype(F32), c0, c1)
        return 0

    lax.fori_loop(0, R, cells, 0)
    for a in range(3):
        for copy in first[a]:
            copy.wait()
        for copy in (first[2], later, ())[a]:
            copy.start()
        part = jnp.dot(s1[...].reshape(R * Q * F, 3 * C), three(w1v, a), preferred_element_type=F32)
        for b in range(3):
            acc[2 - a : 2 - a + R, 2 - b : 2 - b + Q] += part[:, b * C : (b + 1) * C].reshape(R, Q, F, C)
    for copy in later:
        copy.wait()


def rows_kernel(top, bot, acc, plain, csw, vec, w1v, flat, sides, s2, raw, wy, s1, add):
    up, down, _, _ = place()
    for msg, h0, valid in ((top, 0, up), (bot, 2, down)):
        for h in range(2):
            c0, c1 = cached_msg(msg[16 + h])
            put(s1, (h0 + h, pl.ds(0, Q)), msg[pl.ds(h * Q, Q)].reshape(Q * F, C).astype(F32), c0, c1, valid)
    add[0:2] = acc[0:2]
    add[2:4] = acc[4:6]
    for a, (low, targets) in enumerate(((0, (0, 1)), (1, (0, 3)), (2, (2, 3)))):
        part = jnp.dot(s1[low : low + 2].reshape(2 * Q * F, 3 * C), three(w1v, a), preferred_element_type=F32)
        for n, row in enumerate(targets):
            for b in range(3):
                block = part[n * Q * F : (n + 1) * Q * F, b * C : (b + 1) * C]
                add[row, 2 - b : 2 - b + Q] += block.reshape(Q, F, C)
    for n, cached, valid in (
        (0, [c[1:7] for c in cached_msg(top[18])], up),
        (1, cached_row(csw, 0, 1, 6), None),
        (2, cached_row(csw, 16, 1, 6), None),
        (3, cached_row(csw, 32, 1, 6), None),
        (4, cached_row(csw, 48, 1, 6), None),
        (5, [c[1:7] for c in cached_msg(bot[18])], down),
    ):
        total = acc[n, 2:8] if 2 <= n < 4 else add[n if n < 2 else n - 2, 2:8]
        hidden(s2, (n, pl.ds(0, 6)), total.reshape(6 * F, C), vec, cached, valid)
    for k in range(R * Q):
        raw[k] = rows_at(plain, k, F, PITCH).astype(BF16)
    turned = jnp.transpose(flat[...])
    none = jnp.zeros((3 * C, 32), BF16)
    for rh in range(2):
        for rw in range(2):
            targets = reach(rh, rw)
            for patch in range(4):
                parts = []
                for row, col in targets[4 * patch : 4 * patch + 4]:
                    a, b = rh + 1 - row, rw + 1 - col
                    low = (a * 3 + b) * 32
                    parts.append(turned[:, low : low + 32] if 0 <= a <= 2 and 0 <= b <= 2 else none)
                wy[rh * 2 + rw, :, patch * 128 : (patch + 1) * 128] = jnp.concatenate(parts, axis=-1)
    for n, col in enumerate((0, 8)):
        sides[0:2, 2 * n : 2 * n + 2] = add[0:2, col : col + 2]
        sides[2:4, 2 * n : 2 * n + 2] = acc[2:4, col : col + 2]
        sides[4:6, 2 * n : 2 * n + 2] = add[2:4, col : col + 2]


def finish_kernel(
    left, right, top, bot, sides, rows2, raw, csw, chw, vec, w1v, w2v, wy, out,
    s1, acc1, s2, s3, acc2, acch, side_f, side_s,
):
    up, down, west, east = place()
    for n, msg in enumerate((left, right)):
        for c in range(2):
            side_f[n, pl.ds(c * 16, 16)] = msg[16 + c].astype(F32)
        side_s[n] = msg[18].astype(F32)
    for n, (msg, side) in enumerate(((left, west), (right, east))):
        for h in range(8):
            valid = side & up if h < 2 else side & down if h >= 6 else side
            put(
                s1, (h, pl.ds(2 * n, 2)), msg[pl.ds(h * 2, 2)].reshape(2 * F, C).astype(F32),
                [side_f[n, pl.ds(c * 16 + h * 2, 1), :] for c in range(2)],
                [side_f[n, pl.ds(c * 16 + h * 2 + 1, 1), :] for c in range(2)], valid,
            )

    acc1[...] = sides[...]
    def columns(first):
        return jnp.concatenate([s1[a : a + 6, first : first + 2].reshape(12 * F, 3 * C) for a in range(3)], axis=-1)

    def column_tap(b, low, high):
        return jnp.concatenate([w1v[a, 3 * b : 3 * b + 3, :, low:high].reshape(3 * C, high - low) for a in range(3)], axis=0)

    for b, targets in enumerate(((0, 1), (0, 3), (2, 3))):
        part = jnp.dot(columns(b), column_tap(b, 0, 256), preferred_element_type=F32).reshape(6, 2, F, 256)
        for n, col in enumerate(targets):
            acc1[:, col, :, 0:256] += part[:, n]
    for b, moves in ((0, ((0, 0, 0), (1, 0, 1), (1, 1, 0))), (1, ((0, 0, 3), (0, 1, 2), (1, 1, 3)))):
        weight = jnp.concatenate([column_tap(b, 256, 384), column_tap(b + 1, 256, 384)], axis=-1)
        part = jnp.dot(columns(2 * b), weight, preferred_element_type=F32).reshape(6, 2, F, 256)
        for n, tap, col in moves:
            acc1[:, col, :, 256:384] += part[:, n, :, tap * 128 : (tap + 1) * 128]
    s2[:, 2:8] = rows2[...]
    for h in range(6):
        inside = up if h == 0 else down if h == 5 else True
        if h == 0:
            c0, c1 = cached_msg(top[18])
        elif h == 5:
            c0, c1 = cached_msg(bot[18])
        else:
            c0, c1 = cached_row(csw, (h - 1) * 16, 0, Q)
        for n, side in enumerate((west, east)):
            first = [side_s[n, pl.ds(h * 2 + f, 1), :] for f in range(2)]
            keep = jnp.where(side, 1.0, 0.0).astype(F32)
            total = acc1[h, 2 * n : 2 * n + 2].reshape(2 * F, C)
            wide = (total + vec[pl.ds(2, 1), :]).astype(BF16).astype(F32)
            now = act(wide, vec[pl.ds(0, 1), :])
            own_w = 0 if n == 0 else Q - 1
            pair = [now[:F], now[F:]]
            pair[n] = pair[n] * keep
            now = jnp.concatenate(pair, axis=0)
            olds = []
            for f, c in enumerate((c0, c1)):
                two = [first[f] * keep, c[own_w]]
                olds.append(two if n == 0 else two[::-1])
            put(s2, (h, pl.ds(8 * n, 2)), now, olds[0], olds[1], None if inside is True else inside)

    def window(row, rows):
        return jnp.concatenate(
            [s2[row : row + rows, b : b + Q].reshape(rows * Q * F, 3 * C) for b in range(3)], axis=-1
        )

    def one(b):
        return w2v[2, 3 * b : 3 * b + 3, :, 256:384].reshape(3 * C, 128)

    half = R // 2
    size = half * Q * F
    side = [w2v[a, :, :, 256:384].reshape(9 * C, 128) for a in range(2)]
    for top_row in range(0, R, half):
        rows = pl.ds(top_row * Q * F, size)
        for a in range(3):
            part = jnp.dot(
                window(top_row + a, half), w2v[a, :, :, 0:256].reshape(9 * C, 256), preferred_element_type=F32
            )
            if a == 0:
                acc2[rows, 0:256] = part
            else:
                acc2[rows, 0:256] += part
        pair = jnp.dot(window(top_row, half + 1), jnp.concatenate(side, axis=-1), preferred_element_type=F32)
        wider = s2[top_row + 2 : top_row + 2 + half, 0 : Q + 1].reshape(half * (Q + 1) * F, 3 * C)
        two = jnp.dot(wider, jnp.concatenate([one(0), one(1)], axis=-1), preferred_element_type=F32)
        two = two.reshape(half, Q + 1, F, 256)
        last_tap = jnp.dot(
            s2[top_row + 2 : top_row + 2 + half, 2 : 2 + Q].reshape(size, 3 * C), one(2), preferred_element_type=F32
        )
        acc2[rows, 256:384] = (
            pair[:size, :128] + pair[Q * F :, 128:] + last_tap
            + (two[:, :Q, :, :128] + two[:, 1:, :, 128:]).reshape(size, 128)
        )
        for h in range(top_row, top_row + half):
            wide = acc2[pl.ds(h * Q * F, Q * F)] + vec[pl.ds(3, 1), :]
            wide = wide + raw[pl.ds(h * Q, Q)].reshape(Q * F, C).astype(F32)
            c0, c1 = cached_row(chw, h * 16, 0, Q)
            now = act(wide.astype(BF16).astype(F32), vec[pl.ds(1, 1), :])
            for n, part in enumerate(stack(now, c0, c1)):
                part = part.reshape(Q, F, C)
                for w in range(Q):
                    s3[h % 2 * 2 + w % 2, h // 2 * 4 + w // 2, :, pl.ds(n * C, C)] = part[w]
    sums = {}
    for rh in range(2):
        for rw in range(2):
            part = jnp.dot(
                s3[rh * 2 + rw].reshape(8 * F, 3 * C), wy[rh * 2 + rw], preferred_element_type=F32
            )
            for k in range(8):
                for m in range(2):
                    for n in range(2):
                        pp, qq = (k // 4 + rh - 1 + m) % 3, (k % 4 + rw - 1 + n) % 5
                        slot = pp * 4 + qq if qq < 4 else 12 + pp
                        term = part[k * F : (k + 1) * F, (m * 2 + n) * 128 : (m * 2 + n + 1) * 128]
                        sums[slot] = sums[slot] + term if slot in sums else term
    for slot, total in sums.items():
        acch[pl.ds(slot * F, F)] = total
    acch[pl.ds(15 * F, F)] = jnp.zeros((F, 128), F32)

    for f in range(F):
        patches = acch[pl.ds(f, 16, stride=F), :].astype(BF16)
        for g in range(8):
            out[f, g] = patches[8 * (g % 2) : 8 * (g % 2) + 8]


def last_kernel(mine, theirs, bias, out, sums):
    ha_count = 16
    g = lax.axis_index("wa")
    even = g % 2 == 0
    first = [jnp.clip(2 * g - 1 + k, 0, ha_count - 1) * 8 for k in range(4)]

    def held(k, j, low, count):
        where = (first[k] + j, pl.ds(low % 8, count))
        here, there = mine[where].astype(F32), theirs[where].astype(F32)
        return jnp.where(even == (low < 8), here, there)

    lane = lax.broadcasted_iota(jnp.int32, (4, 128), 1)
    row = lax.broadcasted_iota(jnp.int32, (4, 128), 0)
    for k in range(2):
        for pr in range(2):
            other = k if pr == 0 else k + 2
            there = (2 * g + k > 0) if pr == 0 else (2 * g + k < ha_count - 1)
            upright = ((lane < 64) if pr == 0 else (lane >= 64)) & there

            def edge(j, pr=pr, k=k, other=other, upright=upright):
                mine = jnp.broadcast_to(held(k + 1, j, 12 + pr, 1), (4, 128))
                theirs = jnp.broadcast_to(held(other, j, 14, 1), (4, 128))
                return mine + jnp.where(upright, theirs, 0.0)

            for j in range(8):
                total = held(k + 1, j, pr * 4, 4)
                total = total + jnp.where(upright, held(other, j, 8, 4), 0.0)
                if j > 0:
                    total = total + jnp.where((row == 0) & (lane % 64 < 32), edge(j - 1), 0.0)
                if j < 7:
                    total = total + jnp.where((row == 3) & (lane % 64 >= 32), edge(j + 1), 0.0)
                sums[pl.ds((2 * k + pr) * 32 + j * 4, 4)] = total + bias[pl.ds(0, 1), :]
    out[...] = sums[...].astype(BF16)


def shape(*dims, dtype=BF16):
    return jax.ShapeDtypeStruct(dims, dtype)


def near(*dims, dtype=BF16):
    return pltpu.VMEM(dims, dtype)


def far(array):
    return pltpu.with_memory_space_constraint(array, pltpu.HBM)


def kernel(body, outs, ins, scratch, limit, name, flops=0, moved=0):
    return pl.pallas_call(
        body,
        out_shape=outs,
        in_specs=ins,
        out_specs=[VM] * len(outs),
        scratch_shapes=scratch,
        compiler_params=pltpu.CompilerParams(vmem_limit_bytes=limit * 2**20),
        cost_estimate=pl.CostEstimate(flops=flops, bytes_accessed=moved, transcendentals=0),
        name=name,
    )


def around(axis, step):
    count = lax.axis_size(axis)
    return [(n, (n + step) % count) for n in range(count)]


def local(
    features, cache_first, cache_second, cache_head, gain_first, gain_second, gain_head,
    conv_first, conv_second, conv_head, bias_first, bias_second, bias_head,
):
    own, plain, lo, hi, cfw, csw, chw, vec, bias = kernel(
        first_kernel,
        [near(32, F, C), near(3, F * PITCH, 128, dtype=F32), near(MSG, F, C), near(MSG, F, C)]
        + [near(3, 64, 128, dtype=F32)] * 3 + [near(8, C, dtype=F32), near(8, 128, dtype=F32)],
        [ANY] * 10,
        [
            pltpu.VMEM((F, R, Q, C), BF16),
            pltpu.VMEM((3, 2, R, Q, C), BF16),
        ]
        + [pltpu.VMEM((C,), F32)] * 5
        + [
            pltpu.VMEM((32,), F32),
            pltpu.VMEM((3, F * PITCH, 128), F32),
            pltpu.SemaphoreType.DMA((13,)),
        ],
        12, "act_first",
    )(*[far(v) for v in (features, cache_first, cache_second, cache_head, gain_first, gain_second, gain_head,
                         bias_first, bias_second, bias_head)])
    top = lax.ppermute(hi, "ha", around("ha", 1))
    bot = lax.ppermute(lo, "ha", around("ha", -1))
    cell_flops = 2 * F * 27 * C * C
    sums1, w1v, w2v, flat = kernel(
        inner_kernel,
        [near(R + 2, Q + 2, F, C, dtype=F32), near(3, 9, C, C), near(3, 9, C, C), near(9 * 32, 3 * C)],
        [VM] * 2 + [ANY] * 3,
        [pltpu.VMEM((R * Q, F, 3 * C), BF16), pltpu.SemaphoreType.DMA((7,))],
        12, "inner", 32 * cell_flops, 17 * 2**20,
    )(own, cfw, far(conv_first), far(conv_second), far(jnp.swapaxes(conv_head, 3, 4)))
    to_left, to_right = kernel(
        pack_kernel,
        [near(MSG, F, C)] * 2,
        [VM] * 6,
        [pltpu.VMEM((3, 128, 128), F32)] * 2,
        4, "pack_columns",
    )(own, top, bot, cfw, csw, flat)
    left = lax.ppermute(to_right, "wa", around("wa", 1))
    right = lax.ppermute(to_left, "wa", around("wa", -1))
    sides, rows2, raw, wy = kernel(
        rows_kernel,
        [near(R + 2, 4, F, C, dtype=F32), near(R + 2, 6, F, 3 * C), near(32, F, C),
         near(4, 3 * C, 512)],
        [VM] * 8,
        [pltpu.VMEM((4, Q, F, 3 * C), BF16), pltpu.VMEM((4, Q + 2, F, C), F32)],
        16, "rows", 16 * cell_flops, 10 * 2**20,
    )(top, bot, sums1, plain, csw, vec, w1v, flat)
    (slots,) = kernel(
        finish_kernel,
        [shape(F, 8, 8, 128)],
        [VM] * 13,
        [
            pltpu.VMEM((8, 4, F, 3 * C), BF16),
            pltpu.VMEM((R + 2, 4, F, C), F32),
            pltpu.VMEM((R + 2, Q + 2, F, 3 * C), BF16),
            pltpu.VMEM((4, 8, F, 3 * C), BF16),
            pltpu.VMEM((R * Q * F, C), F32),
            pltpu.VMEM((16 * F, 128), F32),
            pltpu.VMEM((2, 32, C), F32),
            pltpu.VMEM((2, 16, C), F32),
        ],
        20, "finish", 48 * cell_flops, 20 * 2**20,
    )(left, right, top, bot, sides, rows2, raw, csw, chw, vec, w1v, w2v, wy)
    arrived = lax.all_to_all(slots.reshape(F * 8, 8, 128), ("ha", "wa"), 0, 0, tiled=True)
    pairs = [(n, n ^ 1) for n in range(lax.axis_size("wa"))]
    swapped = lax.ppermute(arrived, "wa", pairs)
    return pl.pallas_call(
        last_kernel,
        out_shape=shape(128, 128),
        in_specs=[VM] * 3,
        out_specs=VM,
        scratch_shapes=[pltpu.VMEM((128, 128), F32)],
        compiler_params=pltpu.CompilerParams(vmem_limit_bytes=4 * 2**20),
        name="sum_patches",
    )(arrived, swapped, bias)


def solution(mesh):
    tile = P(None, "ha", "wa", None)
    return jax.shard_map(
        local,
        mesh=mesh,
        in_specs=(tile,) * 4 + (P(),) * 9,
        out_specs=P(("ha", "wa"), None),
        check_vma=False,
    )
```

```python
import jax
import jax.numpy as jnp
from jax import lax
from jax.experimental import pallas as pl
from jax.experimental.pallas import tpu as pltpu
from jax.sharding import PartitionSpec as P

BF16 = jnp.bfloat16
F32 = jnp.float32
F, R, Q, C = 16, 4, 8, 384
MSG = 19
PITCH = 40
VM = pl.BlockSpec(memory_space=pltpu.VMEM)
ANY = pl.BlockSpec(memory_space=pl.ANY)


def act(wide, half_gain):
    scale = lax.rsqrt(jnp.mean(wide * wide, axis=-1, keepdims=True) + 1e-06)
    h = wide * scale * half_gain
    return h + h * jnp.tanh(h)


def line(ref):
    return ref[...].reshape(1, -1)


def put_rows(ref, start, value):
    for n in range(3):
        ref[n, pl.ds(start, value.shape[0])] = value[:, n * 128 : (n + 1) * 128]


def rows_at(ref, start, count, stride):
    where = pl.ds(start, count, stride=stride) if stride > 1 else pl.ds(start, count)
    return jnp.concatenate([ref[n, where, :] for n in range(3)], axis=-1)


def stack(now, c0, c1):
    row = lax.broadcasted_iota(jnp.int32, now.shape, 0) % F
    c0, c1 = (jnp.concatenate([jnp.broadcast_to(c, (F, C)) for c in cs], axis=0) for cs in (c0, c1))
    one = jnp.where(row == 0, c1, pltpu.roll(now, 1, 0))
    two = jnp.where(row == 0, c0, jnp.where(row == 1, c1, pltpu.roll(now, 2, 0)))
    return two.astype(BF16), one.astype(BF16), now.astype(BF16)


def put(dst, where, now, c0, c1, valid=None):
    if valid is not None:
        keep = jnp.where(valid, 1.0, 0.0).astype(F32)
        now, c0, c1 = now * keep, [c * keep for c in c0], [c * keep for c in c1]
    for n, part in enumerate(stack(now, c0, c1)):
        dst[where + (slice(None), pl.ds(n * C, C))] = part.reshape(-1, F, C)


def bring(pairs, sems):
    copies = [pltpu.make_async_copy(src, dst, sems.at[n]) for n, (src, dst) in enumerate(pairs)]
    for copy in copies:
        copy.start()
    return copies


def first_kernel(
    feat_h, cf_h, cs_h, ch_h, g1_h, g2_h, gh_h, b1_h, b2_h, b3_h, own, plain, lo, hi, cfw, csw, chw, vec, bias,
    feat, caches, g1, g2, gh, b1, b2, b3, wide, sems,
):
    parts = [pl.ds(4 * n, 4) for n in range(4)]
    copies = bring(
        [(g1_h, g1)] + [(feat_h.at[part], feat.at[part]) for part in parts]
        + [(cf_h, caches.at[0]), (cs_h, caches.at[1]), (ch_h, caches.at[2]),
           (g2_h, g2), (gh_h, gh), (b1_h, b1), (b2_h, b2), (b3_h, b3)], sems
    )
    copies[0].wait()
    half = 0.5 * line(g1)
    for n, part in enumerate(parts):
        copies[1 + n].wait()
        x = feat[part].astype(F32).reshape(4 * R * Q, C)
        y = act(x, half)
        for m in range(4):
            put_rows(plain, (n * 4 + m) * PITCH, x[m * R * Q : (m + 1) * R * Q])
            put_rows(wide, (n * 4 + m) * PITCH, y[m * R * Q : (m + 1) * R * Q])
    for k in range(R * Q):
        cell = rows_at(wide, k, F, PITCH).astype(BF16)
        own[k] = cell
        if k < 16:
            lo[k] = cell
        else:
            hi[k - 16] = cell
    for copy in copies[5:]:
        copy.wait()
    for n, value in enumerate((0.5 * line(g2), 0.5 * line(gh), line(b1), line(b2))):
        vec[pl.ds(n, 1)] = value
    bias[pl.ds(0, 1)] = jnp.concatenate([line(b3)] * 4, axis=-1)
    for n, out in enumerate((cfw, csw, chw)):
        for h in range(R):
            for f in range(2):
                put_rows(out, h * 16 + f * 8, caches[n, f, h].astype(F32))
    for n in range(2):
        lo[16 + n] = rows_at(cfw, n * 16, 16, 1).astype(BF16)
        hi[16 + n] = rows_at(cfw, (2 + n) * 16, 16, 1).astype(BF16)
    lo[18] = rows_at(csw, 0, 16, 1).astype(BF16)
    hi[18] = rows_at(csw, 48, 16, 1).astype(BF16)


def pack_kernel(own, top, bot, cfw, csw, after, left, right, wide_f, wide_s):
    del after
    for n in range(2):
        put_rows(wide_f, n * 16, top[16 + n].astype(F32))
        put_rows(wide_f, (6 + n) * 16, bot[16 + n].astype(F32))
    put_rows(wide_s, 0, top[18].astype(F32))
    put_rows(wide_s, 5 * 16, bot[18].astype(F32))
    for n in range(3):
        wide_f[n, pl.ds(32, 64)] = cfw[n]
        wide_s[n, pl.ds(16, 64)] = csw[n]
        wide_s[n, pl.ds(96, 32)] = jnp.zeros((32, 128), F32)
    for out, base, edge in ((left, 0, 0), (right, 6, 7)):
        for c in range(2):
            for h in range(8):
                w = base + c
                if h < 2:
                    cell = top[h * Q + w]
                elif h < 6:
                    cell = own[(h - 2) * Q + w]
                else:
                    cell = bot[(h - 6) * Q + w]
                out[h * 2 + c] = cell
            out[16 + c] = rows_at(wide_f, base + c, 16, 8).astype(BF16)
        out[18] = rows_at(wide_s, edge, 16, 8).astype(BF16)


def cached_row(ref, base, w0, count):
    return [[rows_at(ref, base + 8 * f + w0 + w, 1, 1) for w in range(count)] for f in range(2)]


def cached_msg(block, count=Q):
    block = block.astype(F32)
    return [[block[8 * f + w : 8 * f + w + 1] for w in range(count)] for f in range(2)]


def three(weight, a):
    return jnp.concatenate([weight[a, 3 * b : 3 * b + 3].reshape(3 * C, C) for b in range(3)], axis=-1)


def hidden(dst, where, total, vec, cached, valid=None):
    wide = (total + vec[pl.ds(2, 1), :]).astype(BF16).astype(F32)
    put(dst, where, act(wide, vec[pl.ds(0, 1), :]), cached[0], cached[1], valid)


def place():
    ha, wa = lax.axis_index("ha"), lax.axis_index("wa")
    return ha > 0, ha < lax.axis_size("ha") - 1, wa > 0, wa < lax.axis_size("wa") - 1


def reach(rh, rw):
    return [
        (2 * (rh - 1 + m) + r, 2 * (rw - 1 + n) + s)
        for m in range(2) for n in range(2) for r in range(2) for s in range(2)
    ]


def inner_kernel(own, cfw, w1, w2, wh, acc, w1v, w2v, flat, s1, sems):
    def group(src, dst, a, sem):
        return [
            pltpu.make_async_copy(src.at[t, a, b], dst.at[a, b * 3 + t], sem) for b in range(3) for t in range(3)
        ]

    first = [group(w1, w1v, a, sems.at[a]) for a in range(3)]
    later = [copy for a in range(3) for copy in group(w2, w2v, a, sems.at[3 + a])]
    for t in range(3):
        for a in range(3):
            for b in range(3):
                later.append(
                    pltpu.make_async_copy(
                        wh.at[t, a, b], flat.at[pl.ds((a * 3 + b) * 32, 32), pl.ds(t * C, C)], sems.at[6]
                    )
                )
    for copies in first[:2]:
        for copy in copies:
            copy.start()
    acc[...] = jnp.zeros_like(acc)

    def cells(h, _):
        c0, c1 = cached_row(cfw, h * 16, 0, Q)
        put(s1, (pl.ds(h * Q, Q),), own[pl.ds(h * Q, Q)].reshape(Q * F, C).astype(F32), c0, c1)
        return 0

    lax.fori_loop(0, R, cells, 0)
    for a in range(3):
        for copy in first[a]:
            copy.wait()
        for copy in (first[2], later, ())[a]:
            copy.start()
        part = jnp.dot(s1[...].reshape(R * Q * F, 3 * C), three(w1v, a), preferred_element_type=F32)
        for b in range(3):
            acc[2 - a : 2 - a + R, 2 - b : 2 - b + Q] += part[:, b * C : (b + 1) * C].reshape(R, Q, F, C)
    for copy in later:
        copy.wait()


def rows_kernel(top, bot, acc, plain, csw, vec, w1v, flat, sides, s2, raw, wy, s1, add):
    up, down, _, _ = place()
    for msg, h0, valid in ((top, 0, up), (bot, 2, down)):
        for h in range(2):
            c0, c1 = cached_msg(msg[16 + h])
            put(s1, (h0 + h, pl.ds(0, Q)), msg[pl.ds(h * Q, Q)].reshape(Q * F, C).astype(F32), c0, c1, valid)
    add[0:2] = acc[0:2]
    add[2:4] = acc[4:6]
    for a, (low, targets) in enumerate(((0, (0, 1)), (1, (0, 3)), (2, (2, 3)))):
        part = jnp.dot(s1[low : low + 2].reshape(2 * Q * F, 3 * C), three(w1v, a), preferred_element_type=F32)
        for n, row in enumerate(targets):
            for b in range(3):
                block = part[n * Q * F : (n + 1) * Q * F, b * C : (b + 1) * C]
                add[row, 2 - b : 2 - b + Q] += block.reshape(Q, F, C)
    for n, cached, valid in (
        (0, [c[1:7] for c in cached_msg(top[18])], up),
        (1, cached_row(csw, 0, 1, 6), None),
        (2, cached_row(csw, 16, 1, 6), None),
        (3, cached_row(csw, 32, 1, 6), None),
        (4, cached_row(csw, 48, 1, 6), None),
        (5, [c[1:7] for c in cached_msg(bot[18])], down),
    ):
        total = acc[n, 2:8] if 2 <= n < 4 else add[n if n < 2 else n - 2, 2:8]
        hidden(s2, (n, pl.ds(0, 6)), total.reshape(6 * F, C), vec, cached, valid)
    for k in range(R * Q):
        raw[k] = rows_at(plain, k, F, PITCH).astype(BF16)
    turned = jnp.transpose(flat[...])
    none = jnp.zeros((3 * C, 32), BF16)
    for rh in range(2):
        for rw in range(2):
            targets = reach(rh, rw)
            for patch in range(4):
                parts = []
                for row, col in targets[4 * patch : 4 * patch + 4]:
                    a, b = rh + 1 - row, rw + 1 - col
                    low = (a * 3 + b) * 32
                    parts.append(turned[:, low : low + 32] if 0 <= a <= 2 and 0 <= b <= 2 else none)
                wy[rh * 2 + rw, :, patch * 128 : (patch + 1) * 128] = jnp.concatenate(parts, axis=-1)
    for n, col in enumerate((0, 8)):
        sides[0:2, 2 * n : 2 * n + 2] = add[0:2, col : col + 2]
        sides[2:4, 2 * n : 2 * n + 2] = acc[2:4, col : col + 2]
        sides[4:6, 2 * n : 2 * n + 2] = add[2:4, col : col + 2]


def finish_kernel(
    left, right, top, bot, sides, rows2, raw, csw, chw, vec, w1v, w2v, wy, out,
    s1, acc1, s2, s3, acc2, acch, side_f, side_s,
):
    up, down, west, east = place()
    for n, msg in enumerate((left, right)):
        for c in range(2):
            side_f[n, pl.ds(c * 16, 16)] = msg[16 + c].astype(F32)
        side_s[n] = msg[18].astype(F32)
    for n, (msg, side) in enumerate(((left, west), (right, east))):
        for h in range(8):
            valid = side & up if h < 2 else side & down if h >= 6 else side
            put(
                s1, (h, pl.ds(2 * n, 2)), msg[pl.ds(h * 2, 2)].reshape(2 * F, C).astype(F32),
                [side_f[n, pl.ds(c * 16 + h * 2, 1), :] for c in range(2)],
                [side_f[n, pl.ds(c * 16 + h * 2 + 1, 1), :] for c in range(2)], valid,
            )

    def columns(first):
        return jnp.concatenate([s1[a : a + 6, first : first + 2].reshape(12 * F, 3 * C) for a in range(3)], axis=-1)

    def column_tap(b, low, high):
        return jnp.concatenate([w1v[a, 3 * b : 3 * b + 3, :, low:high].reshape(3 * C, high - low) for a in range(3)], axis=0)

    main, last = slice(0, 256), slice(256, 384)
    for b in (0, 2, 1):
        part = jnp.dot(columns(b), column_tap(b, 0, 256), preferred_element_type=F32).reshape(6, 2, F, 256)
        if b == 1:
            for n, col in enumerate((0, 3)):
                acc1[:, col, :, main] += part[:, n]
        else:
            acc1[:, b : b + 2, :, main] = sides[:, b : b + 2, :, main] + part
    for b in range(2):
        weight = jnp.concatenate([column_tap(b, 256, 384), column_tap(b + 1, 256, 384)], axis=-1)
        part = jnp.dot(columns(2 * b), weight, preferred_element_type=F32).reshape(6, 2, F, 256)
        both = part[:, 0, :, :128] + part[:, 1, :, 128:]
        if b == 0:
            acc1[:, 0, :, last] = sides[:, 0, :, last] + both
            acc1[:, 1, :, last] = sides[:, 1, :, last] + part[:, 1, :, :128]
        else:
            acc1[:, 3, :, last] = sides[:, 3, :, last] + both
            acc1[:, 2, :, last] = sides[:, 2, :, last] + part[:, 0, :, 128:]
    s2[:, 2:8] = rows2[...]
    for h in range(6):
        inside = up if h == 0 else down if h == 5 else True
        if h == 0:
            c0, c1 = cached_msg(top[18])
        elif h == 5:
            c0, c1 = cached_msg(bot[18])
        else:
            c0, c1 = cached_row(csw, (h - 1) * 16, 0, Q)
        for n, side in enumerate((west, east)):
            first = [side_s[n, pl.ds(h * 2 + f, 1), :] for f in range(2)]
            keep = jnp.where(side, 1.0, 0.0).astype(F32)
            total = acc1[h, 2 * n : 2 * n + 2].reshape(2 * F, C)
            wide = (total + vec[pl.ds(2, 1), :]).astype(BF16).astype(F32)
            now = act(wide, vec[pl.ds(0, 1), :])
            own_w = 0 if n == 0 else Q - 1
            pair = [now[:F], now[F:]]
            pair[n] = pair[n] * keep
            now = jnp.concatenate(pair, axis=0)
            olds = []
            for f, c in enumerate((c0, c1)):
                two = [first[f] * keep, c[own_w]]
                olds.append(two if n == 0 else two[::-1])
            put(s2, (h, pl.ds(8 * n, 2)), now, olds[0], olds[1], None if inside is True else inside)

    def window(row, rows):
        return jnp.concatenate(
            [s2[row : row + rows, b : b + Q].reshape(rows * Q * F, 3 * C) for b in range(3)], axis=-1
        )

    def one(b):
        return w2v[2, 3 * b : 3 * b + 3, :, 256:384].reshape(3 * C, 128)

    half = R // 2
    size = half * Q * F
    side = [w2v[a, :, :, 256:384].reshape(9 * C, 128) for a in range(2)]
    for top_row in range(0, R, half):
        rows = pl.ds(top_row * Q * F, size)
        for a in range(3):
            part = jnp.dot(
                window(top_row + a, half), w2v[a, :, :, 0:256].reshape(9 * C, 256), preferred_element_type=F32
            )
            if a == 0:
                acc2[rows, 0:256] = part
            else:
                acc2[rows, 0:256] += part
        pair = jnp.dot(window(top_row, half + 1), jnp.concatenate(side, axis=-1), preferred_element_type=F32)
        wider = s2[top_row + 2 : top_row + 2 + half, 0 : Q + 1].reshape(half * (Q + 1) * F, 3 * C)
        two = jnp.dot(wider, jnp.concatenate([one(0), one(1)], axis=-1), preferred_element_type=F32)
        two = two.reshape(half, Q + 1, F, 256)
        last_tap = jnp.dot(
            s2[top_row + 2 : top_row + 2 + half, 2 : 2 + Q].reshape(size, 3 * C), one(2), preferred_element_type=F32
        )
        acc2[rows, 256:384] = (
            pair[:size, :128] + pair[Q * F :, 128:] + last_tap
            + (two[:, :Q, :, :128] + two[:, 1:, :, 128:]).reshape(size, 128)
        )
        for h in range(top_row, top_row + half):
            wide = acc2[pl.ds(h * Q * F, Q * F)] + vec[pl.ds(3, 1), :]
            wide = wide + raw[pl.ds(h * Q, Q)].reshape(Q * F, C).astype(F32)
            c0, c1 = cached_row(chw, h * 16, 0, Q)
            now = act(wide.astype(BF16).astype(F32), vec[pl.ds(1, 1), :])
            for n, part in enumerate(stack(now, c0, c1)):
                part = part.reshape(Q, F, C)
                for w in range(Q):
                    s3[h % 2 * 2 + w % 2, h // 2 * 4 + w // 2, :, pl.ds(n * C, C)] = part[w]
    sums = {}
    for rh in range(2):
        for rw in range(2):
            part = jnp.dot(
                s3[rh * 2 + rw].reshape(8 * F, 3 * C), wy[rh * 2 + rw], preferred_element_type=F32
            )
            for k in range(8):
                for m in range(2):
                    for n in range(2):
                        pp, qq = (k // 4 + rh - 1 + m) % 3, (k % 4 + rw - 1 + n) % 5
                        slot = pp * 4 + qq if qq < 4 else 12 + pp
                        term = part[k * F : (k + 1) * F, (m * 2 + n) * 128 : (m * 2 + n + 1) * 128]
                        sums[slot] = sums[slot] + term if slot in sums else term
    for slot, total in sums.items():
        acch[pl.ds(slot * F, F)] = total
    acch[pl.ds(15 * F, F)] = jnp.zeros((F, 128), F32)

    for f in range(F):
        patches = acch[pl.ds(f, 16, stride=F), :].astype(BF16)
        for g in range(8):
            out[f, g] = patches[8 * (g % 2) : 8 * (g % 2) + 8]


def last_kernel(mine, theirs, bias, out, sums):
    ha_count = 16
    g = lax.axis_index("wa")
    even = g % 2 == 0
    first = [jnp.clip(2 * g - 1 + k, 0, ha_count - 1) * 8 for k in range(4)]

    halves = {}
    for k in range(4):
        for j in range(8):
            here, there = mine[first[k] + j].astype(F32), theirs[first[k] + j].astype(F32)
            halves[k, j] = jnp.where(even, here, there), jnp.where(even, there, here)

    def held(k, j, low, count):
        return halves[k, j][low // 8][low % 8 : low % 8 + count]

    lane = lax.broadcasted_iota(jnp.int32, (4, 128), 1)
    row = lax.broadcasted_iota(jnp.int32, (4, 128), 0)
    for k in range(2):
        for pr in range(2):
            other = k if pr == 0 else k + 2
            there = (2 * g + k > 0) if pr == 0 else (2 * g + k < ha_count - 1)
            upright = ((lane < 64) if pr == 0 else (lane >= 64)) & there

            def edge(j, pr=pr, k=k, other=other, upright=upright):
                mine = jnp.broadcast_to(held(k + 1, j, 12 + pr, 1), (4, 128))
                theirs = jnp.broadcast_to(held(other, j, 14, 1), (4, 128))
                return mine + jnp.where(upright, theirs, 0.0)

            for j in range(8):
                total = held(k + 1, j, pr * 4, 4)
                total = total + jnp.where(upright, held(other, j, 8, 4), 0.0)
                if j > 0:
                    total = total + jnp.where((row == 0) & (lane % 64 < 32), edge(j - 1), 0.0)
                if j < 7:
                    total = total + jnp.where((row == 3) & (lane % 64 >= 32), edge(j + 1), 0.0)
                sums[pl.ds((2 * k + pr) * 32 + j * 4, 4)] = total + bias[pl.ds(0, 1), :]
    out[...] = sums[...].astype(BF16)


def shape(*dims, dtype=BF16):
    return jax.ShapeDtypeStruct(dims, dtype)


def near(*dims, dtype=BF16):
    return pltpu.VMEM(dims, dtype)


def far(array):
    return pltpu.with_memory_space_constraint(array, pltpu.HBM)


def kernel(body, outs, ins, scratch, limit, name, flops=0, moved=0):
    return pl.pallas_call(
        body,
        out_shape=outs,
        in_specs=ins,
        out_specs=[VM] * len(outs),
        scratch_shapes=scratch,
        compiler_params=pltpu.CompilerParams(vmem_limit_bytes=limit * 2**20),
        cost_estimate=pl.CostEstimate(flops=flops, bytes_accessed=moved, transcendentals=0),
        name=name,
    )


def around(axis, step):
    count = lax.axis_size(axis)
    return [(n, (n + step) % count) for n in range(count)]


def local(
    features, cache_first, cache_second, cache_head, gain_first, gain_second, gain_head,
    conv_first, conv_second, conv_head, bias_first, bias_second, bias_head,
):
    own, plain, lo, hi, cfw, csw, chw, vec, bias = kernel(
        first_kernel,
        [near(32, F, C), near(3, F * PITCH, 128, dtype=F32), near(MSG, F, C), near(MSG, F, C)]
        + [near(3, 64, 128, dtype=F32)] * 3 + [near(8, C, dtype=F32), near(8, 128, dtype=F32)],
        [ANY] * 10,
        [
            pltpu.VMEM((F, R, Q, C), BF16),
            pltpu.VMEM((3, 2, R, Q, C), BF16),
        ]
        + [pltpu.VMEM((C,), F32)] * 5
        + [
            pltpu.VMEM((32,), F32),
            pltpu.VMEM((3, F * PITCH, 128), F32),
            pltpu.SemaphoreType.DMA((13,)),
        ],
        12, "act_first",
    )(*[far(v) for v in (features, cache_first, cache_second, cache_head, gain_first, gain_second, gain_head,
                         bias_first, bias_second, bias_head)])
    top = lax.ppermute(hi, "ha", around("ha", 1))
    bot = lax.ppermute(lo, "ha", around("ha", -1))
    cell_flops = 2 * F * 27 * C * C
    sums1, w1v, w2v, flat = kernel(
        inner_kernel,
        [near(R + 2, Q + 2, F, C, dtype=F32), near(3, 9, C, C), near(3, 9, C, C), near(9 * 32, 3 * C)],
        [VM] * 2 + [ANY] * 3,
        [pltpu.VMEM((R * Q, F, 3 * C), BF16), pltpu.SemaphoreType.DMA((7,))],
        12, "inner", 32 * cell_flops, 17 * 2**20,
    )(own, cfw, far(conv_first), far(conv_second), far(jnp.swapaxes(conv_head, 3, 4)))
    to_left, to_right = kernel(
        pack_kernel,
        [near(MSG, F, C)] * 2,
        [VM] * 6,
        [pltpu.VMEM((3, 128, 128), F32)] * 2,
        4, "pack_columns",
    )(own, top, bot, cfw, csw, flat)
    left = lax.ppermute(to_right, "wa", around("wa", 1))
    right = lax.ppermute(to_left, "wa", around("wa", -1))
    sides, rows2, raw, wy = kernel(
        rows_kernel,
        [near(R + 2, 4, F, C, dtype=F32), near(R + 2, 6, F, 3 * C), near(32, F, C),
         near(4, 3 * C, 512)],
        [VM] * 8,
        [pltpu.VMEM((4, Q, F, 3 * C), BF16), pltpu.VMEM((4, Q + 2, F, C), F32)],
        16, "rows", 16 * cell_flops, 10 * 2**20,
    )(top, bot, sums1, plain, csw, vec, w1v, flat)
    (slots,) = kernel(
        finish_kernel,
        [shape(F, 8, 8, 128)],
        [VM] * 13,
        [
            pltpu.VMEM((8, 4, F, 3 * C), BF16),
            pltpu.VMEM((R + 2, 4, F, C), F32),
            pltpu.VMEM((R + 2, Q + 2, F, 3 * C), BF16),
            pltpu.VMEM((4, 8, F, 3 * C), BF16),
            pltpu.VMEM((R * Q * F, C), F32),
            pltpu.VMEM((16 * F, 128), F32),
            pltpu.VMEM((2, 32, C), F32),
            pltpu.VMEM((2, 16, C), F32),
        ],
        20, "finish", 48 * cell_flops, 20 * 2**20,
    )(left, right, top, bot, sides, rows2, raw, csw, chw, vec, w1v, w2v, wy)
    arrived = lax.all_to_all(slots.reshape(F * 8, 8, 128), ("ha", "wa"), 0, 0, tiled=True)
    pairs = [(n, n ^ 1) for n in range(lax.axis_size("wa"))]
    swapped = lax.ppermute(arrived, "wa", pairs)
    return pl.pallas_call(
        last_kernel,
        out_shape=shape(128, 128),
        in_specs=[VM] * 3,
        out_specs=VM,
        scratch_shapes=[pltpu.VMEM((128, 128), F32)],
        compiler_params=pltpu.CompilerParams(vmem_limit_bytes=4 * 2**20),
        name="sum_patches",
    )(arrived, swapped, bias)


def solution(mesh):
    tile = P(None, "ha", "wa", None)
    return jax.shard_map(
        local,
        mesh=mesh,
        in_specs=(tile,) * 4 + (P(),) * 9,
        out_specs=P(("ha", "wa"), None),
        check_vma=False,
    )
```

```python
import jax
import jax.numpy as jnp
from jax import lax
from jax.experimental import pallas as pl
from jax.experimental.pallas import tpu as pltpu
from jax.sharding import PartitionSpec as P

BF16 = jnp.bfloat16
F32 = jnp.float32
F, R, Q, C = 16, 4, 8, 384
MSG = 19
PITCH = 40
VM = pl.BlockSpec(memory_space=pltpu.VMEM)
ANY = pl.BlockSpec(memory_space=pl.ANY)


def act(wide, half_gain):
    scale = lax.rsqrt(jnp.mean(wide * wide, axis=-1, keepdims=True) + 1e-06)
    h = wide * scale * half_gain
    return h + h * jnp.tanh(h)


def line(ref):
    return ref[...].reshape(1, -1)


def put_rows(ref, start, value):
    for n in range(3):
        ref[n, pl.ds(start, value.shape[0])] = value[:, n * 128 : (n + 1) * 128]


def rows_at(ref, start, count, stride):
    where = pl.ds(start, count, stride=stride) if stride > 1 else pl.ds(start, count)
    return jnp.concatenate([ref[n, where, :] for n in range(3)], axis=-1)


def stack(now, c0, c1):
    row = lax.broadcasted_iota(jnp.int32, now.shape, 0) % F
    c0, c1 = (jnp.concatenate([jnp.broadcast_to(c, (F, C)) for c in cs], axis=0) for cs in (c0, c1))
    one = jnp.where(row == 0, c1, pltpu.roll(now, 1, 0))
    two = jnp.where(row == 0, c0, jnp.where(row == 1, c1, pltpu.roll(now, 2, 0)))
    return two.astype(BF16), one.astype(BF16), now.astype(BF16)


def put(dst, where, now, c0, c1, valid=None):
    if valid is not None:
        keep = jnp.where(valid, 1.0, 0.0).astype(F32)
        now, c0, c1 = now * keep, [c * keep for c in c0], [c * keep for c in c1]
    for n, part in enumerate(stack(now, c0, c1)):
        dst[where + (slice(None), pl.ds(n * C, C))] = part.reshape(-1, F, C)


def bring(pairs, sems):
    copies = [pltpu.make_async_copy(src, dst, sems.at[n]) for n, (src, dst) in enumerate(pairs)]
    for copy in copies:
        copy.start()
    return copies


def first_kernel(
    feat_h, cf_h, cs_h, ch_h, g1_h, g2_h, gh_h, b1_h, b2_h, b3_h, own, plain, lo, hi, cfw, csw, chw, vec, bias,
    feat, caches, g1, g2, gh, b1, b2, b3, wide, sems,
):
    parts = [pl.ds(4 * n, 4) for n in range(4)]
    copies = bring(
        [(g1_h, g1)] + [(feat_h.at[part], feat.at[part]) for part in parts]
        + [(cf_h, caches.at[0]), (cs_h, caches.at[1]), (ch_h, caches.at[2]),
           (g2_h, g2), (gh_h, gh), (b1_h, b1), (b2_h, b2), (b3_h, b3)], sems
    )
    copies[0].wait()
    half = 0.5 * line(g1)
    for n, part in enumerate(parts):
        copies[1 + n].wait()
        x = feat[part].astype(F32).reshape(4 * R * Q, C)
        y = act(x, half)
        for m in range(4):
            put_rows(plain, (n * 4 + m) * PITCH, x[m * R * Q : (m + 1) * R * Q])
            put_rows(wide, (n * 4 + m) * PITCH, y[m * R * Q : (m + 1) * R * Q])
    for k in range(R * Q):
        cell = rows_at(wide, k, F, PITCH).astype(BF16)
        own[k] = cell
        if k < 16:
            lo[k] = cell
        else:
            hi[k - 16] = cell
    for copy in copies[5:]:
        copy.wait()
    for n, value in enumerate((0.5 * line(g2), 0.5 * line(gh), line(b1), line(b2))):
        vec[pl.ds(n, 1)] = value
    bias[pl.ds(0, 1)] = jnp.concatenate([line(b3)] * 4, axis=-1)
    for n, out in enumerate((cfw, csw, chw)):
        for h in range(R):
            for f in range(2):
                put_rows(out, h * 16 + f * 8, caches[n, f, h].astype(F32))
    for n in range(2):
        lo[16 + n] = rows_at(cfw, n * 16, 16, 1).astype(BF16)
        hi[16 + n] = rows_at(cfw, (2 + n) * 16, 16, 1).astype(BF16)
    lo[18] = rows_at(csw, 0, 16, 1).astype(BF16)
    hi[18] = rows_at(csw, 48, 16, 1).astype(BF16)


def pack_kernel(own, top, bot, cfw, csw, after, left, right, wide_f, wide_s):
    del after
    for n in range(2):
        put_rows(wide_f, n * 16, top[16 + n].astype(F32))
        put_rows(wide_f, (6 + n) * 16, bot[16 + n].astype(F32))
    put_rows(wide_s, 0, top[18].astype(F32))
    put_rows(wide_s, 5 * 16, bot[18].astype(F32))
    for n in range(3):
        wide_f[n, pl.ds(32, 64)] = cfw[n]
        wide_s[n, pl.ds(16, 64)] = csw[n]
        wide_s[n, pl.ds(96, 40)] = jnp.zeros((40, 128), F32)
    for out, base, edge in ((left, 0, 0), (right, 6, 7)):
        for c in range(2):
            for h in range(8):
                w = base + c
                if h < 2:
                    cell = top[h * Q + w]
                elif h < 6:
                    cell = own[(h - 2) * Q + w]
                else:
                    cell = bot[(h - 6) * Q + w]
                out[h * 2 + c] = cell
            out[16 + c] = rows_at(wide_f, base + c, 16, 8).astype(BF16)
        out[18] = rows_at(wide_s, edge, 16, 8).astype(BF16)


def cached_row(ref, base, w0, count):
    return [[rows_at(ref, base + 8 * f + w0 + w, 1, 1) for w in range(count)] for f in range(2)]


def cached_msg(block, count=Q):
    block = block.astype(F32)
    return [[block[8 * f + w : 8 * f + w + 1] for w in range(count)] for f in range(2)]


def three(weight, a):
    return jnp.concatenate([weight[a, 3 * b : 3 * b + 3].reshape(3 * C, C) for b in range(3)], axis=-1)


def hidden(dst, where, total, vec, cached, valid=None):
    wide = (total + vec[pl.ds(2, 1), :]).astype(BF16).astype(F32)
    put(dst, where, act(wide, vec[pl.ds(0, 1), :]), cached[0], cached[1], valid)


def place():
    ha, wa = lax.axis_index("ha"), lax.axis_index("wa")
    return ha > 0, ha < lax.axis_size("ha") - 1, wa > 0, wa < lax.axis_size("wa") - 1


def reach(rh, rw):
    return [
        (2 * (rh - 1 + m) + r, 2 * (rw - 1 + n) + s)
        for m in range(2) for n in range(2) for r in range(2) for s in range(2)
    ]


def inner_kernel(own, cfw, w1, w2, wh, acc, w1v, w2v, flat, s1, sems):
    def group(src, dst, a, sem):
        return [
            pltpu.make_async_copy(src.at[t, a, b], dst.at[a, b * 3 + t], sem) for b in range(3) for t in range(3)
        ]

    first = [group(w1, w1v, a, sems.at[a]) for a in range(3)]
    later = [copy for a in range(3) for copy in group(w2, w2v, a, sems.at[3 + a])]
    for t in range(3):
        for a in range(3):
            for b in range(3):
                later.append(
                    pltpu.make_async_copy(
                        wh.at[t, a, b], flat.at[pl.ds((a * 3 + b) * 32, 32), pl.ds(t * C, C)], sems.at[6]
                    )
                )
    for copies in first[:2]:
        for copy in copies:
            copy.start()
    acc[...] = jnp.zeros_like(acc)

    def cells(h, _):
        c0, c1 = cached_row(cfw, h * 16, 0, Q)
        put(s1, (pl.ds(h * Q, Q),), own[pl.ds(h * Q, Q)].reshape(Q * F, C).astype(F32), c0, c1)
        return 0

    lax.fori_loop(0, R, cells, 0)
    for a in range(3):
        for copy in first[a]:
            copy.wait()
        for copy in (first[2], later, ())[a]:
            copy.start()
        part = jnp.dot(s1[...].reshape(R * Q * F, 3 * C), three(w1v, a), preferred_element_type=F32)
        for b in range(3):
            acc[2 - a : 2 - a + R, 2 - b : 2 - b + Q] += part[:, b * C : (b + 1) * C].reshape(R, Q, F, C)
    for copy in later:
        copy.wait()


def rows_kernel(top, bot, acc, plain, csw, vec, w1v, flat, sides, s2, raw, wy, s1, add):
    up, down, _, _ = place()
    for msg, h0, valid in ((top, 0, up), (bot, 2, down)):
        for h in range(2):
            c0, c1 = cached_msg(msg[16 + h])
            put(s1, (h0 + h, pl.ds(0, Q)), msg[pl.ds(h * Q, Q)].reshape(Q * F, C).astype(F32), c0, c1, valid)
    add[0:2] = acc[0:2]
    add[2:4] = acc[4:6]
    for a, (low, targets) in enumerate(((0, (0, 1)), (1, (0, 3)), (2, (2, 3)))):
        part = jnp.dot(s1[low : low + 2].reshape(2 * Q * F, 3 * C), three(w1v, a), preferred_element_type=F32)
        for n, row in enumerate(targets):
            for b in range(3):
                block = part[n * Q * F : (n + 1) * Q * F, b * C : (b + 1) * C]
                add[row, 2 - b : 2 - b + Q] += block.reshape(Q, F, C)
    for n, cached, valid in (
        (0, [c[1:7] for c in cached_msg(top[18])], up),
        (1, cached_row(csw, 0, 1, 6), None),
        (2, cached_row(csw, 16, 1, 6), None),
        (3, cached_row(csw, 32, 1, 6), None),
        (4, cached_row(csw, 48, 1, 6), None),
        (5, [c[1:7] for c in cached_msg(bot[18])], down),
    ):
        total = acc[n, 2:8] if 2 <= n < 4 else add[n if n < 2 else n - 2, 2:8]
        hidden(s2, (n, pl.ds(0, 6)), total.reshape(6 * F, C), vec, cached, valid)
    for k in range(R * Q):
        raw[k] = rows_at(plain, k, F, PITCH).astype(BF16)
    turned = jnp.transpose(flat[...])
    none = jnp.zeros((3 * C, 32), BF16)
    for rh in range(2):
        for rw in range(2):
            targets = reach(rh, rw)
            for patch in range(4):
                parts = []
                for row, col in targets[4 * patch : 4 * patch + 4]:
                    a, b = rh + 1 - row, rw + 1 - col
                    low = (a * 3 + b) * 32
                    parts.append(turned[:, low : low + 32] if 0 <= a <= 2 and 0 <= b <= 2 else none)
                wy[rh * 2 + rw, :, patch * 128 : (patch + 1) * 128] = jnp.concatenate(parts, axis=-1)
    for n, col in enumerate((0, 8)):
        sides[0:2, 2 * n : 2 * n + 2] = add[0:2, col : col + 2]
        sides[2:4, 2 * n : 2 * n + 2] = acc[2:4, col : col + 2]
        sides[4:6, 2 * n : 2 * n + 2] = add[2:4, col : col + 2]


def finish_kernel(
    left, right, top, bot, sides, rows2, raw, csw, chw, vec, w1v, w2v, wy, out,
    s1, acc1, s2, s3, acc2, acch, side_f, side_s,
):
    up, down, west, east = place()
    for n, msg in enumerate((left, right)):
        for c in range(2):
            side_f[n, pl.ds(c * 16, 16)] = msg[16 + c].astype(F32)
        side_s[n] = msg[18].astype(F32)
    for n, (msg, side) in enumerate(((left, west), (right, east))):
        for h in range(8):
            valid = side & up if h < 2 else side & down if h >= 6 else side
            put(
                s1, (h, pl.ds(2 * n, 2)), msg[pl.ds(h * 2, 2)].reshape(2 * F, C).astype(F32),
                [side_f[n, pl.ds(c * 16 + h * 2, 1), :] for c in range(2)],
                [side_f[n, pl.ds(c * 16 + h * 2 + 1, 1), :] for c in range(2)], valid,
            )

    def columns(first):
        return jnp.concatenate([s1[a : a + 6, first : first + 2].reshape(12 * F, 3 * C) for a in range(3)], axis=-1)

    def column_tap(b, low, high):
        return jnp.concatenate([w1v[a, 3 * b : 3 * b + 3, :, low:high].reshape(3 * C, high - low) for a in range(3)], axis=0)

    main, last = slice(0, 256), slice(256, 384)
    for b in (0, 2, 1):
        part = jnp.dot(columns(b), column_tap(b, 0, 256), preferred_element_type=F32).reshape(6, 2, F, 256)
        if b == 1:
            for n, col in enumerate((0, 3)):
                acc1[:, col, :, main] += part[:, n]
        else:
            acc1[:, b : b + 2, :, main] = sides[:, b : b + 2, :, main] + part
    for b in range(2):
        weight = jnp.concatenate([column_tap(b, 256, 384), column_tap(b + 1, 256, 384)], axis=-1)
        part = jnp.dot(columns(2 * b), weight, preferred_element_type=F32).reshape(6, 2, F, 256)
        both = part[:, 0, :, :128] + part[:, 1, :, 128:]
        if b == 0:
            acc1[:, 0, :, last] = sides[:, 0, :, last] + both
            acc1[:, 1, :, last] = sides[:, 1, :, last] + part[:, 1, :, :128]
        else:
            acc1[:, 3, :, last] = sides[:, 3, :, last] + both
            acc1[:, 2, :, last] = sides[:, 2, :, last] + part[:, 0, :, 128:]
    s2[:, 2:8] = rows2[...]
    for h in range(6):
        inside = up if h == 0 else down if h == 5 else True
        if h == 0:
            c0, c1 = cached_msg(top[18])
        elif h == 5:
            c0, c1 = cached_msg(bot[18])
        else:
            c0, c1 = cached_row(csw, (h - 1) * 16, 0, Q)
        for n, side in enumerate((west, east)):
            first = [side_s[n, pl.ds(h * 2 + f, 1), :] for f in range(2)]
            keep = jnp.where(side, 1.0, 0.0).astype(F32)
            total = acc1[h, 2 * n : 2 * n + 2].reshape(2 * F, C)
            wide = (total + vec[pl.ds(2, 1), :]).astype(BF16).astype(F32)
            now = act(wide, vec[pl.ds(0, 1), :])
            own_w = 0 if n == 0 else Q - 1
            pair = [now[:F], now[F:]]
            pair[n] = pair[n] * keep
            now = jnp.concatenate(pair, axis=0)
            olds = []
            for f, c in enumerate((c0, c1)):
                two = [first[f] * keep, c[own_w]]
                olds.append(two if n == 0 else two[::-1])
            put(s2, (h, pl.ds(8 * n, 2)), now, olds[0], olds[1], None if inside is True else inside)

    def window(row, rows):
        return jnp.concatenate(
            [s2[row : row + rows, b : b + Q].reshape(rows * Q * F, 3 * C) for b in range(3)], axis=-1
        )

    def one(b):
        return w2v[2, 3 * b : 3 * b + 3, :, 256:384].reshape(3 * C, 128)

    half = R // 2
    size = half * Q * F
    side = [w2v[a, :, :, 256:384].reshape(9 * C, 128) for a in range(2)]
    for top_row in range(0, R, half):
        rows = pl.ds(top_row * Q * F, size)
        for a in range(3):
            part = jnp.dot(
                window(top_row + a, half), w2v[a, :, :, 0:256].reshape(9 * C, 256), preferred_element_type=F32
            )
            if a == 0:
                acc2[rows, 0:256] = part
            else:
                acc2[rows, 0:256] += part
        pair = jnp.dot(window(top_row, half + 1), jnp.concatenate(side, axis=-1), preferred_element_type=F32)
        wider = s2[top_row + 2 : top_row + 2 + half, 0 : Q + 1].reshape(half * (Q + 1) * F, 3 * C)
        two = jnp.dot(wider, jnp.concatenate([one(0), one(1)], axis=-1), preferred_element_type=F32)
        two = two.reshape(half, Q + 1, F, 256)
        last_tap = jnp.dot(
            s2[top_row + 2 : top_row + 2 + half, 2 : 2 + Q].reshape(size, 3 * C), one(2), preferred_element_type=F32
        )
        acc2[rows, 256:384] = (
            pair[:size, :128] + pair[Q * F :, 128:] + last_tap
            + (two[:, :Q, :, :128] + two[:, 1:, :, 128:]).reshape(size, 128)
        )
        for h in range(top_row, top_row + half):
            wide = acc2[pl.ds(h * Q * F, Q * F)] + vec[pl.ds(3, 1), :]
            wide = wide + raw[pl.ds(h * Q, Q)].reshape(Q * F, C).astype(F32)
            c0, c1 = cached_row(chw, h * 16, 0, Q)
            now = act(wide.astype(BF16).astype(F32), vec[pl.ds(1, 1), :])
            for n, part in enumerate(stack(now, c0, c1)):
                part = part.reshape(Q, F, C)
                for w in range(Q):
                    s3[h % 2 * 2 + w % 2, h // 2 * 4 + w // 2, :, pl.ds(n * C, C)] = part[w]
    sums = {}
    for rh in range(2):
        for rw in range(2):
            part = jnp.dot(
                s3[rh * 2 + rw].reshape(8 * F, 3 * C), wy[rh * 2 + rw], preferred_element_type=F32
            )
            for k in range(8):
                for m in range(2):
                    for n in range(2):
                        pp, qq = (k // 4 + rh - 1 + m) % 3, (k % 4 + rw - 1 + n) % 5
                        slot = pp * 4 + qq if qq < 4 else 12 + pp
                        term = part[k * F : (k + 1) * F, (m * 2 + n) * 128 : (m * 2 + n + 1) * 128]
                        sums[slot] = sums[slot] + term if slot in sums else term
    for slot, total in sums.items():
        acch[pl.ds(slot * F, F)] = total
    acch[pl.ds(15 * F, F)] = jnp.zeros((F, 128), F32)

    for f in range(F):
        patches = acch[pl.ds(f, 16, stride=F), :]
        halves = [patches[:8].astype(BF16), patches[8:].astype(BF16)]
        for g in range(8):
            out[f, g] = halves[g % 2]


def last_kernel(mine, theirs, bias, out, sums):
    ha_count = 16
    g = lax.axis_index("wa")
    even = g % 2 == 0
    first = [jnp.clip(2 * g - 1 + k, 0, ha_count - 1) * 8 for k in range(4)]

    halves = {}
    for k in range(4):
        for j in range(8):
            here, there = mine[first[k] + j].astype(F32), theirs[first[k] + j].astype(F32)
            halves[k, j] = jnp.where(even, here, there), jnp.where(even, there, here)

    def held(k, j, low, count):
        return halves[k, j][low // 8][low % 8 : low % 8 + count]

    lane = lax.broadcasted_iota(jnp.int32, (4, 128), 1)
    row = lax.broadcasted_iota(jnp.int32, (4, 128), 0)
    for k in range(2):
        for pr in range(2):
            other = k if pr == 0 else k + 2
            there = (2 * g + k > 0) if pr == 0 else (2 * g + k < ha_count - 1)
            upright = ((lane < 64) if pr == 0 else (lane >= 64)) & there

            def edge(j, pr=pr, k=k, other=other, upright=upright):
                mine = jnp.broadcast_to(held(k + 1, j, 12 + pr, 1), (4, 128))
                theirs = jnp.broadcast_to(held(other, j, 14, 1), (4, 128))
                return mine + jnp.where(upright, theirs, 0.0)

            for j in range(8):
                total = held(k + 1, j, pr * 4, 4)
                total = total + jnp.where(upright, held(other, j, 8, 4), 0.0)
                if j > 0:
                    total = total + jnp.where((row == 0) & (lane % 64 < 32), edge(j - 1), 0.0)
                if j < 7:
                    total = total + jnp.where((row == 3) & (lane % 64 >= 32), edge(j + 1), 0.0)
                sums[pl.ds((2 * k + pr) * 32 + j * 4, 4)] = total + bias[pl.ds(0, 1), :]
    out[...] = sums[...].astype(BF16)


def shape(*dims, dtype=BF16):
    return jax.ShapeDtypeStruct(dims, dtype)


def near(*dims, dtype=BF16):
    return pltpu.VMEM(dims, dtype)


def far(array):
    return pltpu.with_memory_space_constraint(array, pltpu.HBM)


def kernel(body, outs, ins, scratch, limit, name, flops=0, moved=0):
    return pl.pallas_call(
        body,
        out_shape=outs,
        in_specs=ins,
        out_specs=[VM] * len(outs),
        scratch_shapes=scratch,
        compiler_params=pltpu.CompilerParams(vmem_limit_bytes=limit * 2**20),
        cost_estimate=pl.CostEstimate(flops=flops, bytes_accessed=moved, transcendentals=0),
        name=name,
    )


def around(axis, step):
    count = lax.axis_size(axis)
    return [(n, (n + step) % count) for n in range(count)]


def local(
    features, cache_first, cache_second, cache_head, gain_first, gain_second, gain_head,
    conv_first, conv_second, conv_head, bias_first, bias_second, bias_head,
):
    own, plain, lo, hi, cfw, csw, chw, vec, bias = kernel(
        first_kernel,
        [near(32, F, C), near(3, (F + 1) * PITCH, 128, dtype=F32), near(MSG, F, C), near(MSG, F, C)]
        + [near(3, 64, 128, dtype=F32)] * 3 + [near(8, C, dtype=F32), near(8, 128, dtype=F32)],
        [ANY] * 10,
        [
            pltpu.VMEM((F, R, Q, C), BF16),
            pltpu.VMEM((3, 2, R, Q, C), BF16),
        ]
        + [pltpu.VMEM((C,), F32)] * 5
        + [
            pltpu.VMEM((32,), F32),
            pltpu.VMEM((3, (F + 1) * PITCH, 128), F32),
            pltpu.SemaphoreType.DMA((13,)),
        ],
        12, "act_first",
    )(*[far(v) for v in (features, cache_first, cache_second, cache_head, gain_first, gain_second, gain_head,
                         bias_first, bias_second, bias_head)])
    top = lax.ppermute(hi, "ha", around("ha", 1))
    bot = lax.ppermute(lo, "ha", around("ha", -1))
    cell_flops = 2 * F * 27 * C * C
    sums1, w1v, w2v, flat = kernel(
        inner_kernel,
        [near(R + 2, Q + 2, F, C, dtype=F32), near(3, 9, C, C), near(3, 9, C, C), near(9 * 32, 3 * C)],
        [VM] * 2 + [ANY] * 3,
        [pltpu.VMEM((R * Q, F, 3 * C), BF16), pltpu.SemaphoreType.DMA((7,))],
        12, "inner", 32 * cell_flops, 17 * 2**20,
    )(own, cfw, far(conv_first), far(conv_second), far(jnp.swapaxes(conv_head, 3, 4)))
    to_left, to_right = kernel(
        pack_kernel,
        [near(MSG, F, C)] * 2,
        [VM] * 6,
        [pltpu.VMEM((3, 136, 128), F32)] * 2,
        4, "pack_columns",
    )(own, top, bot, cfw, csw, flat)
    left = lax.ppermute(to_right, "wa", around("wa", 1))
    right = lax.ppermute(to_left, "wa", around("wa", -1))
    sides, rows2, raw, wy = kernel(
        rows_kernel,
        [near(R + 2, 4, F, C, dtype=F32), near(R + 2, 6, F, 3 * C), near(32, F, C),
         near(4, 3 * C, 512)],
        [VM] * 8,
        [pltpu.VMEM((4, Q, F, 3 * C), BF16), pltpu.VMEM((4, Q + 2, F, C), F32)],
        16, "rows", 16 * cell_flops, 10 * 2**20,
    )(top, bot, sums1, plain, csw, vec, w1v, flat)
    (slots,) = kernel(
        finish_kernel,
        [shape(F, 8, 8, 128)],
        [VM] * 13,
        [
            pltpu.VMEM((8, 4, F, 3 * C), BF16),
            pltpu.VMEM((R + 2, 4, F, C), F32),
            pltpu.VMEM((R + 2, Q + 2, F, 3 * C), BF16),
            pltpu.VMEM((4, 8, F, 3 * C), BF16),
            pltpu.VMEM((R * Q * F, C), F32),
            pltpu.VMEM((17 * F, 128), F32),
            pltpu.VMEM((2, 32, C), F32),
            pltpu.VMEM((2, 16, C), F32),
        ],
        20, "finish", 48 * cell_flops, 20 * 2**20,
    )(left, right, top, bot, sides, rows2, raw, csw, chw, vec, w1v, w2v, wy)
    arrived = lax.all_to_all(slots.reshape(F * 8, 8, 128), ("ha", "wa"), 0, 0, tiled=True)
    pairs = [(n, n ^ 1) for n in range(lax.axis_size("wa"))]
    swapped = lax.ppermute(arrived, "wa", pairs)
    return pl.pallas_call(
        last_kernel,
        out_shape=shape(128, 128),
        in_specs=[VM] * 3,
        out_specs=VM,
        scratch_shapes=[pltpu.VMEM((128, 128), F32)],
        compiler_params=pltpu.CompilerParams(vmem_limit_bytes=4 * 2**20),
        name="sum_patches",
    )(arrived, swapped, bias)


def solution(mesh):
    tile = P(None, "ha", "wa", None)
    return jax.shard_map(
        local,
        mesh=mesh,
        in_specs=(tile,) * 4 + (P(),) * 9,
        out_specs=P(("ha", "wa"), None),
        check_vma=False,
    )
```

```python
import jax
import jax.numpy as jnp
from jax import lax
from jax.experimental import pallas as pl
from jax.experimental.pallas import tpu as pltpu
from jax.sharding import PartitionSpec as P

BF16 = jnp.bfloat16
F32 = jnp.float32
F, R, Q, C = 16, 4, 8, 384
MSG = 19
PITCH = 36
VM = pl.BlockSpec(memory_space=pltpu.VMEM)
ANY = pl.BlockSpec(memory_space=pl.ANY)


def act(wide, half_gain):
    scale = lax.rsqrt(jnp.mean(wide * wide, axis=-1, keepdims=True) + 1e-06)
    h = wide * scale * half_gain
    return h + h * jnp.tanh(h)


def line(ref):
    return ref[...].reshape(1, -1)


def put_rows(ref, start, value):
    for n in range(3):
        ref[n, pl.ds(start, value.shape[0])] = value[:, n * 128 : (n + 1) * 128]


def rows_at(ref, start, count, stride):
    where = pl.ds(start, count, stride=stride) if stride > 1 else pl.ds(start, count)
    return jnp.concatenate([ref[n, where, :] for n in range(3)], axis=-1)


def stack(now, c0, c1):
    row = lax.broadcasted_iota(jnp.int32, now.shape, 0) % F
    c0, c1 = (jnp.concatenate([jnp.broadcast_to(c, (F, C)) for c in cs], axis=0) for cs in (c0, c1))
    one = jnp.where(row == 0, c1, pltpu.roll(now, 1, 0))
    two = jnp.where(row == 0, c0, jnp.where(row == 1, c1, pltpu.roll(now, 2, 0)))
    return two.astype(BF16), one.astype(BF16), now.astype(BF16)


def put(dst, where, now, c0, c1, valid=None):
    if valid is not None:
        keep = jnp.where(valid, 1.0, 0.0).astype(F32)
        now, c0, c1 = now * keep, [c * keep for c in c0], [c * keep for c in c1]
    for n, part in enumerate(stack(now, c0, c1)):
        dst[where + (slice(None), pl.ds(n * C, C))] = part.reshape(-1, F, C)


def bring(pairs, sems):
    copies = [pltpu.make_async_copy(src, dst, sems.at[n]) for n, (src, dst) in enumerate(pairs)]
    for copy in copies:
        copy.start()
    return copies


def first_kernel(
    feat_h, cf_h, cs_h, ch_h, g1_h, g2_h, gh_h, b1_h, b2_h, b3_h, own, plain, lo, hi, cfw, csw, chw, vec, bias,
    feat, caches, g1, g2, gh, b1, b2, b3, wide, sems,
):
    parts = [pl.ds(4 * n, 4) for n in range(4)]
    copies = bring(
        [(g1_h, g1)] + [(feat_h.at[part], feat.at[part]) for part in parts]
        + [(cf_h, caches.at[0]), (cs_h, caches.at[1]), (ch_h, caches.at[2]),
           (g2_h, g2), (gh_h, gh), (b1_h, b1), (b2_h, b2), (b3_h, b3)], sems
    )
    copies[0].wait()
    half = 0.5 * line(g1)
    for n, part in enumerate(parts):
        copies[1 + n].wait()
        x = feat[part].astype(F32).reshape(4 * R * Q, C)
        y = act(x, half)
        for m in range(4):
            put_rows(plain, (n * 4 + m) * PITCH, x[m * R * Q : (m + 1) * R * Q])
            put_rows(wide, (n * 4 + m) * PITCH, y[m * R * Q : (m + 1) * R * Q])
    for k in range(R * Q):
        cell = rows_at(wide, k, F, PITCH).astype(BF16)
        own[k] = cell
        if k < 16:
            lo[k] = cell
        else:
            hi[k - 16] = cell
    for copy in copies[5:]:
        copy.wait()
    for n, value in enumerate((0.5 * line(g2), 0.5 * line(gh), line(b1), line(b2))):
        vec[pl.ds(n, 1)] = value
    bias[pl.ds(0, 1)] = jnp.concatenate([line(b3)] * 4, axis=-1)
    for n, out in enumerate((cfw, csw, chw)):
        for h in range(R):
            for f in range(2):
                put_rows(out, h * 16 + f * 8, caches[n, f, h].astype(F32))
    for n in range(2):
        lo[16 + n] = rows_at(cfw, n * 16, 16, 1).astype(BF16)
        hi[16 + n] = rows_at(cfw, (2 + n) * 16, 16, 1).astype(BF16)
    lo[18] = rows_at(csw, 0, 16, 1).astype(BF16)
    hi[18] = rows_at(csw, 48, 16, 1).astype(BF16)


def pack_kernel(own, top, bot, cfw, csw, after, left, right, wide_f, wide_s):
    del after
    for n in range(2):
        put_rows(wide_f, n * 16, top[16 + n].astype(F32))
        put_rows(wide_f, (6 + n) * 16, bot[16 + n].astype(F32))
    put_rows(wide_s, 0, top[18].astype(F32))
    put_rows(wide_s, 5 * 16, bot[18].astype(F32))
    for n in range(3):
        wide_f[n, pl.ds(32, 64)] = cfw[n]
        wide_s[n, pl.ds(16, 64)] = csw[n]
        wide_s[n, pl.ds(96, 40)] = jnp.zeros((40, 128), F32)
    for out, base, edge in ((left, 0, 0), (right, 6, 7)):
        for c in range(2):
            for h in range(8):
                w = base + c
                if h < 2:
                    cell = top[h * Q + w]
                elif h < 6:
                    cell = own[(h - 2) * Q + w]
                else:
                    cell = bot[(h - 6) * Q + w]
                out[h * 2 + c] = cell
            out[16 + c] = rows_at(wide_f, base + c, 16, 8).astype(BF16)
        out[18] = rows_at(wide_s, edge, 16, 8).astype(BF16)


def cached_row(ref, base, w0, count):
    return [[rows_at(ref, base + 8 * f + w0 + w, 1, 1) for w in range(count)] for f in range(2)]


def cached_msg(block, count=Q):
    block = block.astype(F32)
    return [[block[8 * f + w : 8 * f + w + 1] for w in range(count)] for f in range(2)]


def three(weight, a):
    return jnp.concatenate([weight[a, 3 * b : 3 * b + 3].reshape(3 * C, C) for b in range(3)], axis=-1)


def hidden(dst, where, total, vec, cached, valid=None):
    wide = (total + vec[pl.ds(2, 1), :]).astype(BF16).astype(F32)
    put(dst, where, act(wide, vec[pl.ds(0, 1), :]), cached[0], cached[1], valid)


def place():
    ha, wa = lax.axis_index("ha"), lax.axis_index("wa")
    return ha > 0, ha < lax.axis_size("ha") - 1, wa > 0, wa < lax.axis_size("wa") - 1


def reach(rh, rw):
    return [
        (2 * (rh - 1 + m) + r, 2 * (rw - 1 + n) + s)
        for m in range(2) for n in range(2) for r in range(2) for s in range(2)
    ]


def inner_kernel(own, cfw, w1, w2, wh, acc, w1v, w2v, flat, s1, sems):
    def group(src, dst, a, sem):
        return [
            pltpu.make_async_copy(src.at[t, a, b], dst.at[a, b * 3 + t], sem) for b in range(3) for t in range(3)
        ]

    first = [group(w1, w1v, a, sems.at[a]) for a in range(3)]
    later = [copy for a in range(3) for copy in group(w2, w2v, a, sems.at[3 + a])]
    for t in range(3):
        for a in range(3):
            for b in range(3):
                later.append(
                    pltpu.make_async_copy(
                        wh.at[t, a, b], flat.at[pl.ds((a * 3 + b) * 32, 32), pl.ds(t * C, C)], sems.at[6]
                    )
                )
    for copies in first[:2]:
        for copy in copies:
            copy.start()
    acc[...] = jnp.zeros_like(acc)

    for h in range(R):
        c0, c1 = cached_row(cfw, h * 16, 0, Q)
        put(s1, (pl.ds(h * Q, Q),), own[pl.ds(h * Q, Q)].reshape(Q * F, C).astype(F32), c0, c1)
    for a in range(3):
        for copy in first[a]:
            copy.wait()
        for copy in (first[2], later, ())[a]:
            copy.start()
        part = jnp.dot(s1[...].reshape(R * Q * F, 3 * C), three(w1v, a), preferred_element_type=F32)
        for b in range(3):
            acc[2 - a : 2 - a + R, 2 - b : 2 - b + Q] += part[:, b * C : (b + 1) * C].reshape(R, Q, F, C)
    for copy in later:
        copy.wait()


def rows_kernel(top, bot, acc, plain, csw, vec, w1v, flat, sides, s2, raw, wy, s1, add):
    up, down, _, _ = place()
    for msg, h0, valid in ((top, 0, up), (bot, 2, down)):
        for h in range(2):
            c0, c1 = cached_msg(msg[16 + h])
            put(s1, (h0 + h, pl.ds(0, Q)), msg[pl.ds(h * Q, Q)].reshape(Q * F, C).astype(F32), c0, c1, valid)
    add[0:2] = acc[0:2]
    add[2:4] = acc[4:6]
    for a, (low, targets) in enumerate(((0, (0, 1)), (1, (0, 3)), (2, (2, 3)))):
        part = jnp.dot(s1[low : low + 2].reshape(2 * Q * F, 3 * C), three(w1v, a), preferred_element_type=F32)
        for n, row in enumerate(targets):
            for b in range(3):
                block = part[n * Q * F : (n + 1) * Q * F, b * C : (b + 1) * C]
                add[row, 2 - b : 2 - b + Q] += block.reshape(Q, F, C)
    for n, cached, valid in (
        (0, [c[1:7] for c in cached_msg(top[18])], up),
        (1, cached_row(csw, 0, 1, 6), None),
        (2, cached_row(csw, 16, 1, 6), None),
        (3, cached_row(csw, 32, 1, 6), None),
        (4, cached_row(csw, 48, 1, 6), None),
        (5, [c[1:7] for c in cached_msg(bot[18])], down),
    ):
        total = acc[n, 2:8] if 2 <= n < 4 else add[n if n < 2 else n - 2, 2:8]
        hidden(s2, (n, pl.ds(0, 6)), total.reshape(6 * F, C), vec, cached, valid)
    for k in range(R * Q):
        raw[k] = rows_at(plain, k, F, PITCH).astype(BF16)
    turned = jnp.transpose(flat[...])
    none = jnp.zeros((3 * C, 32), BF16)
    for rh in range(2):
        for rw in range(2):
            targets = reach(rh, rw)
            for patch in range(4):
                parts = []
                for row, col in targets[4 * patch : 4 * patch + 4]:
                    a, b = rh + 1 - row, rw + 1 - col
                    low = (a * 3 + b) * 32
                    parts.append(turned[:, low : low + 32] if 0 <= a <= 2 and 0 <= b <= 2 else none)
                wy[rh * 2 + rw, :, patch * 128 : (patch + 1) * 128] = jnp.concatenate(parts, axis=-1)
    for n, col in enumerate((0, 8)):
        sides[0:2, 2 * n : 2 * n + 2] = add[0:2, col : col + 2]
        sides[2:4, 2 * n : 2 * n + 2] = acc[2:4, col : col + 2]
        sides[4:6, 2 * n : 2 * n + 2] = add[2:4, col : col + 2]


def finish_kernel(
    left, right, top, bot, sides, rows2, raw, csw, chw, vec, w1v, w2v, wy, out,
    s1, acc1, s2, s3, acc2, acch, side_f, side_s,
):
    up, down, west, east = place()
    for n, msg in enumerate((left, right)):
        for c in range(2):
            side_f[n, pl.ds(c * 16, 16)] = msg[16 + c].astype(F32)
        side_s[n] = msg[18].astype(F32)
    for n, (msg, side) in enumerate(((left, west), (right, east))):
        for h in range(8):
            valid = side & up if h < 2 else side & down if h >= 6 else side
            put(
                s1, (h, pl.ds(2 * n, 2)), msg[pl.ds(h * 2, 2)].reshape(2 * F, C).astype(F32),
                [side_f[n, pl.ds(c * 16 + h * 2, 1), :] for c in range(2)],
                [side_f[n, pl.ds(c * 16 + h * 2 + 1, 1), :] for c in range(2)], valid,
            )

    def columns(first):
        return jnp.concatenate([s1[a : a + 6, first : first + 2].reshape(12 * F, 3 * C) for a in range(3)], axis=-1)

    def column_tap(b, low, high):
        return jnp.concatenate([w1v[a, 3 * b : 3 * b + 3, :, low:high].reshape(3 * C, high - low) for a in range(3)], axis=0)

    main, last = slice(0, 256), slice(256, 384)
    for b in (0, 2, 1):
        part = jnp.dot(columns(b), column_tap(b, 0, 256), preferred_element_type=F32).reshape(6, 2, F, 256)
        if b == 1:
            for n, col in enumerate((0, 3)):
                acc1[:, col, :, main] += part[:, n]
        else:
            acc1[:, b : b + 2, :, main] = sides[:, b : b + 2, :, main] + part
    for b in range(2):
        weight = jnp.concatenate([column_tap(b, 256, 384), column_tap(b + 1, 256, 384)], axis=-1)
        part = jnp.dot(columns(2 * b), weight, preferred_element_type=F32).reshape(6, 2, F, 256)
        both = part[:, 0, :, :128] + part[:, 1, :, 128:]
        if b == 0:
            acc1[:, 0, :, last] = sides[:, 0, :, last] + both
            acc1[:, 1, :, last] = sides[:, 1, :, last] + part[:, 1, :, :128]
        else:
            acc1[:, 3, :, last] = sides[:, 3, :, last] + both
            acc1[:, 2, :, last] = sides[:, 2, :, last] + part[:, 0, :, 128:]
    s2[:, 2:8] = rows2[...]
    for h in range(6):
        inside = up if h == 0 else down if h == 5 else True
        if h == 0:
            c0, c1 = cached_msg(top[18])
        elif h == 5:
            c0, c1 = cached_msg(bot[18])
        else:
            c0, c1 = cached_row(csw, (h - 1) * 16, 0, Q)
        for n, side in enumerate((west, east)):
            first = [side_s[n, pl.ds(h * 2 + f, 1), :] for f in range(2)]
            keep = jnp.where(side, 1.0, 0.0).astype(F32)
            total = acc1[h, 2 * n : 2 * n + 2].reshape(2 * F, C)
            wide = (total + vec[pl.ds(2, 1), :]).astype(BF16).astype(F32)
            now = act(wide, vec[pl.ds(0, 1), :])
            own_w = 0 if n == 0 else Q - 1
            pair = [now[:F], now[F:]]
            pair[n] = pair[n] * keep
            now = jnp.concatenate(pair, axis=0)
            olds = []
            for f, c in enumerate((c0, c1)):
                two = [first[f] * keep, c[own_w]]
                olds.append(two if n == 0 else two[::-1])
            put(s2, (h, pl.ds(8 * n, 2)), now, olds[0], olds[1], None if inside is True else inside)

    def window(row, rows):
        return jnp.concatenate(
            [s2[row : row + rows, b : b + Q].reshape(rows * Q * F, 3 * C) for b in range(3)], axis=-1
        )

    def one(b):
        return w2v[2, 3 * b : 3 * b + 3, :, 256:384].reshape(3 * C, 128)

    half = R // 2
    size = half * Q * F
    side = [w2v[a, :, :, 256:384].reshape(9 * C, 128) for a in range(2)]
    for top_row in range(0, R, half):
        rows = pl.ds(top_row * Q * F, size)
        for a in range(3):
            part = jnp.dot(
                window(top_row + a, half), w2v[a, :, :, 0:256].reshape(9 * C, 256), preferred_element_type=F32
            )
            if a == 0:
                acc2[rows, 0:256] = part
            else:
                acc2[rows, 0:256] += part
        pair = jnp.dot(window(top_row, half + 1), jnp.concatenate(side, axis=-1), preferred_element_type=F32)
        wider = s2[top_row + 2 : top_row + 2 + half, 0 : Q + 1].reshape(half * (Q + 1) * F, 3 * C)
        two = jnp.dot(wider, jnp.concatenate([one(0), one(1)], axis=-1), preferred_element_type=F32)
        two = two.reshape(half, Q + 1, F, 256)
        last_tap = jnp.dot(
            s2[top_row + 2 : top_row + 2 + half, 2 : 2 + Q].reshape(size, 3 * C), one(2), preferred_element_type=F32
        )
        acc2[rows, 256:384] = (
            pair[:size, :128] + pair[Q * F :, 128:] + last_tap
            + (two[:, :Q, :, :128] + two[:, 1:, :, 128:]).reshape(size, 128)
        )
        for h in range(top_row, top_row + half):
            wide = acc2[pl.ds(h * Q * F, Q * F)] + vec[pl.ds(3, 1), :]
            wide = wide + raw[pl.ds(h * Q, Q)].reshape(Q * F, C).astype(F32)
            c0, c1 = cached_row(chw, h * 16, 0, Q)
            now = act(wide.astype(BF16).astype(F32), vec[pl.ds(1, 1), :])
            for n, part in enumerate(stack(now, c0, c1)):
                part = part.reshape(Q, F, C)
                for w in range(Q):
                    s3[h % 2 * 2 + w % 2, h // 2 * 4 + w // 2, :, pl.ds(n * C, C)] = part[w]
    sums = {}
    for rh in range(2):
        for rw in range(2):
            part = jnp.dot(
                s3[rh * 2 + rw].reshape(8 * F, 3 * C), wy[rh * 2 + rw], preferred_element_type=F32
            )
            for k in range(8):
                for m in range(2):
                    for n in range(2):
                        pp, qq = (k // 4 + rh - 1 + m) % 3, (k % 4 + rw - 1 + n) % 5
                        slot = pp * 4 + qq if qq < 4 else 12 + pp
                        term = part[k * F : (k + 1) * F, (m * 2 + n) * 128 : (m * 2 + n + 1) * 128]
                        sums[slot] = sums[slot] + term if slot in sums else term
    for slot, total in sums.items():
        acch[pl.ds(slot * F, F)] = total
    acch[pl.ds(15 * F, F)] = jnp.zeros((F, 128), F32)

    for f in range(F):
        patches = acch[pl.ds(f, 16, stride=F), :]
        halves = [patches[:8].astype(BF16), patches[8:].astype(BF16)]
        for g in range(8):
            out[f, g] = halves[g % 2]


def last_kernel(mine, theirs, bias, out, sums):
    ha_count = 16
    g = lax.axis_index("wa")
    even = g % 2 == 0
    first = [jnp.clip(2 * g - 1 + k, 0, ha_count - 1) * 8 for k in range(4)]

    halves = {}
    for k in range(4):
        for j in range(8):
            here, there = mine[first[k] + j].astype(F32), theirs[first[k] + j].astype(F32)
            halves[k, j] = jnp.where(even, here, there), jnp.where(even, there, here)

    def held(k, j, low, count):
        return halves[k, j][low // 8][low % 8 : low % 8 + count]

    lane = lax.broadcasted_iota(jnp.int32, (4, 128), 1)
    row = lax.broadcasted_iota(jnp.int32, (4, 128), 0)
    for k in range(2):
        for pr in range(2):
            other = k if pr == 0 else k + 2
            there = (2 * g + k > 0) if pr == 0 else (2 * g + k < ha_count - 1)
            upright = ((lane < 64) if pr == 0 else (lane >= 64)) & there

            def edge(j, pr=pr, k=k, other=other, upright=upright):
                mine = jnp.broadcast_to(held(k + 1, j, 12 + pr, 1), (4, 128))
                theirs = jnp.broadcast_to(held(other, j, 14, 1), (4, 128))
                return mine + jnp.where(upright, theirs, 0.0)

            for j in range(8):
                total = held(k + 1, j, pr * 4, 4)
                total = total + jnp.where(upright, held(other, j, 8, 4), 0.0)
                if j > 0:
                    total = total + jnp.where((row == 0) & (lane % 64 < 32), edge(j - 1), 0.0)
                if j < 7:
                    total = total + jnp.where((row == 3) & (lane % 64 >= 32), edge(j + 1), 0.0)
                sums[pl.ds((2 * k + pr) * 32 + j * 4, 4)] = total + bias[pl.ds(0, 1), :]
    out[...] = sums[...].astype(BF16)


def shape(*dims, dtype=BF16):
    return jax.ShapeDtypeStruct(dims, dtype)


def near(*dims, dtype=BF16):
    return pltpu.VMEM(dims, dtype)


def far(array):
    return pltpu.with_memory_space_constraint(array, pltpu.HBM)


def kernel(body, outs, ins, scratch, limit, name, flops=0, moved=0):
    return pl.pallas_call(
        body,
        out_shape=outs,
        in_specs=ins,
        out_specs=[VM] * len(outs),
        scratch_shapes=scratch,
        compiler_params=pltpu.CompilerParams(vmem_limit_bytes=limit * 2**20),
        cost_estimate=pl.CostEstimate(flops=flops, bytes_accessed=moved, transcendentals=0),
        name=name,
    )


def around(axis, step):
    count = lax.axis_size(axis)
    return [(n, (n + step) % count) for n in range(count)]


def local(
    features, cache_first, cache_second, cache_head, gain_first, gain_second, gain_head,
    conv_first, conv_second, conv_head, bias_first, bias_second, bias_head,
):
    own, plain, lo, hi, cfw, csw, chw, vec, bias = kernel(
        first_kernel,
        [near(32, F, C), near(3, (F + 1) * PITCH, 128, dtype=F32), near(MSG, F, C), near(MSG, F, C)]
        + [near(3, 64, 128, dtype=F32)] * 3 + [near(8, C, dtype=F32), near(8, 128, dtype=F32)],
        [ANY] * 10,
        [
            pltpu.VMEM((F, R, Q, C), BF16),
            pltpu.VMEM((3, 2, R, Q, C), BF16),
        ]
        + [pltpu.VMEM((C,), F32)] * 5
        + [
            pltpu.VMEM((32,), F32),
            pltpu.VMEM((3, (F + 1) * PITCH, 128), F32),
            pltpu.SemaphoreType.DMA((13,)),
        ],
        12, "act_first",
    )(*[far(v) for v in (features, cache_first, cache_second, cache_head, gain_first, gain_second, gain_head,
                         bias_first, bias_second, bias_head)])
    top = lax.ppermute(hi, "ha", around("ha", 1))
    bot = lax.ppermute(lo, "ha", around("ha", -1))
    cell_flops = 2 * F * 27 * C * C
    sums1, w1v, w2v, flat = kernel(
        inner_kernel,
        [near(R + 2, Q + 2, F, C, dtype=F32), near(3, 9, C, C), near(3, 9, C, C), near(9 * 32, 3 * C)],
        [VM] * 2 + [ANY] * 3,
        [pltpu.VMEM((R * Q, F, 3 * C), BF16), pltpu.SemaphoreType.DMA((7,))],
        12, "inner", 32 * cell_flops, 17 * 2**20,
    )(own, cfw, far(conv_first), far(conv_second), far(jnp.swapaxes(conv_head, 3, 4)))
    to_left, to_right = kernel(
        pack_kernel,
        [near(MSG, F, C)] * 2,
        [VM] * 6,
        [pltpu.VMEM((3, 136, 128), F32)] * 2,
        4, "pack_columns",
    )(own, top, bot, cfw, csw, flat)
    left = lax.ppermute(to_right, "wa", around("wa", 1))
    right = lax.ppermute(to_left, "wa", around("wa", -1))
    sides, rows2, raw, wy = kernel(
        rows_kernel,
        [near(R + 2, 4, F, C, dtype=F32), near(R + 2, 6, F, 3 * C), near(32, F, C),
         near(4, 3 * C, 512)],
        [VM] * 8,
        [pltpu.VMEM((4, Q, F, 3 * C), BF16), pltpu.VMEM((4, Q + 2, F, C), F32)],
        16, "rows", 16 * cell_flops, 10 * 2**20,
    )(top, bot, sums1, plain, csw, vec, w1v, flat)
    (slots,) = kernel(
        finish_kernel,
        [shape(F, 8, 8, 128)],
        [VM] * 13,
        [
            pltpu.VMEM((8, 4, F, 3 * C), BF16),
            pltpu.VMEM((R + 2, 4, F, C), F32),
            pltpu.VMEM((R + 2, Q + 2, F, 3 * C), BF16),
            pltpu.VMEM((4, 8, F, 3 * C), BF16),
            pltpu.VMEM((R * Q * F, C), F32),
            pltpu.VMEM((17 * F, 128), F32),
            pltpu.VMEM((2, 32, C), F32),
            pltpu.VMEM((2, 16, C), F32),
        ],
        20, "finish", 48 * cell_flops, 20 * 2**20,
    )(left, right, top, bot, sides, rows2, raw, csw, chw, vec, w1v, w2v, wy)
    arrived = lax.all_to_all(slots.reshape(F * 8, 8, 128), ("ha", "wa"), 0, 0, tiled=True)
    pairs = [(n, n ^ 1) for n in range(lax.axis_size("wa"))]
    swapped = lax.ppermute(arrived, "wa", pairs)
    return pl.pallas_call(
        last_kernel,
        out_shape=shape(128, 128),
        in_specs=[VM] * 3,
        out_specs=VM,
        scratch_shapes=[pltpu.VMEM((128, 128), F32)],
        compiler_params=pltpu.CompilerParams(vmem_limit_bytes=4 * 2**20),
        name="sum_patches",
    )(arrived, swapped, bias)


def solution(mesh):
    tile = P(None, "ha", "wa", None)
    return jax.shard_map(
        local,
        mesh=mesh,
        in_specs=(tile,) * 4 + (P(),) * 9,
        out_specs=P(("ha", "wa"), None),
        check_vma=False,
    )
```

```python
import jax
import jax.numpy as jnp
from jax import lax
from jax.experimental import pallas as pl
from jax.experimental.pallas import tpu as pltpu
from jax.sharding import PartitionSpec as P

BF16 = jnp.bfloat16
F32 = jnp.float32
F, R, Q, C = 16, 4, 8, 384
MSG = 19
PITCH = 40
VM = pl.BlockSpec(memory_space=pltpu.VMEM)
ANY = pl.BlockSpec(memory_space=pl.ANY)


def act(wide, half_gain):
    scale = lax.rsqrt(jnp.mean(wide * wide, axis=-1, keepdims=True) + 1e-06)
    h = wide * scale * half_gain
    return h + h * jnp.tanh(h)


def line(ref):
    return ref[...].reshape(1, -1)


def put_rows(ref, start, value):
    for n in range(3):
        ref[n, pl.ds(start, value.shape[0])] = value[:, n * 128 : (n + 1) * 128]


def rows_at(ref, start, count, stride):
    where = pl.ds(start, count, stride=stride) if stride > 1 else pl.ds(start, count)
    return jnp.concatenate([ref[n, where, :] for n in range(3)], axis=-1)


def stack(now, c0, c1):
    row = lax.broadcasted_iota(jnp.int32, now.shape, 0) % F
    c0, c1 = (jnp.concatenate([jnp.broadcast_to(c, (F, C)) for c in cs], axis=0) for cs in (c0, c1))
    one = jnp.where(row == 0, c1, pltpu.roll(now, 1, 0))
    two = jnp.where(row == 0, c0, jnp.where(row == 1, c1, pltpu.roll(now, 2, 0)))
    return two.astype(BF16), one.astype(BF16), now.astype(BF16)


def put(dst, where, now, c0, c1, valid=None):
    if valid is not None:
        keep = jnp.where(valid, 1.0, 0.0).astype(F32)
        now, c0, c1 = now * keep, [c * keep for c in c0], [c * keep for c in c1]
    for n, part in enumerate(stack(now, c0, c1)):
        dst[where + (slice(None), pl.ds(n * C, C))] = part.reshape(-1, F, C)


def bring(pairs, sems):
    copies = [pltpu.make_async_copy(src, dst, sems.at[n]) for n, (src, dst) in enumerate(pairs)]
    for copy in copies:
        copy.start()
    return copies


def first_kernel(
    feat_h, cf_h, cs_h, ch_h, g1_h, g2_h, gh_h, b1_h, b2_h, b3_h, own, plain, lo, hi, cfw, csw, chw, vec, bias,
    feat, caches, g1, g2, gh, b1, b2, b3, wide, sems,
):
    parts = [pl.ds(4 * n, 4) for n in range(4)]
    copies = bring(
        [(g1_h, g1)] + [(feat_h.at[part], feat.at[part]) for part in parts]
        + [(cf_h, caches.at[0]), (cs_h, caches.at[1]), (ch_h, caches.at[2]),
           (g2_h, g2), (gh_h, gh), (b1_h, b1), (b2_h, b2), (b3_h, b3)], sems
    )
    copies[0].wait()
    half = 0.5 * line(g1)
    for n, part in enumerate(parts):
        copies[1 + n].wait()
        x = feat[part].astype(F32).reshape(4 * R * Q, C)
        y = act(x, half)
        for m in range(4):
            put_rows(plain, (n * 4 + m) * PITCH, x[m * R * Q : (m + 1) * R * Q])
            put_rows(wide, (n * 4 + m) * PITCH, y[m * R * Q : (m + 1) * R * Q])
    for k in range(R * Q):
        cell = rows_at(wide, k, F, PITCH).astype(BF16)
        own[k] = cell
        if k < 16:
            lo[k] = cell
        else:
            hi[k - 16] = cell
    for copy in copies[5:]:
        copy.wait()
    for n, value in enumerate((0.5 * line(g2), 0.5 * line(gh), line(b1), line(b2))):
        vec[pl.ds(n, 1)] = value
    bias[pl.ds(0, 1)] = jnp.concatenate([line(b3)] * 4, axis=-1)
    for n, out in enumerate((cfw, csw, chw)):
        for h in range(R):
            for f in range(2):
                put_rows(out, h * 16 + f * 8, caches[n, f, h].astype(F32))
    for n in range(2):
        lo[16 + n] = rows_at(cfw, n * 16, 16, 1).astype(BF16)
        hi[16 + n] = rows_at(cfw, (2 + n) * 16, 16, 1).astype(BF16)
    lo[18] = rows_at(csw, 0, 16, 1).astype(BF16)
    hi[18] = rows_at(csw, 48, 16, 1).astype(BF16)


def pack_kernel(own, top, bot, cfw, csw, after, left, right, wide_f, wide_s):
    del after
    for n in range(2):
        put_rows(wide_f, n * 16, top[16 + n].astype(F32))
        put_rows(wide_f, (6 + n) * 16, bot[16 + n].astype(F32))
    put_rows(wide_s, 0, top[18].astype(F32))
    put_rows(wide_s, 5 * 16, bot[18].astype(F32))
    for n in range(3):
        wide_f[n, pl.ds(32, 64)] = cfw[n]
        wide_s[n, pl.ds(16, 64)] = csw[n]
        wide_s[n, pl.ds(96, 40)] = jnp.zeros((40, 128), F32)
    for out, base, edge in ((left, 0, 0), (right, 6, 7)):
        for c in range(2):
            for h in range(8):
                w = base + c
                if h < 2:
                    cell = top[h * Q + w]
                elif h < 6:
                    cell = own[(h - 2) * Q + w]
                else:
                    cell = bot[(h - 6) * Q + w]
                out[h * 2 + c] = cell
            out[16 + c] = rows_at(wide_f, base + c, 16, 8).astype(BF16)
        out[18] = rows_at(wide_s, edge, 16, 8).astype(BF16)


def cached_row(ref, base, w0, count):
    return [[rows_at(ref, base + 8 * f + w0 + w, 1, 1) for w in range(count)] for f in range(2)]


def cached_msg(block, count=Q):
    block = block.astype(F32)
    return [[block[8 * f + w : 8 * f + w + 1] for w in range(count)] for f in range(2)]


def three(weight, a):
    return jnp.concatenate([weight[a, 3 * b : 3 * b + 3].reshape(3 * C, C) for b in range(3)], axis=-1)


def hidden(dst, where, total, vec, cached, valid=None):
    wide = (total + vec[pl.ds(2, 1), :]).astype(BF16).astype(F32)
    put(dst, where, act(wide, vec[pl.ds(0, 1), :]), cached[0], cached[1], valid)


def place():
    ha, wa = lax.axis_index("ha"), lax.axis_index("wa")
    return ha > 0, ha < lax.axis_size("ha") - 1, wa > 0, wa < lax.axis_size("wa") - 1


def reach(rh, rw):
    return [
        (2 * (rh - 1 + m) + r, 2 * (rw - 1 + n) + s)
        for m in range(2) for n in range(2) for r in range(2) for s in range(2)
    ]


def inner_kernel(own, cfw, w1, w2, wh, acc, w1v, w2v, flat, s1, sems):
    def group(src, dst, a, sem):
        return [
            pltpu.make_async_copy(src.at[t, a, b], dst.at[a, b * 3 + t], sem) for b in range(3) for t in range(3)
        ]

    first = [group(w1, w1v, a, sems.at[a]) for a in range(3)]
    later = [copy for a in range(3) for copy in group(w2, w2v, a, sems.at[3 + a])]
    for t in range(3):
        for a in range(3):
            for b in range(3):
                later.append(
                    pltpu.make_async_copy(
                        wh.at[t, a, b], flat.at[pl.ds((a * 3 + b) * 32, 32), pl.ds(t * C, C)], sems.at[6]
                    )
                )
    for copies in first[:2]:
        for copy in copies:
            copy.start()
    acc[...] = jnp.zeros_like(acc)

    def cells(h, _):
        c0, c1 = cached_row(cfw, h * 16, 0, Q)
        put(s1, (pl.ds(h * Q, Q),), own[pl.ds(h * Q, Q)].reshape(Q * F, C).astype(F32), c0, c1)
        return 0

    lax.fori_loop(0, R, cells, 0)
    for a in range(3):
        for copy in first[a]:
            copy.wait()
        for copy in (first[2], later, ())[a]:
            copy.start()
        part = jnp.dot(s1[...].reshape(R * Q * F, 3 * C), three(w1v, a), preferred_element_type=F32)
        for b in range(3):
            acc[2 - a : 2 - a + R, 2 - b : 2 - b + Q] += part[:, b * C : (b + 1) * C].reshape(R, Q, F, C)
    for copy in later:
        copy.wait()


def rows_kernel(top, bot, acc, plain, csw, vec, w1v, flat, sides, s2, raw, wy, s1, add):
    up, down, _, _ = place()
    for msg, h0, valid in ((top, 0, up), (bot, 2, down)):
        for h in range(2):
            c0, c1 = cached_msg(msg[16 + h])
            put(s1, (h0 + h, pl.ds(0, Q)), msg[pl.ds(h * Q, Q)].reshape(Q * F, C).astype(F32), c0, c1, valid)
    add[0:2] = acc[0:2]
    add[2:4] = acc[4:6]
    for a, (low, targets) in enumerate(((0, (0, 1)), (1, (0, 3)), (2, (2, 3)))):
        part = jnp.dot(s1[low : low + 2].reshape(2 * Q * F, 3 * C), three(w1v, a), preferred_element_type=F32)
        for n, row in enumerate(targets):
            for b in range(3):
                block = part[n * Q * F : (n + 1) * Q * F, b * C : (b + 1) * C]
                add[row, 2 - b : 2 - b + Q] += block.reshape(Q, F, C)
    for n, cached, valid in (
        (0, [c[1:7] for c in cached_msg(top[18])], up),
        (1, cached_row(csw, 0, 1, 6), None),
        (2, cached_row(csw, 16, 1, 6), None),
        (3, cached_row(csw, 32, 1, 6), None),
        (4, cached_row(csw, 48, 1, 6), None),
        (5, [c[1:7] for c in cached_msg(bot[18])], down),
    ):
        total = acc[n, 2:8] if 2 <= n < 4 else add[n if n < 2 else n - 2, 2:8]
        hidden(s2, (n, pl.ds(0, 6)), total.reshape(6 * F, C), vec, cached, valid)
    for k in range(R * Q):
        raw[k] = rows_at(plain, k, F, PITCH).astype(BF16)
    turned = jnp.transpose(flat[...])
    none = jnp.zeros((3 * C, 32), BF16)
    for rh in range(2):
        for rw in range(2):
            targets = reach(rh, rw)
            for patch in range(4):
                parts = []
                for row, col in targets[4 * patch : 4 * patch + 4]:
                    a, b = rh + 1 - row, rw + 1 - col
                    low = (a * 3 + b) * 32
                    parts.append(turned[:, low : low + 32] if 0 <= a <= 2 and 0 <= b <= 2 else none)
                wy[rh * 2 + rw, :, patch * 128 : (patch + 1) * 128] = jnp.concatenate(parts, axis=-1)
    for n, col in enumerate((0, 8)):
        sides[0:2, 2 * n : 2 * n + 2] = add[0:2, col : col + 2]
        sides[2:4, 2 * n : 2 * n + 2] = acc[2:4, col : col + 2]
        sides[4:6, 2 * n : 2 * n + 2] = add[2:4, col : col + 2]


def finish_kernel(
    left, right, top, bot, sides, rows2, raw, csw, chw, vec, w1v, w2v, wy, out,
    s1, acc1, s2, s3, acc2, acch, side_f, side_s,
):
    up, down, west, east = place()
    for n, msg in enumerate((left, right)):
        for c in range(2):
            side_f[n, pl.ds(c * 16, 16)] = msg[16 + c].astype(F32)
        side_s[n] = msg[18].astype(F32)
    for n, (msg, side) in enumerate(((left, west), (right, east))):
        for h in range(8):
            valid = side & up if h < 2 else side & down if h >= 6 else side
            put(
                s1, (h, pl.ds(2 * n, 2)), msg[pl.ds(h * 2, 2)].reshape(2 * F, C).astype(F32),
                [side_f[n, pl.ds(c * 16 + h * 2, 1), :] for c in range(2)],
                [side_f[n, pl.ds(c * 16 + h * 2 + 1, 1), :] for c in range(2)], valid,
            )

    def columns(first):
        return jnp.concatenate([s1[a : a + 6, first : first + 2].reshape(12 * F, 3 * C) for a in range(3)], axis=-1)

    def column_tap(b, low, high):
        return jnp.concatenate([w1v[a, 3 * b : 3 * b + 3, :, low:high].reshape(3 * C, high - low) for a in range(3)], axis=0)

    main, last = slice(0, 256), slice(256, 384)
    for b in (0, 2, 1):
        part = jnp.dot(columns(b), column_tap(b, 0, 256), preferred_element_type=F32).reshape(6, 2, F, 256)
        if b == 1:
            for n, col in enumerate((0, 3)):
                acc1[:, col, :, main] += part[:, n]
        else:
            acc1[:, b : b + 2, :, main] = sides[:, b : b + 2, :, main] + part
    for b in range(2):
        weight = jnp.concatenate([column_tap(b, 256, 384), column_tap(b + 1, 256, 384)], axis=-1)
        part = jnp.dot(columns(2 * b), weight, preferred_element_type=F32).reshape(6, 2, F, 256)
        both = part[:, 0, :, :128] + part[:, 1, :, 128:]
        if b == 0:
            acc1[:, 0, :, last] = sides[:, 0, :, last] + both
            acc1[:, 1, :, last] = sides[:, 1, :, last] + part[:, 1, :, :128]
        else:
            acc1[:, 3, :, last] = sides[:, 3, :, last] + both
            acc1[:, 2, :, last] = sides[:, 2, :, last] + part[:, 0, :, 128:]
    s2[:, 2:8] = rows2[...]
    for h in range(6):
        inside = up if h == 0 else down if h == 5 else True
        if h == 0:
            c0, c1 = cached_msg(top[18])
        elif h == 5:
            c0, c1 = cached_msg(bot[18])
        else:
            c0, c1 = cached_row(csw, (h - 1) * 16, 0, Q)
        for n, side in enumerate((west, east)):
            first = [side_s[n, pl.ds(h * 2 + f, 1), :] for f in range(2)]
            keep = jnp.where(side, 1.0, 0.0).astype(F32)
            total = acc1[h, 2 * n : 2 * n + 2].reshape(2 * F, C)
            wide = (total + vec[pl.ds(2, 1), :]).astype(BF16).astype(F32)
            now = act(wide, vec[pl.ds(0, 1), :])
            own_w = 0 if n == 0 else Q - 1
            pair = [now[:F], now[F:]]
            pair[n] = pair[n] * keep
            now = jnp.concatenate(pair, axis=0)
            olds = []
            for f, c in enumerate((c0, c1)):
                two = [first[f] * keep, c[own_w]]
                olds.append(two if n == 0 else two[::-1])
            put(s2, (h, pl.ds(8 * n, 2)), now, olds[0], olds[1], None if inside is True else inside)

    def window(row, rows):
        return jnp.concatenate(
            [s2[row : row + rows, b : b + Q].reshape(rows * Q * F, 3 * C) for b in range(3)], axis=-1
        )

    def one(b):
        return w2v[2, 3 * b : 3 * b + 3, :, 256:384].reshape(3 * C, 128)

    half = R
    size = half * Q * F
    side = [w2v[a, :, :, 256:384].reshape(9 * C, 128) for a in range(2)]
    for top_row in range(0, R, half):
        rows = pl.ds(top_row * Q * F, size)
        for a in range(3):
            part = jnp.dot(
                window(top_row + a, half), w2v[a, :, :, 0:256].reshape(9 * C, 256), preferred_element_type=F32
            )
            if a == 0:
                acc2[rows, 0:256] = part
            else:
                acc2[rows, 0:256] += part
        pair = jnp.dot(window(top_row, half + 1), jnp.concatenate(side, axis=-1), preferred_element_type=F32)
        wider = s2[top_row + 2 : top_row + 2 + half, 0 : Q + 1].reshape(half * (Q + 1) * F, 3 * C)
        two = jnp.dot(wider, jnp.concatenate([one(0), one(1)], axis=-1), preferred_element_type=F32)
        two = two.reshape(half, Q + 1, F, 256)
        last_tap = jnp.dot(
            s2[top_row + 2 : top_row + 2 + half, 2 : 2 + Q].reshape(size, 3 * C), one(2), preferred_element_type=F32
        )
        acc2[rows, 256:384] = (
            pair[:size, :128] + pair[Q * F :, 128:] + last_tap
            + (two[:, :Q, :, :128] + two[:, 1:, :, 128:]).reshape(size, 128)
        )
        for h in range(top_row, top_row + half):
            wide = acc2[pl.ds(h * Q * F, Q * F)] + vec[pl.ds(3, 1), :]
            wide = wide + raw[pl.ds(h * Q, Q)].reshape(Q * F, C).astype(F32)
            c0, c1 = cached_row(chw, h * 16, 0, Q)
            now = act(wide.astype(BF16).astype(F32), vec[pl.ds(1, 1), :])
            for n, part in enumerate(stack(now, c0, c1)):
                part = part.reshape(Q, F, C)
                for w in range(Q):
                    s3[h % 2 * 2 + w % 2, h // 2 * 4 + w // 2, :, pl.ds(n * C, C)] = part[w]
    sums = {}
    for rh in range(2):
        for rw in range(2):
            part = jnp.dot(
                s3[rh * 2 + rw].reshape(8 * F, 3 * C), wy[rh * 2 + rw], preferred_element_type=F32
            )
            for k in range(8):
                for m in range(2):
                    for n in range(2):
                        pp, qq = (k // 4 + rh - 1 + m) % 3, (k % 4 + rw - 1 + n) % 5
                        slot = pp * 4 + qq if qq < 4 else 12 + pp
                        term = part[k * F : (k + 1) * F, (m * 2 + n) * 128 : (m * 2 + n + 1) * 128]
                        sums[slot] = sums[slot] + term if slot in sums else term
    for slot, total in sums.items():
        acch[pl.ds(slot * F, F)] = total
    acch[pl.ds(15 * F, F)] = jnp.zeros((F, 128), F32)

    for f in range(F):
        patches = acch[pl.ds(f, 16, stride=F), :]
        halves = [patches[:8].astype(BF16), patches[8:].astype(BF16)]
        for g in range(8):
            out[f, g] = halves[g % 2]


def last_kernel(mine, theirs, bias, out, sums):
    ha_count = 16
    g = lax.axis_index("wa")
    even = g % 2 == 0
    first = [jnp.clip(2 * g - 1 + k, 0, ha_count - 1) * 8 for k in range(4)]

    halves = {}
    for k in range(4):
        for j in range(8):
            here, there = mine[first[k] + j].astype(F32), theirs[first[k] + j].astype(F32)
            halves[k, j] = jnp.where(even, here, there), jnp.where(even, there, here)

    def held(k, j, low, count):
        return halves[k, j][low // 8][low % 8 : low % 8 + count]

    lane = lax.broadcasted_iota(jnp.int32, (4, 128), 1)
    row = lax.broadcasted_iota(jnp.int32, (4, 128), 0)
    for k in range(2):
        for pr in range(2):
            other = k if pr == 0 else k + 2
            there = (2 * g + k > 0) if pr == 0 else (2 * g + k < ha_count - 1)
            upright = ((lane < 64) if pr == 0 else (lane >= 64)) & there

            def edge(j, pr=pr, k=k, other=other, upright=upright):
                mine = jnp.broadcast_to(held(k + 1, j, 12 + pr, 1), (4, 128))
                theirs = jnp.broadcast_to(held(other, j, 14, 1), (4, 128))
                return mine + jnp.where(upright, theirs, 0.0)

            for j in range(8):
                total = held(k + 1, j, pr * 4, 4)
                total = total + jnp.where(upright, held(other, j, 8, 4), 0.0)
                if j > 0:
                    total = total + jnp.where((row == 0) & (lane % 64 < 32), edge(j - 1), 0.0)
                if j < 7:
                    total = total + jnp.where((row == 3) & (lane % 64 >= 32), edge(j + 1), 0.0)
                sums[pl.ds((2 * k + pr) * 32 + j * 4, 4)] = total + bias[pl.ds(0, 1), :]
    out[...] = sums[...].astype(BF16)


def shape(*dims, dtype=BF16):
    return jax.ShapeDtypeStruct(dims, dtype)


def near(*dims, dtype=BF16):
    return pltpu.VMEM(dims, dtype)


def far(array):
    return pltpu.with_memory_space_constraint(array, pltpu.HBM)


def kernel(body, outs, ins, scratch, limit, name, flops=0, moved=0):
    return pl.pallas_call(
        body,
        out_shape=outs,
        in_specs=ins,
        out_specs=[VM] * len(outs),
        scratch_shapes=scratch,
        compiler_params=pltpu.CompilerParams(vmem_limit_bytes=limit * 2**20),
        cost_estimate=pl.CostEstimate(flops=flops, bytes_accessed=moved, transcendentals=0),
        name=name,
    )


def around(axis, step):
    count = lax.axis_size(axis)
    return [(n, (n + step) % count) for n in range(count)]


def local(
    features, cache_first, cache_second, cache_head, gain_first, gain_second, gain_head,
    conv_first, conv_second, conv_head, bias_first, bias_second, bias_head,
):
    own, plain, lo, hi, cfw, csw, chw, vec, bias = kernel(
        first_kernel,
        [near(32, F, C), near(3, (F + 1) * PITCH, 128, dtype=F32), near(MSG, F, C), near(MSG, F, C)]
        + [near(3, 64, 128, dtype=F32)] * 3 + [near(8, C, dtype=F32), near(8, 128, dtype=F32)],
        [ANY] * 10,
        [
            pltpu.VMEM((F, R, Q, C), BF16),
            pltpu.VMEM((3, 2, R, Q, C), BF16),
        ]
        + [pltpu.VMEM((C,), F32)] * 5
        + [
            pltpu.VMEM((32,), F32),
            pltpu.VMEM((3, (F + 1) * PITCH, 128), F32),
            pltpu.SemaphoreType.DMA((13,)),
        ],
        12, "act_first",
    )(*[far(v) for v in (features, cache_first, cache_second, cache_head, gain_first, gain_second, gain_head,
                         bias_first, bias_second, bias_head)])
    top = lax.ppermute(hi, "ha", around("ha", 1))
    bot = lax.ppermute(lo, "ha", around("ha", -1))
    cell_flops = 2 * F * 27 * C * C
    sums1, w1v, w2v, flat = kernel(
        inner_kernel,
        [near(R + 2, Q + 2, F, C, dtype=F32), near(3, 9, C, C), near(3, 9, C, C), near(9 * 32, 3 * C)],
        [VM] * 2 + [ANY] * 3,
        [pltpu.VMEM((R * Q, F, 3 * C), BF16), pltpu.SemaphoreType.DMA((7,))],
        12, "inner", 32 * cell_flops, 17 * 2**20,
    )(own, cfw, far(conv_first), far(conv_second), far(jnp.swapaxes(conv_head, 3, 4)))
    to_left, to_right = kernel(
        pack_kernel,
        [near(MSG, F, C)] * 2,
        [VM] * 6,
        [pltpu.VMEM((3, 136, 128), F32)] * 2,
        4, "pack_columns",
    )(own, top, bot, cfw, csw, flat)
    left = lax.ppermute(to_right, "wa", around("wa", 1))
    right = lax.ppermute(to_left, "wa", around("wa", -1))
    sides, rows2, raw, wy = kernel(
        rows_kernel,
        [near(R + 2, 4, F, C, dtype=F32), near(R + 2, 6, F, 3 * C), near(32, F, C),
         near(4, 3 * C, 512)],
        [VM] * 8,
        [pltpu.VMEM((4, Q, F, 3 * C), BF16), pltpu.VMEM((4, Q + 2, F, C), F32)],
        16, "rows", 16 * cell_flops, 10 * 2**20,
    )(top, bot, sums1, plain, csw, vec, w1v, flat)
    (slots,) = kernel(
        finish_kernel,
        [shape(F, 8, 8, 128)],
        [VM] * 13,
        [
            pltpu.VMEM((8, 4, F, 3 * C), BF16),
            pltpu.VMEM((R + 2, 4, F, C), F32),
            pltpu.VMEM((R + 2, Q + 2, F, 3 * C), BF16),
            pltpu.VMEM((4, 8, F, 3 * C), BF16),
            pltpu.VMEM((R * Q * F, C), F32),
            pltpu.VMEM((17 * F, 128), F32),
            pltpu.VMEM((2, 32, C), F32),
            pltpu.VMEM((2, 16, C), F32),
        ],
        20, "finish", 48 * cell_flops, 20 * 2**20,
    )(left, right, top, bot, sides, rows2, raw, csw, chw, vec, w1v, w2v, wy)
    arrived = lax.all_to_all(slots.reshape(F * 8, 8, 128), ("ha", "wa"), 0, 0, tiled=True)
    pairs = [(n, n ^ 1) for n in range(lax.axis_size("wa"))]
    swapped = lax.ppermute(arrived, "wa", pairs)
    return pl.pallas_call(
        last_kernel,
        out_shape=shape(128, 128),
        in_specs=[VM] * 3,
        out_specs=VM,
        scratch_shapes=[pltpu.VMEM((128, 128), F32)],
        compiler_params=pltpu.CompilerParams(vmem_limit_bytes=4 * 2**20),
        name="sum_patches",
    )(arrived, swapped, bias)


def solution(mesh):
    tile = P(None, "ha", "wa", None)
    return jax.shard_map(
        local,
        mesh=mesh,
        in_specs=(tile,) * 4 + (P(),) * 9,
        out_specs=P(("ha", "wa"), None),
        check_vma=False,
    )
```
